32 devices in a mesh: dp: 4 (over y, core), seq: 8 (over z, x).
Axes of the slice: x: 2, y: 2, z: 4, core: 2. Of those that a mesh axis runs over, the one named last changes fastest.
Arguments:
- tokens: bfloat16 [2, 4, 2048, 768], P(None, 'dp', 'seq'), may hold values from -6 to 6
- cotangent: bfloat16 [2, 4, 2048, 768], P(None, 'dp', 'seq'), may hold values from -6 to 6
- norm_in: bfloat16 [768], P(('dp', 'seq')), may hold values from 0.5 to 1.5
- w_in: bfloat16 [768, 3352], P(('dp', 'seq')), may hold values from -0.21875 to 0.21875
- conv_w: bfloat16 [1792, 4], P(('dp', 'seq')), may hold values from -3 to 3
- conv_b: bfloat16 [1792], P(('dp', 'seq')), may hold values from -3 to 3
- dt_bias: float32 [24], replicated, may hold values from -5.5 to -4
- a_log: float32 [24], replicated, may hold values from -3.9 to 1.6
- skip: float32 [24], replicated, may hold values from 0.5 to 1.5
- norm_out: bfloat16 [1536], P(('dp', 'seq')), may hold values from 0.5 to 1.5
- w_out: bfloat16 [1536, 768], P(('dp', 'seq')), may hold values from -0.15625 to 0.15625
Outputs:
- block_out: bfloat16 [2, 4, 2048, 768], P(None, 'dp', 'seq')
- grad_tokens: bfloat16 [2, 4, 2048, 768], P(None, 'dp', 'seq')
- grad_norm_in: float32 [768], P(('dp', 'seq'))
- grad_w_in: float32 [768, 3352], P(('dp', 'seq'))
- grad_conv_w: float32 [1792, 4], P(('dp', 'seq'))
- grad_conv_b: float32 [1792], P(('dp', 'seq'))
- grad_dt_bias: float32 [24], replicated
- grad_a_log: float32 [24], replicated
- grad_skip: float32 [24], replicated
- grad_norm_out: float32 [1536], P(('dp', 'seq'))
- grad_w_out: float32 [1536, 768], P(('dp', 'seq'))
The draws below stay inside these ranges and needn't reach their ends.
All inputs are finite; a program needn't handle non-finite values.
Results may differ from the reference program's by a relative error of at most 0.012.
Values may be sent and summed in bfloat16 or wider, within the bound.
No kernel may reach another device: no remote copies, remote signals or barrier semaphores. Data moves between devices by JAX's collectives and lax.ppermute only.
A program may use at most 256 MiB of HBM per device.

```python
import jax
import jax.numpy as jnp
from jax import lax

D = 768
H = 24
HP = 64
N = 128
KW = 4
PIECE = 256
SEQ_LEN = 2048
MB = 2
DI = 1536
CONV = 1792
PROJ = 3352
SEQS = 4
LENGTH = 2048


def block_scale(stream_key, extent, split, smallest, high):
    level, own = 1.0, jax.random.fold_in(stream_key, 6)
    for dim, parts in split:
        heights = jnp.exp(jax.random.uniform(jax.random.fold_in(own, dim), (parts,), jnp.float32, smallest / len(split), high / len(split)))
        level = level * jnp.repeat(heights, extent[dim] // parts).reshape([-1 if axis == dim else 1 for axis in range(len(extent))])
    return level


def scatter_about(stream_key, dims, scale, most, shards=(), kind=jnp.bfloat16):
    level = block_scale(stream_key, dims, shards, -0.22, 0.18) if shards else 1.0
    drawn = jax.random.normal(stream_key, dims, jnp.float32) * scale * level
    return jnp.minimum(jnp.maximum(drawn, -most), most).astype(kind)


def setup_inputs(seed: int = 0) -> dict:
    arg_keys = jax.random.split(jax.random.key(seed), 12)
    return {
        "tokens": scatter_about(arg_keys[0], (MB, SEQS, LENGTH, D), 1.0, 6.0, ((1, 4), (2, 8))),
        "cotangent": scatter_about(arg_keys[1], (MB, SEQS, LENGTH, D), 1.0, 6.0, ((1, 4), (2, 8))),
        "norm_in": jnp.clip(1.0 + 0.1 * jax.random.normal(arg_keys[2], (D,), jnp.float32), 0.5, 1.5).astype(jnp.bfloat16),
        "w_in": scatter_about(arg_keys[3], (D, PROJ), D ** -0.5, 0.21875, ((0, 32),)),
        "conv_w": scatter_about(arg_keys[4], (CONV, KW), KW ** -0.5, 3.0, ((0, 32),)),
        "conv_b": scatter_about(arg_keys[5], (CONV,), 0.5, 3.0, ((0, 32),)),
        "dt_bias": jnp.clip(jax.random.uniform(arg_keys[6], (H,), jnp.float32, -5.5, -4.0), -5.5, -4.0),
        "a_log": jnp.clip(jax.random.uniform(arg_keys[7], (H,), jnp.float32, -3.9, 1.6), -3.9, 1.6),
        "skip": jnp.clip(jax.random.uniform(arg_keys[8], (H,), jnp.float32, 0.5, 1.5), 0.5, 1.5),
        "norm_out": jnp.clip(1.0 + 0.1 * jax.random.normal(arg_keys[9], (DI,), jnp.float32), 0.5, 1.5).astype(jnp.bfloat16),
        "w_out": scatter_about(arg_keys[10], (DI, D), DI ** -0.5, 0.15625, ((0, 32),)),
    }


epsilon = 1e-05

@jax.custom_vjp
def low(v):
    return lax.optimization_barrier(v.astype(jnp.bfloat16)).astype(jnp.float32)

@jax.custom_vjp
def low_back(v):
    return v

def low_keep(v):
    return (low(v), None)

def low_pass(kept, grad):
    return (grad,)

def back_keep(v):
    return (v, None)

def back_low(kept, grad):
    return (low(grad),)
low.defvjp(low_keep, low_pass)
low_back.defvjp(back_keep, back_low)

def product(left, right):
    return jnp.dot(left, right, precision=lax.Precision.HIGHEST)

def forward_seq(sequence, norm_in, w_in, conv_w, conv_b, dt_bias, a_log, skip, norm_out, w_out):
    inner = H * HP
    length = sequence.shape[0]
    blocks = length // PIECE
    hidden = low(sequence * lax.rsqrt(lax.optimization_barrier(jnp.mean(sequence * sequence, axis=-1, keepdims=True)) + epsilon) * norm_in)
    projected = low(low_back(product(hidden, w_in)))
    gate_part = projected[:, :inner]
    conv_in = projected[:, inner:2 * inner + 2 * N]
    raw_step = projected[:, 2 * inner + 2 * N:]
    padded = jnp.concatenate([jnp.zeros((KW - 1, conv_in.shape[1]), jnp.float32), conv_in], axis=0)
    summed = conv_b
    for shift_k in range(KW):
        summed = summed + conv_w[:, shift_k] * padded[shift_k:shift_k + length]
    activated = low(jax.nn.silu(summed))
    values = activated[:, :inner].reshape(blocks, PIECE, H, HP)
    bmat = activated[:, inner:inner + N].reshape(blocks, PIECE, N)
    cmat = activated[:, inner + N:].reshape(blocks, PIECE, N)
    step_size = jax.nn.softplus(raw_step + dt_bias)
    rates = (step_size * -jnp.exp(a_log)).reshape(blocks, PIECE, H)
    step_blocks = step_size.reshape(blocks, PIECE, H)
    lower = (jnp.arange(PIECE)[:, None] >= jnp.arange(PIECE)[None, :])[:, :, None]
    highest = lax.Precision.HIGHEST

    def span_step(state, inputs):
        block_vals, block_b, block_c, block_step, block_rate = inputs
        cumul = jnp.cumsum(block_rate, axis=0)
        scores = low_back(product(block_c, block_b.T))
        differ = cumul[:, None, :] - cumul[None, :, :]
        decay = jnp.where(lower, jnp.exp(jnp.where(lower, differ, 0.0)), 0.0)
        mixing = low(scores[:, :, None] * decay * block_step[None, :, :])
        intra = jnp.einsum('tsh,shp->thp', mixing, block_vals, precision=highest)
        offset = low_back(jnp.einsum('tn,hpn->thp', block_c, low(state), precision=highest))
        result = intra + jnp.exp(cumul)[:, :, None] * offset + skip[None, :, None] * block_vals
        weights = low(jnp.exp(cumul[-1][None, :] - cumul)[:, :, None] * block_step[:, :, None] * block_vals)
        local_state = low_back(jnp.einsum('shp,sn->hpn', weights, block_b, precision=highest))
        new_state = jnp.exp(cumul[-1])[:, None, None] * state + local_state
        return (new_state, result)
    start = jnp.zeros((H, HP, N), jnp.float32)
    _, pieces = lax.scan(jax.checkpoint(span_step), start, (values, bmat, cmat, step_blocks, rates))
    ssd = low_back(pieces.reshape(length, inner))
    gated = ssd * jax.nn.silu(gate_part)
    normed = low(gated * lax.rsqrt(lax.optimization_barrier(jnp.mean(gated * gated, axis=-1, keepdims=True)) + epsilon) * norm_out)
    return sequence + product(normed, w_out)

def reference(tokens, cotangent, norm_in, w_in, conv_w, conv_b, dt_bias, a_log, skip, norm_out, w_out):
    params = tuple((p.astype(jnp.float32) for p in (norm_in, w_in, conv_w, conv_b, dt_bias, a_log, skip, norm_out, w_out)))
    flat_tokens = tokens.reshape(-1, SEQ_LEN, D).astype(jnp.float32)
    flat_cot = cotangent.reshape(-1, SEQ_LEN, D).astype(jnp.float32)

    def per_sequence(totals, pair):
        sequence, tangent = pair
        result, pull = jax.vjp(forward_seq, sequence, *params)
        grads = pull(tangent)
        totals = tuple((a + b for a, b in zip(totals, grads[1:])))
        return (totals, (result.astype(jnp.bfloat16), grads[0].astype(jnp.bfloat16)))
    zeros = tuple((jnp.zeros_like(p) for p in params))
    totals, (outputs, grad_flat) = lax.scan(per_sequence, zeros, (flat_tokens, flat_cot))
    block_out = outputs.reshape(tokens.shape)
    grad_tokens = grad_flat.reshape(tokens.shape)
    return (block_out, grad_tokens, totals[0], totals[1], totals[2], totals[3], totals[4], totals[5], totals[6], totals[7], totals[8])
```

```python
import math

import jax
import jax.numpy as jnp
from jax import lax
from jax.experimental import pallas as pl
from jax.experimental.pallas import tpu as pltpu
from jax.sharding import Mesh
from jax.sharding import PartitionSpec as P

H = 24
HP = 64
N = 128
KW = 4
SEQ_LEN = 2048
PIECE = 256
D = 768
DI = H * HP
CONV = DI + 2 * N
PC = 1920
GROUPS = 3
GC = PC // GROUPS
NEAR = SEQ_LEN // PIECE
NB = N // NEAR
HALO = 16
LANES = 128
EPS = 1e-05
F32 = jnp.float32
BF16 = jnp.bfloat16
AX = ("dp", "far", "near")
MIB = 1 << 20


def dot(a, b):
    return lax.dot_general(a, b, (((1,), (0,)), ((), ())), preferred_element_type=F32)


def dot_nt(a, b):
    return lax.dot_general(a, b, (((1,), (1,)), ((), ())), preferred_element_type=F32)


def dot_tn(a, b):
    return lax.dot_general(a, b, (((0,), (0,)), ((), ())), preferred_element_type=F32)


def split(x):
    high = x.astype(BF16)
    return high, (x - high.astype(F32)).astype(BF16)


def heads_to_lanes():
    head = lax.broadcasted_iota(jnp.int32, (LANES, DI), 0)
    lane = lax.broadcasted_iota(jnp.int32, (LANES, DI), 1)
    return jnp.where((lane >> 6) == head, 1.0, 0.0).astype(BF16)


def expand(x, spread):
    high, low = split(x)
    return dot(high, spread) + dot(low, spread)


def collect(high, low, spread):
    return dot_nt(high, spread) + dot_nt(low, spread)


def triangle(count, lower):
    row = lax.broadcasted_iota(jnp.int32, (count, count), 0)
    col = lax.broadcasted_iota(jnp.int32, (count, count), 1)
    return (row >= col) if lower else (row <= col)


def running(mask, x):
    ones = jnp.where(mask, 1.0, 0.0).astype(BF16)
    high, rest = split(x)
    left = x - high.astype(F32)
    mid, low = split(left)
    return dot(ones, high) + dot(ones, mid) + dot(ones, low)


def softplus(z):
    e = jnp.exp(-jnp.abs(z))
    near = e * (1.0 + e * (-0.5 + e * (1.0 / 3.0 + e * (-0.25 + e * 0.2))))
    return jnp.maximum(z, 0.0) + jnp.where(e < 0.02, near, jnp.log(1.0 + e))


def params(limit):
    return pltpu.CompilerParams(vmem_limit_bytes=limit * MIB)


def cost(flops, nbytes, trans=0):
    return pl.CostEstimate(flops=int(flops), bytes_accessed=int(nbytes), transcendentals=int(trans))


def whole(shape):
    return pl.BlockSpec(shape, lambda *_: (0,) * len(shape))


def per_row(shape):
    return pl.BlockSpec((1,) + shape, lambda r: (r,) + (0,) * len(shape))


def struct(shape, kind):
    return jax.ShapeDtypeStruct(shape, kind)


def assemble(core, mine, recv, weight_s):
    count, rows, _ = mine[0].shape
    for g in range(GROUPS):
        cols = slice(g * GC, (g + 1) * GC)
        for y in range(count):
            first = pl.multiple_of((2 * y + core) * rows, 16)
            other = pl.multiple_of((2 * y + 1 - core) * rows, 16)
            weight_s[pl.ds(first, rows), cols] = mine[g][y]
            weight_s[pl.ds(other, rows), cols] = recv[g][y]


def enter_kernel(
    core_ref, tok, halo, m0, m1, m2, r0, r1, r2, par, heads,
    hid, conv, raw, act, dsilu, step, cum, pay, weight, ext
):
    @pl.when(pl.program_id(0) == 0)
    def _():
        assemble(core_ref[0], (m0, m1, m2), (r0, r1, r2), weight)

    gain = par[5:6, :D].astype(F32)
    rows = jnp.concatenate([halo[0], tok[0]], axis=0).astype(F32)
    scale = lax.rsqrt(jnp.mean(rows * rows, axis=-1, keepdims=True) + EPS)
    hidden = (rows * scale * gain).astype(BF16)
    hid[0] = hidden[HALO:]
    for t in range(CONV // 256):
        cols = slice(t * 256, (t + 1) * 256)
        part = dot(hidden, weight[:, cols]).astype(BF16)
        conv[0, :, cols] = part
        ext[:, cols] = part.astype(F32)
    for t in range(CONV // LANES):
        cols = slice(t * LANES, (t + 1) * LANES)
        total = par[4:5, cols].astype(F32)
        for k in range(KW):
            total = total + par[k : k + 1, cols].astype(F32) * ext[pl.ds(HALO - KW + 1 + k, PIECE), cols]
        gate = jax.nn.sigmoid(total)
        act[0, :, cols] = (total * gate).astype(BF16)
        dsilu[0, :, cols] = gate * (1.0 + total * (1.0 - gate))
    raw_step = dot(hidden[HALO:], weight[:, CONV:]).astype(BF16).astype(F32)
    raw[0] = raw_step
    size = softplus(raw_step + heads[0:1])
    cumul = running(triangle(PIECE, True), size * -jnp.exp(heads[1:2]))
    step[0] = size
    cum[0] = cumul
    spread = heads_to_lanes()
    last = cumul[PIECE - 1 :]
    reach = jnp.exp(last - cumul) * size
    bmat = act[0, :, DI : DI + N]
    for t in range(DI // 256):
        cols = slice(t * 256, (t + 1) * 256)
        weights = (expand(reach, spread[:, cols]) * act[0, :, cols].astype(F32)).astype(BF16)
        state = dot_tn(bmat, weights).astype(BF16)
        pay[:, 0, :, cols] = state.reshape(NEAR, NB, 256)
    growth = jnp.exp(last)
    high, low = split(growth)
    row = lax.broadcasted_iota(jnp.int32, (NB, LANES), 0)
    growths = jnp.where(row == 0, high.astype(F32), jnp.where(row == 1, low.astype(F32), 0.0))
    for j in range(NEAR):
        pay[j, 0, :, DI:] = growths.astype(BF16)


def pass_kernel(backward, pieces, growths, out):
    spread = heads_to_lanes()
    count = out.shape[1]
    for r in range(count):
        high = jnp.concatenate([growths[j, r, 0:1, :] for j in range(NEAR)], axis=0)
        low = jnp.concatenate([growths[j, r, 1:2, :] for j in range(NEAR)], axis=0)
        grow = dot(high, spread) + dot(low, spread)
        state = jnp.zeros((NB, DI), F32)
        order = range(NEAR - 1, -1, -1) if backward else range(NEAR)
        for j in order:
            out[j, r] = state.astype(BF16)
            state = grow[j : j + 1] * state + pieces[j, r, :, :DI].astype(F32)


def inside_kernel(act, step, cum, intra, xdt_s):
    spread = heads_to_lanes()
    size, cumul = step[0], cum[0]
    for t in range(DI // 256):
        cols = slice(t * 256, (t + 1) * 256)
        xdt_s[:, cols] = (expand(size, spread[:, cols]) * act[0, :, cols].astype(F32)).astype(BF16)
    bmat, cmat = act[0, :, DI : DI + N], act[0, :, DI + N :]
    scores = dot_nt(cmat, bmat)
    lower = triangle(PIECE, True)
    turned = cumul.T
    left = lax.broadcasted_iota(jnp.int32, (PIECE, LANES), 1) < HP
    for pair in range(H // 2):
        cols = slice(pair * LANES, (pair + 1) * LANES)
        xdt = xdt_s[:, cols]
        both = []
        for h in (2 * pair, 2 * pair + 1):
            differ = cumul[:, h : h + 1] - turned[h : h + 1, :]
            mix = (scores * jnp.exp(jnp.where(lower, differ, -1e30))).astype(BF16)
            both.append(dot(mix, xdt))
        intra[0, :, cols] = jnp.where(left, both[0], both[1])


def gate_kernel(hid, cot, wg0, wg1, wo, gate, dnorm):
    gate[0, :, :D] = dot(hid[0], wg0[...]).astype(BF16)
    gate[0, :, D:] = dot(hid[0], wg1[...]).astype(BF16)
    dnorm[0] = dot_nt(cot[0], wo[...])


def middle_kernel(
    st, act, intra, cum, gate, dnorm, par, heads,
    normed, dgate, dy, reach, pay, sums, off_s, grow_s, high_s, low_s, doff_s, sum_s
):
    spread = heads_to_lanes()
    state = st[:, 0].reshape(N, DI)
    cmat = act[0, :, DI + N :]
    off_s[...] = dot(cmat, state)
    grow_s[...] = expand(jnp.exp(cum[0]), spread)
    skip = expand(jnp.broadcast_to(heads[2:3], (8, LANES)), spread)[0:1]
    gain = par[6:7, :DI].astype(F32)
    sum_s[...] = jnp.zeros_like(sum_s)
    size = 16

    def chunk(i, carry):
        at = pl.ds(pl.multiple_of(i * size, size), size)
        value = act[0, at, :DI].astype(F32)
        grow = grow_s[at, :]
        base = intra[0, at, :] + grow * off_s[at, :]
        ssd = base + skip * value
        z = gate[0, at, :].astype(F32)
        sig = jax.nn.sigmoid(z)
        silu = z * sig
        gated = ssd * silu
        scale = lax.rsqrt(jnp.mean(gated * gated, axis=-1, keepdims=True) + EPS)
        unit = gated * scale
        normed[0, at, :] = (unit * gain).astype(BF16)
        d_normed = dnorm[0, at, :]
        sum_s[0:8] += (d_normed * unit).reshape(size // 8, 8, DI).sum(axis=0)
        d_unit = d_normed * gain
        along = jnp.mean(d_unit * unit, axis=-1, keepdims=True)
        d_gated = scale * (d_unit - unit * along)
        dgate[0, at, :] = (d_gated * ssd * (sig * (1.0 + z * (1.0 - sig)))).astype(BF16)
        d_ssd = (d_gated * silu).astype(BF16)
        dy[0, at, :] = d_ssd
        d_ssd = d_ssd.astype(F32)
        doff_s[at, :] = (grow * d_ssd).astype(BF16)
        sum_s[8:16] += (d_ssd * value).reshape(size // 8, 8, DI).sum(axis=0)
        high, low = split(d_ssd * base)
        high_s[at, :] = high
        low_s[at, :] = low
        return carry

    lax.fori_loop(0, PIECE // size, chunk, 0)
    d_state = dot_tn(cmat, doff_s[...]).astype(BF16)
    pay[:, 0] = d_state.reshape(NEAR, NB, DI)
    reach[0] = collect(high_s[...], low_s[...], spread)
    high, low = split(sum_s[8:16])
    sums[0, 0:8] = sum_s[0:8]
    sums[0, 8:16, :LANES] = collect(high, low, spread)
    sums[0, 8:16, LANES:] = jnp.zeros((8, DI - LANES), F32)


def outer_kernel(core_ref, tok, cot, hid, normed, dgate, wo, out, keep, send, total):
    core = core_ref[0]
    count = tok.shape[0]
    for r in range(count):
        out[r] = (tok[r].astype(F32) + dot(normed[r], wo[...])).astype(BF16)
    tangent = cot[...].reshape(count * PIECE, D)
    hidden = hid[...].reshape(count * PIECE, D)
    blocks = keep.shape[0]
    left = [
        dot_tn(normed[...].reshape(count * PIECE, DI), tangent),
        dot_tn(hidden, dgate[:, :, :D].reshape(count * PIECE, D)),
        dot_tn(hidden, dgate[:, :, D:].reshape(count * PIECE, D)),
    ]
    base = 0
    for part in left:
        total[: part.shape[0]] = part
        rows = part.shape[0] // (2 * blocks)
        for y in range(blocks):
            mine = pl.multiple_of((2 * y + core) * rows, 16)
            other = pl.multiple_of((2 * y + 1 - core) * rows, 16)
            keep[y, base : base + rows] = total[pl.ds(mine, rows)]
            send[y, base : base + rows] = total[pl.ds(other, rows)].astype(BF16)
        base += rows


def pair_kernel(act, step, cum, dy, st, u, dcm, dbm, xdt_s, doff_s, dsc_s):
    spread = heads_to_lanes()
    size, cumul = step[0], cum[0]
    grown = jnp.exp(cumul)
    for t in range(DI // 256):
        cols = slice(t * 256, (t + 1) * 256)
        xdt_s[:, cols] = (expand(size, spread[:, cols]) * act[0, :, cols].astype(F32)).astype(BF16)
        doff_s[:, cols] = (expand(grown, spread[:, cols]) * dy[0, :, cols].astype(F32)).astype(BF16)
    bmat, cmat = act[0, :, DI : DI + N], act[0, :, DI + N :]
    scores = dot_nt(cmat, bmat)
    lower = triangle(PIECE, True)
    turned = cumul.T
    dsc_s[...] = jnp.zeros_like(dsc_s)
    left = lax.broadcasted_iota(jnp.int32, (PIECE, LANES), 1) < HP
    zero = jnp.zeros((PIECE, LANES), BF16)
    for pair in range(H // 2):
        cols = slice(pair * LANES, (pair + 1) * LANES)
        xdt = xdt_s[:, cols]
        slope = dy[0, :, cols]
        slope_t = slope.astype(F32).T.astype(BF16)
        both = []
        for side in (0, 1):
            h = 2 * pair + side
            differ = cumul[:, h : h + 1] - turned[h : h + 1, :]
            decay = jnp.exp(jnp.where(lower, differ, -1e30))
            mix = (scores * decay).astype(BF16)
            own = jnp.where(left, slope, zero) if side == 0 else jnp.where(left, zero, slope)
            dsc_s[...] += dot_nt(own, xdt) * decay
            both.append(dot(slope_t[side * HP : (side + 1) * HP], mix))
        u[0, :, cols] = jnp.concatenate(both, axis=0).T
    d_scores = dsc_s[...].astype(BF16)
    state = st[:, 0].reshape(N, DI)
    dcm[0] = dot_nt(doff_s[...], state) + dot(d_scores, bmat)
    dbm[0] = dot_tn(d_scores, cmat)


def back_kernel(
    later, st, act, cum, step, raw, u, dcm, dbm, dy, dsilu, reach, heads,
    dpre, edge, draw, hsum, dw_s, far_s, size_s, high_s, low_s, wts_s, sum_s
):
    spread = heads_to_lanes()
    size, cumul = step[0], cum[0]
    last = cumul[PIECE - 1 :]
    d_local = later[:, 0].reshape(N, DI)
    bmat = act[0, :, DI : DI + N]
    dw_s[...] = dot(bmat, d_local)
    far_s[...] = expand(jnp.exp(last - cumul), spread)
    size_s[...] = expand(size, spread)
    skip = expand(jnp.broadcast_to(heads[2:3], (8, LANES)), spread)[0:1]
    sum_s[...] = jnp.zeros_like(sum_s)
    rows = 16

    def chunk(i, carry):
        at = pl.ds(pl.multiple_of(i * rows, rows), rows)
        value = act[0, at, :DI].astype(F32)
        far, long = far_s[at, :], size_s[at, :]
        through = far * dw_s[at, :]
        d_xdt = u[0, at, :] + through
        d_value = long * d_xdt + skip * dy[0, at, :].astype(F32)
        dpre[0, at, :DI] = d_value * dsilu[0, at, :DI]
        high, low = split(value * d_xdt)
        high_s[at, :] = high
        low_s[at, :] = low
        xdt = long * value
        wts_s[at, :] = (far * xdt).astype(BF16)
        sum_s[0:8] += (xdt * through).reshape(rows // 8, 8, DI).sum(axis=0)
        return carry

    lax.fori_loop(0, PIECE // rows, chunk, 0)
    for j in range(NEAR):
        prod = later[j, 0].astype(F32) * st[j, 0].astype(F32)
        sum_s[8:16] += prod.reshape(NB // 8, 8, DI).sum(axis=0)
    d_bmat = dbm[0] + dot_nt(wts_s[...], d_local)
    dpre[0, :, DI : DI + N] = d_bmat * dsilu[0, :, DI : DI + N]
    dpre[0, :, DI + N :] = dcm[0] * dsilu[0, :, DI + N :]
    edge[0] = dpre[0, 0:8, :]
    q = collect(high_s[...], low_s[...], spread)
    high, low = split(sum_s[...])
    sums = collect(high, low, spread)
    d_last = jnp.sum(sums[0:8], axis=0, keepdims=True)
    d_last = d_last + jnp.exp(last) * jnp.sum(sums[8:16], axis=0, keepdims=True)
    d_cum = reach[0] - size * q
    row = lax.broadcasted_iota(jnp.int32, (PIECE, LANES), 0)
    d_cum = d_cum + jnp.where(row == PIECE - 1, d_last, 0.0)
    d_rate = running(triangle(PIECE, False), d_cum)
    decay = jnp.exp(heads[1:2])
    d_size = q - d_rate * decay
    d_raw = d_size * jax.nn.sigmoid(raw[0] + heads[0:1])
    draw[0] = d_raw
    for_bias = jnp.sum(d_raw, axis=0, keepdims=True)
    for_log = -jnp.sum(d_rate * size, axis=0, keepdims=True) * decay
    pick = lax.broadcasted_iota(jnp.int32, (8, LANES), 0)
    hsum[0] = jnp.where(pick == 0, for_bias, jnp.where(pick == 1, for_log, 0.0))


def input_kernel(core_ref, dpre, edge, draw, hid, par, dproj, k0, k1, k2, s0, s1, s2, ext, total):
    core = core_ref[0]
    count = dpre.shape[0]
    for r in range(count):
        ext[:PIECE] = dpre[r]
        ext[PIECE:] = edge[r]
        for t in range(CONV // LANES):
            cols = slice(t * LANES, (t + 1) * LANES)
            sum_k = par[KW - 1 : KW, cols].astype(F32) * ext[0:PIECE, cols]
            for k in range(KW - 1):
                sum_k = sum_k + par[k : k + 1, cols].astype(F32) * ext[pl.ds(KW - 1 - k, PIECE), cols]
            dproj[r, :, cols] = sum_k.astype(BF16)
        dproj[r, :, CONV:] = draw[r].astype(BF16)
    hidden = hid[...].reshape(count * PIECE, D)
    for g, (keep, send) in enumerate(((k0, s0), (k1, s1), (k2, s2))):
        total[...] = dot_tn(hidden, dproj[:, :, g * GC : (g + 1) * GC].reshape(count * PIECE, GC))
        blocks, rows, _ = keep.shape
        for y in range(blocks):
            mine = pl.multiple_of((2 * y + core) * rows, 16)
            other = pl.multiple_of((2 * y + 1 - core) * rows, 16)
            keep[y] = total[pl.ds(mine, rows)]
            send[y] = total[pl.ds(other, rows)].astype(BF16)


def token_kernel(
    tok, cot, dgate, dproj, wg0, wg1, weight, par, dpre, conv, sums, hsum,
    grad, small, dh_s, ext, acc
):
    r = pl.program_id(0)
    dh_s[...] = (
        dot_nt(dgate[0, :, :D], wg0[...])
        + dot_nt(dgate[0, :, D:], wg1[...])
        + dot_nt(dproj[0], weight[...])
    )
    gain = par[5:6, :D].astype(F32)

    @pl.when(r == 0)
    def _():
        acc[...] = jnp.zeros_like(acc)
        small[...] = jnp.zeros_like(small)

    rows = 32

    def chunk(i, carry):
        at = pl.ds(pl.multiple_of(i * rows, rows), rows)
        x = tok[0, at, :].astype(F32)
        scale = lax.rsqrt(jnp.mean(x * x, axis=-1, keepdims=True) + EPS)
        unit = x * scale
        d_hidden = dh_s[at, :]
        acc[...] += (d_hidden * unit).reshape(rows // 8, 8, D).sum(axis=0)
        d_unit = d_hidden * gain
        along = jnp.mean(d_unit * unit, axis=-1, keepdims=True)
        grad[0, at, :] = (cot[0, at, :].astype(F32) + scale * (d_unit - unit * along)).astype(BF16)
        return carry

    lax.fori_loop(0, PIECE // rows, chunk, 0)
    for t in range(CONV // LANES):
        cols = slice(t * LANES, (t + 1) * LANES)
        slope = dpre[0, :, cols]
        ext[...] = conv[0, :, cols].astype(F32)
        for k in range(KW):
            prod = slope * ext[pl.ds(HALO - KW + 1 + k, PIECE), :]
            small[k : k + 1, cols] += jnp.sum(prod, axis=0, keepdims=True)
        small[4:5, cols] += jnp.sum(slope, axis=0, keepdims=True)
    small[6:7, :DI] += jnp.sum(sums[0, 0:8], axis=0, keepdims=True)
    small[7:8, 0:LANES] += hsum[0, 0:1]
    small[7:8, LANES : 2 * LANES] += hsum[0, 1:2]
    small[7:8, 2 * LANES : 3 * LANES] += jnp.sum(sums[0, 8:16, :LANES], axis=0, keepdims=True)

    @pl.when(r == pl.num_programs(0) - 1)
    def _():
        small[5:6, :D] = jnp.sum(acc[...], axis=0, keepdims=True)


def local(size, tokens, cotangent, norm_in, w_in, conv_w, conv_b, dt_bias, a_log, skip, norm_out, w_out):
    devices, along = size
    bits = int(math.log2(devices))
    core_bit = int(math.log2(along))
    me = lax.axis_index(AX)
    core = ((me >> core_bit) & 1).astype(jnp.int32)
    core_arg = core.reshape(1)
    high_bits = list(range(bits - 1, core_bit, -1))
    far_bits = list(range(core_bit - 1, -1, -1))
    dims = [far_bits[-1:], far_bits[:-1], high_bits] if core_bit == 3 else [far_bits[-3:], far_bits[:-3], high_bits]
    orders = [
        dims[1] + dims[2] + dims[0],
        dims[0] + dims[1] + dims[2],
        dims[2] + dims[0] + dims[1],
    ]

    def swap(x, bit):
        return lax.ppermute(x, AX, [(i, i ^ (1 << bit)) for i in range(devices)])

    def bit_of(bit):
        return (me >> bit) & 1

    def gather(x, order):
        have = []
        for bit in order:
            other = swap(x, bit)
            have = sorted(have + [bit], reverse=True)
            mine = bit_of(bit) == 0
            low, high = jnp.where(mine, x, other), jnp.where(mine, other, x)
            x = jnp.stack([low, high], axis=have.index(bit))
        return x

    def scatter(x, order):
        have = sorted(order, reverse=True)
        for bit in order:
            axis = have.index(bit)
            mine = lax.dynamic_index_in_dim(x, bit_of(bit), axis, False)
            other = lax.dynamic_index_in_dim(x, 1 - bit_of(bit), axis, False)
            x = mine + swap(other.astype(BF16), bit).astype(F32)
            have.remove(bit)
        return x

    micro, batch, count = tokens.shape[:3]
    tok = tokens.reshape(micro * batch, count, D)
    cot = cotangent.reshape(micro * batch, count, D)
    R = micro * batch
    heads = jnp.zeros((8, LANES), F32)
    for i, a in enumerate((dt_bias, a_log, skip)):
        heads = heads.at[i, :H].set(a)

    own_conv, own_in, own_out = conv_b.shape[0], norm_in.shape[0], norm_out.shape[0]
    par = jnp.zeros((8, CONV), BF16)
    taps = jnp.concatenate([conv_w.T, conv_b[None]], axis=0)
    par = lax.dynamic_update_slice(par, taps, (0, me * own_conv))
    par = lax.dynamic_update_slice(par, norm_in[None], (5, me * own_in))
    par = lax.dynamic_update_slice(par, norm_out[None], (6, me * own_out))
    for bit in range(bits):
        par = par + swap(par, bit)

    halo = lax.ppermute(tok[:, count - HALO :], "near", [(i, i + 1) for i in range(NEAR - 1)])
    rows_in = w_in.shape[0]
    first = jnp.pad(w_in[:, DI:], ((0, 0), (0, PC - (w_in.shape[1] - DI))))
    blocks = devices // (2 * along)
    mine, recv = [], []
    for g in range(GROUPS):
        part = gather(first[:, g * GC : (g + 1) * GC], orders[g])
        part = part.reshape(blocks, along * rows_in, GC)
        mine.append(part)
        recv.append(swap(part, core_bit))

    rest = jnp.concatenate([w_in[:, :D], w_in[:, D:DI], w_out], axis=0)
    rest = lax.all_gather(rest, AX, axis=0, tiled=False)
    wg0 = rest[:, :rows_in].reshape(D, D)
    wg1 = rest[:, rows_in : 2 * rows_in].reshape(D, D)
    wo = rest[:, 2 * rows_in :].reshape(DI, D)

    smem = pl.BlockSpec(memory_space=pltpu.SMEM)
    half = (blocks, along * rows_in, GC)
    par_spec, head_spec = whole((8, CONV)), whole((8, LANES))
    row_d, row_i, row_c = per_row((PIECE, D)), per_row((PIECE, DI)), per_row((PIECE, CONV))
    row_l = per_row((PIECE, LANES))
    state_spec = pl.BlockSpec((NEAR, 1, NB, DI), lambda r: (0, r, 0, 0))
    hid, conv, raw, act, dsilu, step, cum, pay, weight = pl.pallas_call(
        enter_kernel,
        grid=(R,),
        in_specs=[smem, row_d, per_row((HALO, D))] + [whole(half)] * 6 + [par_spec, head_spec],
        out_specs=[
            row_d, per_row((HALO + PIECE, CONV)), row_l, row_c, row_c, row_l, row_l,
            pl.BlockSpec((NEAR, 1, NB, DI + LANES), lambda r: (0, r, 0, 0)),
            whole((D, PC)),
        ],
        out_shape=[
            struct((R, PIECE, D), BF16), struct((R, HALO + PIECE, CONV), BF16), struct((R, PIECE, LANES), F32),
            struct((R, PIECE, CONV), BF16), struct((R, PIECE, CONV), F32), struct((R, PIECE, LANES), F32),
            struct((R, PIECE, LANES), F32), struct((NEAR, R, NB, DI + LANES), BF16), struct((D, PC), BF16),
        ],
        scratch_shapes=[pltpu.VMEM((HALO + PIECE, CONV), F32)],
        compiler_params=params(44),
        cost_estimate=cost(R * 2e9, 2e7),
        name="enter",
    )(core_arg, tok, halo, *mine, *recv, par, heads)

    def exchange(x):
        return lax.all_to_all(x, "near", split_axis=0, concat_axis=0, tiled=True)

    def carry_on(pieces, growths, backward):
        shape = pieces.shape
        def kernel(p, g, o):
            pass_kernel(backward, p, g, o)
        return pl.pallas_call(
            kernel,
            grid=(1,),
            in_specs=[whole(shape), pl.BlockSpec((NEAR, R, NB, LANES), lambda r: (0, 0, 0, DI // LANES))],
            out_specs=whole((NEAR, R, NB, DI)),
            out_shape=struct((NEAR, R, NB, DI), BF16),
            compiler_params=params(16),
            cost_estimate=cost(1e7, 2e6),
            name="pass",
        )(pieces, growths)

    pieces = exchange(pay)
    intra = pl.pallas_call(
        inside_kernel,
        grid=(R,),
        in_specs=[row_c, row_l, row_l],
        out_specs=row_i,
        out_shape=struct((R, PIECE, DI), F32),
        scratch_shapes=[pltpu.VMEM((PIECE, DI), BF16)],
        compiler_params=params(32),
        cost_estimate=cost(R * 4e9, 5e6),
        name="inside",
    )(act, step, cum)
    gate, dnorm = pl.pallas_call(
        gate_kernel,
        grid=(R,),
        in_specs=[row_d, row_d, whole((D, D)), whole((D, D)), whole((DI, D))],
        out_specs=[row_i, row_i],
        out_shape=[struct((R, PIECE, DI), BF16), struct((R, PIECE, DI), F32)],
        compiler_params=params(32),
        cost_estimate=cost(R * 2e9, 1e7),
        name="gates",
    )(hid, cot, wg0, wg1, wo)
    st = exchange(carry_on(pieces, pieces, False))

    wide = pltpu.VMEM((PIECE, DI), F32)
    slim = pltpu.VMEM((PIECE, DI), BF16)
    normed, dgate, dy, reach, back, sums = pl.pallas_call(
        middle_kernel,
        grid=(R,),
        in_specs=[state_spec, row_c, row_i, row_l, row_i, row_i, par_spec, head_spec],
        out_specs=[row_i, row_i, row_i, row_l, state_spec, per_row((16, DI))],
        out_shape=[
            struct((R, PIECE, DI), BF16), struct((R, PIECE, DI), BF16), struct((R, PIECE, DI), BF16),
            struct((R, PIECE, LANES), F32), struct((NEAR, R, NB, DI), BF16), struct((R, 16, DI), F32),
        ],
        scratch_shapes=[wide, wide, slim, slim, slim, pltpu.VMEM((16, DI), F32)],
        compiler_params=params(40),
        cost_estimate=cost(R * 2e9, 1.5e7),
        name="middle",
    )(st, act, intra, cum, gate, dnorm, par, heads)

    pieces_b = exchange(back)
    rest_rows = (DI + 2 * D) // (2 * blocks)
    block_out, keep, send = pl.pallas_call(
        outer_kernel,
        grid=(1,),
        in_specs=[
            smem, whole((R, PIECE, D)), whole((R, PIECE, D)), whole((R, PIECE, D)),
            whole((R, PIECE, DI)), whole((R, PIECE, DI)), whole((DI, D)),
        ],
        out_specs=[whole((R, PIECE, D)), whole((blocks, rest_rows, D)), whole((blocks, rest_rows, D))],
        out_shape=[
            struct((R, PIECE, D), BF16), struct((blocks, rest_rows, D), F32), struct((blocks, rest_rows, D), BF16),
        ],
        scratch_shapes=[pltpu.VMEM((DI, D), F32)],
        compiler_params=params(48),
        cost_estimate=cost(6e9, 2e7),
        name="outer",
    )(core_arg, tok, cot, hid, normed, dgate, wo)
    part = (keep + swap(send, core_bit).astype(F32)).reshape((2,) * len(high_bits) + (rest_rows, D))
    part = scatter(part, high_bits)
    cuts = (DI // (2 * blocks), D // (2 * blocks))
    part = jnp.concatenate(
        [
            part[: cuts[0]].reshape(along, cuts[0] // along, D),
            part[cuts[0] : cuts[0] + cuts[1]].reshape(along, rows_in, D),
            part[cuts[0] + cuts[1] :].reshape(along, rows_in, D),
        ],
        axis=1,
    )
    own = lax.psum_scatter(part, ("far", "near"), scatter_dimension=0, tiled=False)
    rows_out = w_out.shape[0]
    g_wout = own[:rows_out]
    g_gate = jnp.concatenate([own[rows_out : rows_out + rows_in], own[rows_out + rows_in :]], axis=1)

    u, dcm, dbm = pl.pallas_call(
        pair_kernel,
        grid=(R,),
        in_specs=[row_c, row_l, row_l, row_i, state_spec],
        out_specs=[row_i, row_l, row_l],
        out_shape=[struct((R, PIECE, DI), F32), struct((R, PIECE, N), F32), struct((R, PIECE, N), F32)],
        scratch_shapes=[slim, slim, pltpu.VMEM((PIECE, PIECE), F32)],
        compiler_params=params(40),
        cost_estimate=cost(R * 8e9, 1e7),
        name="pair",
    )(act, step, cum, dy, st)
    later = exchange(carry_on(pieces_b, pieces, True))

    dpre, edge, draw, hsum = pl.pallas_call(
        back_kernel,
        grid=(R,),
        in_specs=[
            state_spec, state_spec, row_c, row_l, row_l, row_l, row_i, row_l, row_l, row_i, row_c, row_l, head_spec,
        ],
        out_specs=[row_c, per_row((8, CONV)), row_l, per_row((8, LANES))],
        out_shape=[
            struct((R, PIECE, CONV), F32), struct((R, 8, CONV), F32),
            struct((R, PIECE, LANES), F32), struct((R, 8, LANES), F32),
        ],
        scratch_shapes=[wide, wide, wide, slim, slim, slim, pltpu.VMEM((16, DI), F32)],
        compiler_params=params(44),
        cost_estimate=cost(R * 2e9, 1.5e7),
        name="back",
    )(later, st, act, cum, step, raw, u, dcm, dbm, dy, dsilu, reach, heads)
    edge = lax.ppermute(edge, "near", [(i + 1, i) for i in range(NEAR - 1)])

    dproj, k0, k1, k2, s0, s1, s2 = pl.pallas_call(
        input_kernel,
        grid=(1,),
        in_specs=[
            smem, whole((R, PIECE, CONV)), whole((R, 8, CONV)), whole((R, PIECE, LANES)), whole((R, PIECE, D)), par_spec,
        ],
        out_specs=[whole((R, PIECE, PC))] + [whole(half)] * 6,
        out_shape=[struct((R, PIECE, PC), BF16)] + [struct(half, F32)] * 3 + [struct(half, BF16)] * 3,
        scratch_shapes=[pltpu.VMEM((PIECE + 8, CONV), F32), pltpu.VMEM((D, GC), F32)],
        compiler_params=params(44),
        cost_estimate=cost(2e9, 1e7),
        name="input",
    )(core_arg, dpre, edge, draw, hid, par)

    grad_tokens, small = pl.pallas_call(
        token_kernel,
        grid=(R,),
        in_specs=[
            row_d, row_d, row_i, per_row((PIECE, PC)), whole((D, D)), whole((D, D)), whole((D, PC)), par_spec,
            row_c, per_row((HALO + PIECE, CONV)), per_row((16, DI)), per_row((8, LANES)),
        ],
        out_specs=[row_d, whole((8, CONV))],
        out_shape=[struct((R, PIECE, D), BF16), struct((8, CONV), F32)],
        scratch_shapes=[
            pltpu.VMEM((PIECE, D), F32), pltpu.VMEM((HALO + PIECE, LANES), F32), pltpu.VMEM((8, D), F32),
        ],
        compiler_params=params(48),
        cost_estimate=cost(R * 2e9, 1.5e7),
        name="token",
    )(tok, cot, dgate, dproj, wg0, wg1, weight, par, dpre, conv, sums, hsum)

    owned = []
    for g, (keep_g, send_g) in enumerate(((k0, s0), (k1, s1), (k2, s2))):
        part = keep_g + swap(send_g, core_bit).astype(F32)
        part = part.reshape((2,) * (bits - 1) + (rows_in, GC))
        owned.append(scatter(part, orders[g][::-1]))
    g_win = jnp.concatenate([g_gate] + owned, axis=1)[:, : w_in.shape[1]]
    for bit in range(bits):
        small = small + swap(small, bit)
    taps = lax.dynamic_slice(small, (0, me * own_conv), (5, own_conv))
    g_gin = lax.dynamic_slice(small, (5, me * own_in), (1, own_in))[0]
    g_gout = lax.dynamic_slice(small, (6, me * own_out), (1, own_out))[0]
    return (
        block_out.reshape(tokens.shape),
        grad_tokens.reshape(tokens.shape),
        g_gin,
        g_win,
        taps[:KW].T,
        taps[KW],
        small[7, :H],
        small[7, LANES : LANES + H],
        small[7, 2 * LANES : 2 * LANES + H],
        g_gout,
        g_wout,
    )


def solution(mesh):
    dp, seq = mesh.shape["dp"], mesh.shape["seq"]
    inner = Mesh(mesh.devices.reshape(dp, seq // NEAR, NEAR), AX)
    split_seq = ("far", "near")
    act = P(None, "dp", split_seq, None)
    vec, mat = P(AX), P(AX, None)

    def run(*args):
        return local((dp * seq, seq), *args)

    return jax.shard_map(
        run,
        mesh=inner,
        in_specs=(act, act, vec, mat, mat, vec, P(), P(), P(), vec, mat),
        out_specs=(act, act, vec, mat, mat, vec, P(), P(), P(), vec, mat),
        check_vma=False,
    )
```

```python
import functools
import math

import jax
import jax.numpy as jnp
from jax import lax
from jax.experimental import pallas as pl
from jax.experimental.pallas import tpu as pltpu
from jax.sharding import Mesh
from jax.sharding import PartitionSpec as P

H = 24
HP = 64
N = 128
KW = 4
SEQ_LEN = 2048
PIECE = 256
D = 768
DI = H * HP
CONV = DI + 2 * N
PC = 1920
GROUPS = 3
GC = PC // GROUPS
NEAR = SEQ_LEN // PIECE
NB = N // NEAR
HALO = 16
LANES = 128
EPS = 1e-05
F32 = jnp.float32
BF16 = jnp.bfloat16
AX = ("dp", "far", "near")
MIB = 1 << 20


def dot(a, b):
    return lax.dot_general(a, b, (((1,), (0,)), ((), ())), preferred_element_type=F32)


def dot_nt(a, b):
    return lax.dot_general(a, b, (((1,), (1,)), ((), ())), preferred_element_type=F32)


def dot_tn(a, b):
    return lax.dot_general(a, b, (((0,), (0,)), ((), ())), preferred_element_type=F32)


def split(x):
    high = x.astype(BF16)
    return high, (x - high.astype(F32)).astype(BF16)


def heads_to_lanes():
    head = lax.broadcasted_iota(jnp.int32, (LANES, DI), 0)
    lane = lax.broadcasted_iota(jnp.int32, (LANES, DI), 1)
    return jnp.where((lane >> 6) == head, 1.0, 0.0).astype(BF16)


def expand(x, spread):
    high, low = split(x)
    return dot(high, spread) + dot(low, spread)


def collect(high, low, spread):
    return dot_nt(high, spread) + dot_nt(low, spread)


def triangle(count, lower):
    row = lax.broadcasted_iota(jnp.int32, (count, count), 0)
    col = lax.broadcasted_iota(jnp.int32, (count, count), 1)
    return (row >= col) if lower else (row <= col)


def running(mask, x):
    ones = jnp.where(mask, 1.0, 0.0).astype(BF16)
    high, rest = split(x)
    left = x - high.astype(F32)
    mid, low = split(left)
    return dot(ones, high) + dot(ones, mid) + dot(ones, low)


def softplus(z):
    e = jnp.exp(-jnp.abs(z))
    near = e * (1.0 + e * (-0.5 + e * (1.0 / 3.0 + e * (-0.25 + e * 0.2))))
    return jnp.maximum(z, 0.0) + jnp.where(e < 0.02, near, jnp.log(1.0 + e))


def params(limit):
    return pltpu.CompilerParams(vmem_limit_bytes=limit * MIB)


def cost(flops, nbytes, trans=0):
    return pl.CostEstimate(flops=int(flops), bytes_accessed=int(nbytes), transcendentals=int(trans))


def whole(shape):
    return pl.BlockSpec(shape, lambda *_: (0,) * len(shape))


def per_row(shape):
    return pl.BlockSpec((1,) + shape, lambda r: (r,) + (0,) * len(shape))


def struct(shape, kind):
    return jax.ShapeDtypeStruct(shape, kind)


def assemble(core, mine, recv, weight_s):
    count, rows, _ = mine[0].shape
    for g in range(GROUPS):
        cols = slice(g * GC, (g + 1) * GC)
        for y in range(count):
            first = pl.multiple_of((2 * y + core) * rows, 16)
            other = pl.multiple_of((2 * y + 1 - core) * rows, 16)
            weight_s[pl.ds(first, rows), cols] = mine[g][y]
            weight_s[pl.ds(other, rows), cols] = recv[g][y]


def lay_out(weight, par, owned):
    held = weight[:, CONV:]
    for own, kinds in owned:
        rows_in = own * D // CONV if len(kinds) > 1 else (own if kinds[0] == KW + 1 else own // 2)
        devices = D // rows_in
        width = own * devices
        lane = lax.broadcasted_iota(jnp.int32, (LANES, width), 1)
        row = lax.broadcasted_iota(jnp.int32, (LANES, width), 0)
        source = lax.broadcasted_iota(jnp.int32, (devices, D), 1)
        device = lax.broadcasted_iota(jnp.int32, (devices, D), 0)
        place = lax.broadcasted_iota(jnp.int32, (devices, width), 1)
        holder = lax.broadcasted_iota(jnp.int32, (devices, width), 0)
        mine = (place >= holder * own) & (place < holder * own + own)
        for kind in kinds:
            at, block = kind % rows_in, kind // rows_in
            pick = jnp.where(source == device * rows_in + at, 1.0, 0.0).astype(BF16)
            start = H + block * (rows_in * CONV // D)
            spread = jnp.where(row == start + lane % own, 1.0, 0.0).astype(BF16)
            values = dot(dot(pick, held).astype(BF16), spread)
            par[kind : kind + 1, :width] = jnp.sum(jnp.where(mine, values, 0.0), axis=0, keepdims=True)


def enter_kernel(
    owned, core_ref, tok, halo, m0, m1, m2, r0, r1, r2, heads,
    hid, conv, raw, act, dsilu, step, cum, pay, weight, par, ext
):
    @pl.when(pl.program_id(0) == 0)
    def _():
        assemble(core_ref[0], (m0, m1, m2), (r0, r1, r2), weight)
        par[...] = jnp.zeros_like(par)
        lay_out(weight, par, owned)

    gain = par[5:6, :D]
    rows = jnp.concatenate([halo[0], tok[0]], axis=0).astype(F32)
    scale = lax.rsqrt(jnp.mean(rows * rows, axis=-1, keepdims=True) + EPS)
    hidden = (rows * scale * gain).astype(BF16)
    hid[0] = hidden[HALO:]
    for t in range(CONV // 256):
        cols = slice(t * 256, (t + 1) * 256)
        part = dot(hidden, weight[:, cols]).astype(BF16)
        conv[0, :, cols] = part
        ext[:, cols] = part.astype(F32)
    for t in range(CONV // LANES):
        cols = slice(t * LANES, (t + 1) * LANES)
        total = par[4:5, cols]
        for k in range(KW):
            total = total + par[k : k + 1, cols] * ext[pl.ds(HALO - KW + 1 + k, PIECE), cols]
        gate = jax.nn.sigmoid(total)
        act[0, :, cols] = (total * gate).astype(BF16)
        dsilu[0, :, cols] = gate * (1.0 + total * (1.0 - gate))
    raw_step = dot(hidden[HALO:], weight[:, CONV:]).astype(BF16).astype(F32)
    raw_step = jnp.where(lax.broadcasted_iota(jnp.int32, (PIECE, LANES), 1) < H, raw_step, 0.0)
    raw[0] = raw_step
    size = softplus(raw_step + heads[0:1])
    cumul = running(triangle(PIECE, True), size * -jnp.exp(heads[1:2]))
    step[0] = size
    cum[0] = cumul
    spread = heads_to_lanes()
    last = cumul[PIECE - 1 :]
    reach = jnp.exp(last - cumul) * size
    bmat = act[0, :, DI : DI + N]
    for t in range(DI // 256):
        cols = slice(t * 256, (t + 1) * 256)
        weights = (expand(reach, spread[:, cols]) * act[0, :, cols].astype(F32)).astype(BF16)
        state = dot_tn(bmat, weights).astype(BF16)
        pay[:, 0, :, cols] = state.reshape(NEAR, NB, 256)
    growth = jnp.exp(last)
    high, low = split(growth)
    row = lax.broadcasted_iota(jnp.int32, (NB, LANES), 0)
    growths = jnp.where(row == 0, high.astype(F32), jnp.where(row == 1, low.astype(F32), 0.0))
    for j in range(NEAR):
        pay[j, 0, :, DI:] = growths.astype(BF16)


def pass_kernel(backward, pieces, growths, out):
    spread = heads_to_lanes()
    count = out.shape[1]
    for r in range(count):
        high = jnp.concatenate([growths[j, r, 0:1, :] for j in range(NEAR)], axis=0)
        low = jnp.concatenate([growths[j, r, 1:2, :] for j in range(NEAR)], axis=0)
        grow = dot(high, spread) + dot(low, spread)
        state = jnp.zeros((NB, DI), F32)
        order = range(NEAR - 1, -1, -1) if backward else range(NEAR)
        for j in order:
            out[j, r] = state.astype(BF16)
            state = grow[j : j + 1] * state + pieces[j, r, :, :DI].astype(F32)


def inside_kernel(act, step, cum, intra, xdt_s):
    spread = heads_to_lanes()
    size, cumul = step[0], cum[0]
    for t in range(DI // 256):
        cols = slice(t * 256, (t + 1) * 256)
        xdt_s[:, cols] = (expand(size, spread[:, cols]) * act[0, :, cols].astype(F32)).astype(BF16)
    bmat, cmat = act[0, :, DI : DI + N], act[0, :, DI + N :]
    scores = dot_nt(cmat, bmat)
    lower = triangle(PIECE, True)
    turned = cumul.T
    left = lax.broadcasted_iota(jnp.int32, (PIECE, LANES), 1) < HP
    for pair in range(H // 2):
        cols = slice(pair * LANES, (pair + 1) * LANES)
        xdt = xdt_s[:, cols]
        both = []
        for h in (2 * pair, 2 * pair + 1):
            differ = cumul[:, h : h + 1] - turned[h : h + 1, :]
            mix = (scores * jnp.exp(jnp.where(lower, differ, -1e30))).astype(BF16)
            both.append(dot(mix, xdt))
        intra[0, :, cols] = jnp.where(left, both[0], both[1])


def gate_kernel(hid, cot, wg0, wg1, wo, gate, dnorm):
    gate[0, :, :D] = dot(hid[0], wg0[...]).astype(BF16)
    gate[0, :, D:] = dot(hid[0], wg1[...]).astype(BF16)
    dnorm[0] = dot_nt(cot[0], wo[...])


def middle_kernel(
    st, act, intra, cum, gate, dnorm, par, heads,
    normed, dgate, dy, reach, pay, sums, off_s, grow_s, high_s, low_s, doff_s, sum_s
):
    spread = heads_to_lanes()
    state = st[:, 0].reshape(N, DI)
    cmat = act[0, :, DI + N :]
    off_s[...] = dot(cmat, state)
    grow_s[...] = expand(jnp.exp(cum[0]), spread)
    skip = expand(jnp.broadcast_to(heads[2:3], (8, LANES)), spread)[0:1]
    gain = par[6:7, :DI]
    sum_s[...] = jnp.zeros_like(sum_s)
    size = 16

    def chunk(i, carry):
        at = pl.ds(pl.multiple_of(i * size, size), size)
        value = act[0, at, :DI].astype(F32)
        grow = grow_s[at, :]
        base = intra[0, at, :] + grow * off_s[at, :]
        ssd = base + skip * value
        z = gate[0, at, :].astype(F32)
        sig = jax.nn.sigmoid(z)
        silu = z * sig
        gated = ssd * silu
        scale = lax.rsqrt(jnp.mean(gated * gated, axis=-1, keepdims=True) + EPS)
        unit = gated * scale
        normed[0, at, :] = (unit * gain).astype(BF16)
        d_normed = dnorm[0, at, :]
        sum_s[0:8] += (d_normed * unit).reshape(size // 8, 8, DI).sum(axis=0)
        d_unit = d_normed * gain
        along = jnp.mean(d_unit * unit, axis=-1, keepdims=True)
        d_gated = scale * (d_unit - unit * along)
        dgate[0, at, :] = (d_gated * ssd * (sig * (1.0 + z * (1.0 - sig)))).astype(BF16)
        d_ssd = (d_gated * silu).astype(BF16)
        dy[0, at, :] = d_ssd
        d_ssd = d_ssd.astype(F32)
        doff_s[at, :] = (grow * d_ssd).astype(BF16)
        sum_s[8:16] += (d_ssd * value).reshape(size // 8, 8, DI).sum(axis=0)
        high, low = split(d_ssd * base)
        high_s[at, :] = high
        low_s[at, :] = low
        return carry

    lax.fori_loop(0, PIECE // size, chunk, 0)
    d_state = dot_tn(cmat, doff_s[...]).astype(BF16)
    pay[:, 0] = d_state.reshape(NEAR, NB, DI)
    reach[0] = collect(high_s[...], low_s[...], spread)
    high, low = split(sum_s[8:16])
    sums[0, 0:8] = sum_s[0:8]
    sums[0, 8:16, :LANES] = collect(high, low, spread)
    sums[0, 8:16, LANES:] = jnp.zeros((8, DI - LANES), F32)


def outer_kernel(fused, tok, cot, hid, normed, dgate, wo, out, *refs):
    count = tok.shape[0]
    tangent = cot[...].reshape(count * PIECE, D)
    hidden = hid[...].reshape(count * PIECE, D)
    parts = (
        lambda: dot_tn(normed[...].reshape(count * PIECE, DI), tangent),
        lambda: dot_tn(hidden, dgate[:, :, :D].reshape(count * PIECE, D)),
        lambda: dot_tn(hidden, dgate[:, :, D:].reshape(count * PIECE, D)),
    )
    if fused:
        rest, total = refs
        devices = rest.shape[0]
        at = 0
        for part in parts:
            made = part()
            total[at : at + made.shape[0]] = made
            at += made.shape[0]
        long, short = DI // devices, D // devices
        for d in range(devices):
            rest[d] = jnp.concatenate(
                [
                    total[d * long : (d + 1) * long],
                    total[DI + d * short : DI + (d + 1) * short],
                    total[DI + D + d * short : DI + D + (d + 1) * short],
                ],
                axis=0,
            ).astype(BF16)
    else:
        for ref, part in zip(refs, parts):
            ref[...] = part().astype(BF16)
    for r in range(count):
        out[r] = (tok[r].astype(F32) + dot(normed[r], wo[...])).astype(BF16)


def pair_kernel(act, step, cum, dy, st, u, dcm, dbm, xdt_s, doff_s, dsc_s):
    spread = heads_to_lanes()
    size, cumul = step[0], cum[0]
    grown = jnp.exp(cumul)
    for t in range(DI // 256):
        cols = slice(t * 256, (t + 1) * 256)
        xdt_s[:, cols] = (expand(size, spread[:, cols]) * act[0, :, cols].astype(F32)).astype(BF16)
        doff_s[:, cols] = (expand(grown, spread[:, cols]) * dy[0, :, cols].astype(F32)).astype(BF16)
    bmat, cmat = act[0, :, DI : DI + N], act[0, :, DI + N :]
    scores = dot_nt(cmat, bmat)
    lower = triangle(PIECE, True)
    turned = cumul.T
    dsc_s[...] = jnp.zeros_like(dsc_s)
    left = lax.broadcasted_iota(jnp.int32, (PIECE, LANES), 1) < HP
    zero = jnp.zeros((PIECE, LANES), BF16)
    for pair in range(H // 2):
        cols = slice(pair * LANES, (pair + 1) * LANES)
        xdt = xdt_s[:, cols]
        slope = dy[0, :, cols]
        slope_t = slope.astype(F32).T.astype(BF16)
        both = []
        for side in (0, 1):
            h = 2 * pair + side
            differ = cumul[:, h : h + 1] - turned[h : h + 1, :]
            decay = jnp.exp(jnp.where(lower, differ, -1e30))
            mix = (scores * decay).astype(BF16)
            own = jnp.where(left, slope, zero) if side == 0 else jnp.where(left, zero, slope)
            dsc_s[...] += dot_nt(own, xdt) * decay
            both.append(dot(slope_t[side * HP : (side + 1) * HP], mix))
        u[0, :, cols] = jnp.concatenate(both, axis=0).T
    d_scores = dsc_s[...].astype(BF16)
    state = st[:, 0].reshape(N, DI)
    dcm[0] = dot_nt(doff_s[...], state) + dot(d_scores, bmat)
    dbm[0] = dot_tn(d_scores, cmat)


def back_kernel(
    later, st, act, cum, step, raw, u, dcm, dbm, dy, dsilu, reach, heads,
    dpre, edge, draw, hsum, dw_s, far_s, size_s, high_s, low_s, wts_s, sum_s
):
    spread = heads_to_lanes()
    size, cumul = step[0], cum[0]
    last = cumul[PIECE - 1 :]
    d_local = later[:, 0].reshape(N, DI)
    bmat = act[0, :, DI : DI + N]
    dw_s[...] = dot(bmat, d_local)
    far_s[...] = expand(jnp.exp(last - cumul), spread)
    size_s[...] = expand(size, spread)
    skip = expand(jnp.broadcast_to(heads[2:3], (8, LANES)), spread)[0:1]
    sum_s[...] = jnp.zeros_like(sum_s)
    rows = 16

    def chunk(i, carry):
        at = pl.ds(pl.multiple_of(i * rows, rows), rows)
        value = act[0, at, :DI].astype(F32)
        far, long = far_s[at, :], size_s[at, :]
        through = far * dw_s[at, :]
        d_xdt = u[0, at, :] + through
        d_value = long * d_xdt + skip * dy[0, at, :].astype(F32)
        dpre[0, at, :DI] = d_value * dsilu[0, at, :DI]
        high, low = split(value * d_xdt)
        high_s[at, :] = high
        low_s[at, :] = low
        xdt = long * value
        wts_s[at, :] = (far * xdt).astype(BF16)
        sum_s[0:8] += (xdt * through).reshape(rows // 8, 8, DI).sum(axis=0)
        return carry

    lax.fori_loop(0, PIECE // rows, chunk, 0)
    for j in range(NEAR):
        prod = later[j, 0].astype(F32) * st[j, 0].astype(F32)
        sum_s[8:16] += prod.reshape(NB // 8, 8, DI).sum(axis=0)
    d_bmat = dbm[0] + dot_nt(wts_s[...], d_local)
    dpre[0, :, DI : DI + N] = d_bmat * dsilu[0, :, DI : DI + N]
    dpre[0, :, DI + N :] = dcm[0] * dsilu[0, :, DI + N :]
    edge[0] = dpre[0, 0:8, :]
    q = collect(high_s[...], low_s[...], spread)
    high, low = split(sum_s[...])
    sums = collect(high, low, spread)
    d_last = jnp.sum(sums[0:8], axis=0, keepdims=True)
    d_last = d_last + jnp.exp(last) * jnp.sum(sums[8:16], axis=0, keepdims=True)
    d_cum = reach[0] - size * q
    row = lax.broadcasted_iota(jnp.int32, (PIECE, LANES), 0)
    d_cum = d_cum + jnp.where(row == PIECE - 1, d_last, 0.0)
    d_rate = running(triangle(PIECE, False), d_cum)
    decay = jnp.exp(heads[1:2])
    d_size = q - d_rate * decay
    d_raw = d_size * jax.nn.sigmoid(raw[0] + heads[0:1])
    draw[0] = d_raw
    for_bias = jnp.sum(d_raw, axis=0, keepdims=True)
    for_log = -jnp.sum(d_rate * size, axis=0, keepdims=True) * decay
    pick = lax.broadcasted_iota(jnp.int32, (8, LANES), 0)
    hsum[0] = jnp.where(pick == 0, for_bias, jnp.where(pick == 1, for_log, 0.0))


def input_kernel(core_ref, dpre, edge, draw, hid, par, dproj, k0, k1, k2, s0, s1, s2, ext, total):
    core = core_ref[0]
    count = dpre.shape[0]
    for r in range(count):
        ext[:PIECE] = dpre[r]
        ext[PIECE:] = edge[r]
        for t in range(CONV // LANES):
            cols = slice(t * LANES, (t + 1) * LANES)
            sum_k = par[KW - 1 : KW, cols] * ext[0:PIECE, cols]
            for k in range(KW - 1):
                sum_k = sum_k + par[k : k + 1, cols] * ext[pl.ds(KW - 1 - k, PIECE), cols]
            dproj[r, :, cols] = sum_k.astype(BF16)
        dproj[r, :, CONV:] = draw[r].astype(BF16)
    hidden = hid[...].reshape(count * PIECE, D)
    for g, (keep, send) in enumerate(((k0, s0), (k1, s1), (k2, s2))):
        total[...] = dot_tn(hidden, dproj[:, :, g * GC : (g + 1) * GC].reshape(count * PIECE, GC))
        blocks, rows, _ = keep.shape
        for y in range(blocks):
            mine = pl.multiple_of((2 * y + core) * rows, 16)
            other = pl.multiple_of((2 * y + 1 - core) * rows, 16)
            keep[y] = total[pl.ds(mine, rows)]
            send[y] = total[pl.ds(other, rows)].astype(BF16)


def taps_kernel(dpre, conv, sums, hsum, small, ext):
    @pl.when(pl.program_id(0) == 0)
    def _():
        small[...] = jnp.zeros_like(small)

    for t in range(CONV // LANES):
        cols = slice(t * LANES, (t + 1) * LANES)
        slope = dpre[0, :, cols]
        ext[...] = conv[0, :, cols].astype(F32)
        for k in range(KW):
            prod = slope * ext[pl.ds(HALO - KW + 1 + k, PIECE), :]
            small[k : k + 1, cols] += jnp.sum(prod, axis=0, keepdims=True)
        small[4:5, cols] += jnp.sum(slope, axis=0, keepdims=True)
    small[6:7, :DI] += jnp.sum(sums[0, 0:8], axis=0, keepdims=True)
    small[7:8, 0:LANES] += hsum[0, 0:1]
    small[7:8, LANES : 2 * LANES] += hsum[0, 1:2]
    small[7:8, 2 * LANES : 3 * LANES] += jnp.sum(sums[0, 8:16, :LANES], axis=0, keepdims=True)


def slope_kernel(dgate, wg0, wg1, dh):
    dh[0] = dot_nt(dgate[0, :, :D], wg0[...]) + dot_nt(dgate[0, :, D:], wg1[...])


def token_kernel(tok, cot, dh, dproj, weight, par, _, grad, dh_s):
    dh_s[...] = dh[0] + dot_nt(dproj[0], weight[...])
    gain = par[5:6, :D]
    rows = 32

    def chunk(i, carry):
        at = pl.ds(pl.multiple_of(i * rows, rows), rows)
        x = tok[0, at, :].astype(F32)
        scale = lax.rsqrt(jnp.mean(x * x, axis=-1, keepdims=True) + EPS)
        unit = x * scale
        d_unit = dh_s[at, :] * gain
        along = jnp.mean(d_unit * unit, axis=-1, keepdims=True)
        grad[0, at, :] = (cot[0, at, :].astype(F32) + scale * (d_unit - unit * along)).astype(BF16)
        return carry

    lax.fori_loop(0, PIECE // rows, chunk, 0)


def local(size, tokens, cotangent, norm_in, w_in, conv_w, conv_b, dt_bias, a_log, skip, norm_out, w_out):
    devices, along = size
    bits = int(math.log2(devices))
    core_bit = int(math.log2(along))
    me = lax.axis_index(AX)
    core = ((me >> core_bit) & 1).astype(jnp.int32)
    core_arg = core.reshape(1)
    high_bits = list(range(bits - 1, core_bit, -1))
    far_bits = list(range(core_bit - 1, -1, -1))
    dims = [far_bits[-1:], far_bits[:-1], high_bits] if core_bit == 3 else [far_bits[-3:], far_bits[:-3], high_bits]
    orders = [
        dims[1] + dims[2] + dims[0],
        dims[0] + dims[1] + dims[2],
        dims[2] + dims[0] + dims[1],
    ]

    def swap(x, bit):
        return lax.ppermute(x, AX, [(i, i ^ (1 << bit)) for i in range(devices)])

    def bit_of(bit):
        return (me >> bit) & 1

    def gather(x, order):
        have = []
        for bit in order:
            other = swap(x, bit)
            have = sorted(have + [bit], reverse=True)
            mine = bit_of(bit) == 0
            low, high = jnp.where(mine, x, other), jnp.where(mine, other, x)
            x = jnp.stack([low, high], axis=have.index(bit))
        return x

    micro, batch, count = tokens.shape[:3]
    tok = tokens.reshape(micro * batch, count, D)
    cot = cotangent.reshape(micro * batch, count, D)
    R = micro * batch
    heads = jnp.zeros((8, LANES), F32)
    for i, a in enumerate((dt_bias, a_log, skip)):
        heads = heads.at[i, :H].set(a)

    own_conv, own_in, own_out = conv_b.shape[0], norm_in.shape[0], norm_out.shape[0]
    owned_by = ((own_conv, tuple(range(KW + 1))), (own_in, (KW + 1,)), (own_out, (KW + 2,)))

    halo = lax.ppermute(tok[:, count - HALO :], "near", [(i, i + 1) for i in range(NEAR - 1)])
    rows_in = w_in.shape[0]
    kinds = jnp.concatenate(
        [
            conv_w.T,
            conv_b[None],
            jnp.pad(norm_in, (0, own_conv - own_in))[None],
            jnp.pad(norm_out, (0, own_conv - own_out))[None],
        ],
        axis=0,
    )
    turns = -(-kinds.shape[0] // rows_in)
    kinds = jnp.pad(kinds, ((0, turns * rows_in - kinds.shape[0]), (0, 0)))
    kinds = jnp.concatenate([kinds[t * rows_in : (t + 1) * rows_in] for t in range(turns)], axis=1)
    spare = PC - (w_in.shape[1] - DI)
    kinds = jnp.pad(kinds, ((0, 0), (0, spare - kinds.shape[1])))
    first = jnp.concatenate([w_in[:, DI:], kinds], axis=1)
    blocks = devices // (2 * along)
    mine, recv = [], []
    for g in range(GROUPS):
        part = gather(first[:, g * GC : (g + 1) * GC], orders[g])
        part = part.reshape(blocks, along * rows_in, GC)
        mine.append(part)
        recv.append(swap(part, core_bit))

    rest = jnp.concatenate([w_in[:, :D], w_in[:, D:DI], w_out], axis=0)
    rest = lax.all_gather(rest, AX, axis=0, tiled=False)
    wg0 = rest[:, :rows_in].reshape(D, D)
    wg1 = rest[:, rows_in : 2 * rows_in].reshape(D, D)
    wo = rest[:, 2 * rows_in :].reshape(DI, D)

    smem = pl.BlockSpec(memory_space=pltpu.SMEM)
    anywhere = pl.BlockSpec(memory_space=pl.ANY)
    half = (blocks, along * rows_in, GC)
    par_spec, head_spec = whole((8, CONV)), whole((8, LANES))
    row_d, row_i, row_c = per_row((PIECE, D)), per_row((PIECE, DI)), per_row((PIECE, CONV))
    row_l = per_row((PIECE, LANES))
    state_spec = pl.BlockSpec((NEAR, 1, NB, DI), lambda r: (0, r, 0, 0))
    hid, conv, raw, act, dsilu, step, cum, pay, weight, par = pl.pallas_call(
        functools.partial(enter_kernel, owned_by),
        grid=(R,),
        in_specs=[smem, row_d, per_row((HALO, D))] + [whole(half)] * 6 + [head_spec],
        out_specs=[
            row_d, per_row((HALO + PIECE, CONV)), row_l, row_c, row_c, row_l, row_l,
            pl.BlockSpec((NEAR, 1, NB, DI + LANES), lambda r: (0, r, 0, 0)),
            whole((D, PC)),
            par_spec,
        ],
        out_shape=[
            struct((R, PIECE, D), BF16), struct((R, HALO + PIECE, CONV), BF16), struct((R, PIECE, LANES), F32),
            struct((R, PIECE, CONV), BF16), struct((R, PIECE, CONV), F32), struct((R, PIECE, LANES), F32),
            struct((R, PIECE, LANES), F32), struct((NEAR, R, NB, DI + LANES), BF16), struct((D, PC), BF16),
            struct((8, CONV), F32),
        ],
        scratch_shapes=[pltpu.VMEM((HALO + PIECE, CONV), F32)],
        compiler_params=params(60),
        cost_estimate=cost(R * 2e9, 2e7),
        name="enter",
    )(core_arg, tok, halo, *mine, *recv, heads)

    def exchange(x):
        return lax.all_to_all(x, "near", split_axis=0, concat_axis=0, tiled=True)

    def carry_on(pieces, growths, backward, ready):
        shape = pieces.shape

        def kernel(p, g, _, o):
            pass_kernel(backward, p, g, o)

        return pl.pallas_call(
            kernel,
            grid=(1,),
            in_specs=[whole(shape), pl.BlockSpec((NEAR, R, NB, LANES), lambda r: (0, 0, 0, DI // LANES)), anywhere],
            out_specs=whole((NEAR, R, NB, DI)),
            out_shape=struct((NEAR, R, NB, DI), BF16),
            compiler_params=params(60),
            cost_estimate=cost(1e7, 2e6),
            name="pass",
        )(pieces, growths, ready)

    pieces = exchange(pay)
    intra = pl.pallas_call(
        inside_kernel,
        grid=(R,),
        in_specs=[row_c, row_l, row_l],
        out_specs=row_i,
        out_shape=struct((R, PIECE, DI), F32),
        scratch_shapes=[pltpu.VMEM((PIECE, DI), BF16)],
        compiler_params=params(60),
        cost_estimate=cost(R * 4e9, 5e6),
        name="inside",
    )(act, step, cum)
    gate, dnorm = pl.pallas_call(
        gate_kernel,
        grid=(R,),
        in_specs=[row_d, row_d, whole((D, D)), whole((D, D)), whole((DI, D))],
        out_specs=[row_i, row_i],
        out_shape=[struct((R, PIECE, DI), BF16), struct((R, PIECE, DI), F32)],
        compiler_params=params(60),
        cost_estimate=cost(R * 2e9, 1e7),
        name="gates",
    )(hid, cot, wg0, wg1, wo)
    st = exchange(carry_on(pieces, pieces, False, intra))

    wide = pltpu.VMEM((PIECE, DI), F32)
    slim = pltpu.VMEM((PIECE, DI), BF16)
    normed, dgate, dy, reach, back, sums = pl.pallas_call(
        middle_kernel,
        grid=(R,),
        in_specs=[state_spec, row_c, row_i, row_l, row_i, row_i, par_spec, head_spec],
        out_specs=[row_i, row_i, row_i, row_l, state_spec, per_row((16, DI))],
        out_shape=[
            struct((R, PIECE, DI), BF16), struct((R, PIECE, DI), BF16), struct((R, PIECE, DI), BF16),
            struct((R, PIECE, LANES), F32), struct((NEAR, R, NB, DI), BF16), struct((R, 16, DI), F32),
        ],
        scratch_shapes=[wide, wide, slim, slim, slim, pltpu.VMEM((16, DI), F32)],
        compiler_params=params(60),
        cost_estimate=cost(R * 2e9, 1.5e7),
        name="middle",
    )(st, act, intra, cum, gate, dnorm, par, heads)

    pieces_b = exchange(back)
    rows_out = w_out.shape[0]
    fused = rows_in % 8 == 0
    if fused:
        shapes = [(devices, rows_out + 2 * rows_in, D)]
        scratch = [pltpu.VMEM((DI + 2 * D, D), F32)]
    else:
        shapes = [(DI, D), (D, D), (D, D)]
        scratch = []
    block_out, *made = pl.pallas_call(
        functools.partial(outer_kernel, fused),
        grid=(1,),
        in_specs=[
            whole((R, PIECE, D)), whole((R, PIECE, D)), whole((R, PIECE, D)),
            whole((R, PIECE, DI)), whole((R, PIECE, DI)), whole((DI, D)),
        ],
        out_specs=[whole((R, PIECE, D))] + [whole(shape) for shape in shapes],
        out_shape=[struct((R, PIECE, D), BF16)] + [struct(shape, BF16) for shape in shapes],
        scratch_shapes=scratch,
        compiler_params=params(60),
        cost_estimate=cost(6e9, 2e7),
        name="outer",
    )(tok, cot, hid, normed, dgate, wo)
    if not fused:
        made = [jnp.concatenate([part.reshape(devices, part.shape[0] // devices, D) for part in made], axis=1)]
    own = lax.psum_scatter(made[0], AX, scatter_dimension=0, tiled=False).astype(F32)
    g_wout = own[:rows_out]
    g_gate = jnp.concatenate([own[rows_out : rows_out + rows_in], own[rows_out + rows_in :]], axis=1)

    u, dcm, dbm = pl.pallas_call(
        pair_kernel,
        grid=(R,),
        in_specs=[row_c, row_l, row_l, row_i, state_spec],
        out_specs=[row_i, row_l, row_l],
        out_shape=[struct((R, PIECE, DI), F32), struct((R, PIECE, N), F32), struct((R, PIECE, N), F32)],
        scratch_shapes=[slim, slim, pltpu.VMEM((PIECE, PIECE), F32)],
        compiler_params=params(60),
        cost_estimate=cost(R * 8e9, 1e7),
        name="pair",
    )(act, step, cum, dy, st)
    dh = pl.pallas_call(
        slope_kernel,
        grid=(R,),
        in_specs=[row_i, whole((D, D)), whole((D, D))],
        out_specs=row_d,
        out_shape=struct((R, PIECE, D), F32),
        compiler_params=params(60),
        cost_estimate=cost(R * 6e8, 6e6),
        name="slope",
    )(dgate, wg0, wg1)
    later = exchange(carry_on(pieces_b, pieces, True, made[0]))

    dpre, edge, draw, hsum = pl.pallas_call(
        back_kernel,
        grid=(R,),
        in_specs=[
            state_spec, state_spec, row_c, row_l, row_l, row_l, row_i, row_l, row_l, row_i, row_c, row_l, head_spec,
        ],
        out_specs=[row_c, per_row((8, CONV)), row_l, per_row((8, LANES))],
        out_shape=[
            struct((R, PIECE, CONV), F32), struct((R, 8, CONV), F32),
            struct((R, PIECE, LANES), F32), struct((R, 8, LANES), F32),
        ],
        scratch_shapes=[wide, wide, wide, slim, slim, slim, pltpu.VMEM((16, DI), F32)],
        compiler_params=params(60),
        cost_estimate=cost(R * 2e9, 1.5e7),
        name="back",
    )(later, st, act, cum, step, raw, u, dcm, dbm, dy, dsilu, reach, heads)
    edge = lax.ppermute(edge, "near", [(i + 1, i) for i in range(NEAR - 1)])

    dproj, k0, k1, k2, s0, s1, s2 = pl.pallas_call(
        input_kernel,
        grid=(1,),
        in_specs=[
            smem, whole((R, PIECE, CONV)), whole((R, 8, CONV)), whole((R, PIECE, LANES)), whole((R, PIECE, D)), par_spec,
        ],
        out_specs=[whole((R, PIECE, PC))] + [whole(half)] * 6,
        out_shape=[struct((R, PIECE, PC), BF16)] + [struct(half, F32)] * 3 + [struct(half, BF16)] * 3,
        scratch_shapes=[pltpu.VMEM((PIECE + 8, CONV), F32), pltpu.VMEM((D, GC), F32)],
        compiler_params=params(60),
        cost_estimate=cost(2e9, 1e7),
        name="input",
    )(core_arg, dpre, edge, draw, hid, par)

    small = pl.pallas_call(
        taps_kernel,
        grid=(R,),
        in_specs=[row_c, per_row((HALO + PIECE, CONV)), per_row((16, DI)), per_row((8, LANES))],
        out_specs=whole((8, CONV)),
        out_shape=struct((8, CONV), F32),
        scratch_shapes=[pltpu.VMEM((HALO + PIECE, LANES), F32)],
        compiler_params=params(60),
        cost_estimate=cost(2e7, 6e6),
        name="taps",
    )(dpre, conv, sums, hsum)

    states = []
    for keep_g, send_g in ((k0, s0), (k1, s1), (k2, s2)):
        part = keep_g + swap(send_g, core_bit).astype(F32)
        states.append(part.reshape((2,) * (bits - 1) + (rows_in, GC)))
    small = small + swap(small, core_bit)
    grad_tokens = pl.pallas_call(
        token_kernel,
        grid=(R,),
        in_specs=[row_d, row_d, row_d, per_row((PIECE, PC)), whole((D, PC)), par_spec, anywhere],
        out_specs=row_d,
        out_shape=struct((R, PIECE, D), BF16),
        scratch_shapes=[pltpu.VMEM((PIECE, D), F32)],
        compiler_params=params(60),
        cost_estimate=cost(R * 2e9, 1.5e7),
        name="token",
    )(tok, cot, dh, dproj, weight, par, states[0])
    order_s = orders[0][::-1]
    have = [sorted(order, reverse=True) for order in orders]
    for turn in range(bits - 1):
        moved = []
        for g in range(GROUPS):
            bit = orders[g][::-1][turn]
            axis = have[g].index(bit)
            have[g].remove(bit)
            moved.append((
                lax.dynamic_index_in_dim(states[g], bit_of(bit), axis, False),
                swap(lax.dynamic_index_in_dim(states[g], 1 - bit_of(bit), axis, False).astype(BF16), bit),
            ))
        other = swap(small, order_s[turn])
        states = [mine_g + got.astype(F32) for mine_g, got in moved]
        small = small + other
    g_win = jnp.concatenate([g_gate] + states, axis=1)[:, : w_in.shape[1]]
    g_gin = jnp.sum(g_win * w_in.astype(F32), axis=1) / norm_in.astype(F32)
    taps = lax.dynamic_slice(small, (0, me * own_conv), (5, own_conv))
    g_gout = lax.dynamic_slice(small, (6, me * own_out), (1, own_out))[0]
    return (
        block_out.reshape(tokens.shape),
        grad_tokens.reshape(tokens.shape),
        g_gin,
        g_win,
        taps[:KW].T,
        taps[KW],
        small[7, :H],
        small[7, LANES : LANES + H],
        small[7, 2 * LANES : 2 * LANES + H],
        g_gout,
        g_wout,
    )


def solution(mesh):
    dp, seq = mesh.shape["dp"], mesh.shape["seq"]
    inner = Mesh(mesh.devices.reshape(dp, seq // NEAR, NEAR), AX)
    split_seq = ("far", "near")
    act = P(None, "dp", split_seq, None)
    vec, mat = P(AX), P(AX, None)

    def run(*args):
        return local((dp * seq, seq), *args)

    return jax.shard_map(
        run,
        mesh=inner,
        in_specs=(act, act, vec, mat, mat, vec, P(), P(), P(), vec, mat),
        out_specs=(act, act, vec, mat, mat, vec, P(), P(), P(), vec, mat),
        check_vma=False,
    )
```

```python
import functools
import itertools
import math

import jax
import jax.numpy as jnp
from jax import lax
from jax.experimental import pallas as pl
from jax.experimental.pallas import tpu as pltpu
from jax.sharding import Mesh
from jax.sharding import PartitionSpec as P

H = 24
HP = 64
N = 128
KW = 4
SEQ_LEN = 2048
PIECE = 256
D = 768
DI = H * HP
CONV = DI + 2 * N
PC = 1920
WIDTHS = (640, 640, 640)
REST = DI + 2 * D
RWIDTH = REST // len(WIDTHS)
GROUPS = len(WIDTHS)
SPANS = tuple(slice(sum(WIDTHS[:g]), sum(WIDTHS[: g + 1])) for g in range(GROUPS))
NEAR = SEQ_LEN // PIECE
NB = N // NEAR
HALO = 16
LANES = 128
HALO_TURN = 2
EPS = 1e-05
F32 = jnp.float32
BF16 = jnp.bfloat16
AX = ("dp", "far", "near")
MIB = 1 << 20


def dot(a, b):
    return lax.dot_general(a, b, (((1,), (0,)), ((), ())), preferred_element_type=F32)


def dot_nt(a, b):
    return lax.dot_general(a, b, (((1,), (1,)), ((), ())), preferred_element_type=F32)


def dot_tn(a, b):
    return lax.dot_general(a, b, (((0,), (0,)), ((), ())), preferred_element_type=F32)


def split(x):
    high = x.astype(BF16)
    return high, (x - high.astype(F32)).astype(BF16)


def heads_to_lanes():
    head = lax.broadcasted_iota(jnp.int32, (LANES, DI), 0)
    lane = lax.broadcasted_iota(jnp.int32, (LANES, DI), 1)
    return jnp.where((lane >> 6) == head, 1.0, 0.0).astype(BF16)


def expand(x, spread):
    high, low = split(x)
    return dot(high, spread) + dot(low, spread)


def collect(high, low, spread):
    return dot_nt(high, spread) + dot_nt(low, spread)


def triangle(count, lower):
    row = lax.broadcasted_iota(jnp.int32, (count, count), 0)
    col = lax.broadcasted_iota(jnp.int32, (count, count), 1)
    return (row >= col) if lower else (row <= col)


def running(mask, x):
    ones = jnp.where(mask, 1.0, 0.0).astype(BF16)
    high, rest = split(x)
    left = x - high.astype(F32)
    mid, low = split(left)
    return dot(ones, high) + dot(ones, mid) + dot(ones, low)


def softplus(z):
    e = jnp.exp(-jnp.abs(z))
    near = e * (1.0 + e * (-0.5 + e * (1.0 / 3.0 + e * (-0.25 + e * 0.2))))
    return jnp.maximum(z, 0.0) + jnp.where(e < 0.02, near, jnp.log(1.0 + e))


def params(limit):
    return pltpu.CompilerParams(vmem_limit_bytes=limit * MIB)


def cost(flops, nbytes, trans=0):
    return pl.CostEstimate(flops=int(flops), bytes_accessed=int(nbytes), transcendentals=int(trans))


def whole(shape):
    return pl.BlockSpec(shape, lambda *_: (0,) * len(shape))


def per_row(shape):
    return pl.BlockSpec((1,) + shape, lambda r: (r,) + (0,) * len(shape))


def struct(shape, kind):
    return jax.ShapeDtypeStruct(shape, kind)


def assemble(core, mine, recv, weight_s):
    count, rows, _ = mine[0].shape
    for g, cols in enumerate(SPANS):
        for y in range(count):
            first = pl.multiple_of((2 * y + core) * rows, 16)
            other = pl.multiple_of((2 * y + 1 - core) * rows, 16)
            weight_s[pl.ds(first, rows), cols] = mine[g][y]
            weight_s[pl.ds(other, rows), cols] = recv[g][y]


def lay_out(weight, par, owned):
    held = weight[:, CONV:]
    for own, kinds in owned:
        rows_in = own * D // CONV if len(kinds) > 1 else (own if kinds[0] == KW + 1 else own // 2)
        devices = D // rows_in
        width = own * devices
        lane = lax.broadcasted_iota(jnp.int32, (LANES, width), 1)
        row = lax.broadcasted_iota(jnp.int32, (LANES, width), 0)
        source = lax.broadcasted_iota(jnp.int32, (devices, D), 1)
        device = lax.broadcasted_iota(jnp.int32, (devices, D), 0)
        place = lax.broadcasted_iota(jnp.int32, (devices, width), 1)
        holder = lax.broadcasted_iota(jnp.int32, (devices, width), 0)
        mine = (place >= holder * own) & (place < holder * own + own)
        for kind in kinds:
            at, block = kind % rows_in, kind // rows_in
            pick = jnp.where(source == device * rows_in + at, 1.0, 0.0).astype(BF16)
            start = H + block * (rows_in * CONV // D)
            spread = jnp.where(row == start + lane % own, 1.0, 0.0).astype(BF16)
            values = dot(dot(pick, held).astype(BF16), spread)
            par[kind : kind + 1, :width] = jnp.sum(jnp.where(mine, values, 0.0), axis=0, keepdims=True)


def enter_kernel(
    owned, core_ref, tok, halo, heads, *refs
):
    mine, recv, rest = refs[:GROUPS], refs[GROUPS : 2 * GROUPS], refs[2 * GROUPS :]
    hid, conv, raw, act, dsilu, step, cum, pay, weight, par, ext = rest

    @pl.when(pl.program_id(0) == 0)
    def _():
        assemble(core_ref[0], mine, recv, weight)
        par[...] = jnp.zeros_like(par)
        lay_out(weight, par, owned)

    gain = par[5:6, :D]
    rows = jnp.concatenate([halo[0], tok[0]], axis=0).astype(F32)
    scale = lax.rsqrt(jnp.mean(rows * rows, axis=-1, keepdims=True) + EPS)
    hidden = (rows * scale * gain).astype(BF16)
    hid[0] = hidden[HALO:]
    for t in range(CONV // 256):
        cols = slice(t * 256, (t + 1) * 256)
        part = dot(hidden, weight[:, cols]).astype(BF16)
        conv[0, :, cols] = part
        ext[:, cols] = part.astype(F32)
    for t in range(CONV // LANES):
        cols = slice(t * LANES, (t + 1) * LANES)
        total = par[4:5, cols]
        for k in range(KW):
            total = total + par[k : k + 1, cols] * ext[pl.ds(HALO - KW + 1 + k, PIECE), cols]
        gate = jax.nn.sigmoid(total)
        act[0, :, cols] = (total * gate).astype(BF16)
        dsilu[0, :, cols] = gate * (1.0 + total * (1.0 - gate))
    raw_step = dot(hidden[HALO:], weight[:, CONV:]).astype(BF16).astype(F32)
    raw_step = jnp.where(lax.broadcasted_iota(jnp.int32, (PIECE, LANES), 1) < H, raw_step, 0.0)
    raw[0] = raw_step
    size = softplus(raw_step + heads[0:1])
    cumul = running(triangle(PIECE, True), size * -jnp.exp(heads[1:2]))
    step[0] = size
    cum[0] = cumul
    spread = heads_to_lanes()
    last = cumul[PIECE - 1 :]
    reach = jnp.exp(last - cumul) * size
    bmat = act[0, :, DI : DI + N]
    for t in range(DI // 256):
        cols = slice(t * 256, (t + 1) * 256)
        weights = (expand(reach, spread[:, cols]) * act[0, :, cols].astype(F32)).astype(BF16)
        state = dot_tn(bmat, weights).astype(BF16)
        pay[:, 0, :, cols] = state.reshape(NEAR, NB, 256)
    growth = jnp.exp(last)
    high, low = split(growth)
    row = lax.broadcasted_iota(jnp.int32, (NB, LANES), 0)
    growths = jnp.where(row == 0, high.astype(F32), jnp.where(row == 1, low.astype(F32), 0.0))
    for j in range(NEAR):
        pay[j, 0, :, DI:] = growths.astype(BF16)


def pass_kernel(backward, pieces, growths, out):
    spread = heads_to_lanes()
    count = out.shape[1]
    for r in range(count):
        high = jnp.concatenate([growths[j, r, 0:1, :] for j in range(NEAR)], axis=0)
        low = jnp.concatenate([growths[j, r, 1:2, :] for j in range(NEAR)], axis=0)
        grow = dot(high, spread) + dot(low, spread)
        state = jnp.zeros((NB, DI), F32)
        order = range(NEAR - 1, -1, -1) if backward else range(NEAR)
        for j in order:
            out[j, r] = state.astype(BF16)
            state = grow[j : j + 1] * state + pieces[j, r, :, :DI].astype(F32)


def inside_kernel(act, step, cum, intra, xdt_s):
    spread = heads_to_lanes()
    size, cumul = step[0], cum[0]
    for t in range(DI // 256):
        cols = slice(t * 256, (t + 1) * 256)
        xdt_s[:, cols] = (expand(size, spread[:, cols]) * act[0, :, cols].astype(F32)).astype(BF16)
    bmat, cmat = act[0, :, DI : DI + N], act[0, :, DI + N :]
    scores = dot_nt(cmat, bmat)
    lower = triangle(PIECE, True)
    turned = cumul.T
    left = lax.broadcasted_iota(jnp.int32, (PIECE, LANES), 1) < HP
    for pair in range(H // 2):
        cols = slice(pair * LANES, (pair + 1) * LANES)
        xdt = xdt_s[:, cols]
        both = []
        for h in (2 * pair, 2 * pair + 1):
            differ = cumul[:, h : h + 1] - turned[h : h + 1, :]
            mix = (scores * jnp.exp(jnp.where(lower, differ, -1e30))).astype(BF16)
            both.append(dot(mix, xdt))
        intra[0, :, cols] = jnp.where(left, both[0], both[1])


def gate_kernel(hid, cot, wg0, wg1, wo, gate, dnorm):
    gate[0, :, :D] = dot(hid[0], wg0[...]).astype(BF16)
    gate[0, :, D:] = dot(hid[0], wg1[...]).astype(BF16)
    dnorm[0] = dot_nt(cot[0], wo[...])


def middle_kernel(
    st, act, intra, cum, gate, dnorm, par, heads,
    normed, dgate, dy, reach, pay, sums, off_s, grow_s, high_s, low_s, doff_s, sum_s
):
    spread = heads_to_lanes()
    state = st[:, 0].reshape(N, DI)
    cmat = act[0, :, DI + N :]
    off_s[...] = dot(cmat, state)
    grow_s[...] = expand(jnp.exp(cum[0]), spread)
    skip = expand(jnp.broadcast_to(heads[2:3], (8, LANES)), spread)[0:1]
    gain = par[6:7, :DI]
    sum_s[...] = jnp.zeros_like(sum_s)
    size = 16

    def chunk(i, carry):
        at = pl.ds(pl.multiple_of(i * size, size), size)
        value = act[0, at, :DI].astype(F32)
        grow = grow_s[at, :]
        base = intra[0, at, :] + grow * off_s[at, :]
        ssd = base + skip * value
        z = gate[0, at, :].astype(F32)
        sig = jax.nn.sigmoid(z)
        silu = z * sig
        gated = ssd * silu
        scale = lax.rsqrt(jnp.mean(gated * gated, axis=-1, keepdims=True) + EPS)
        unit = gated * scale
        normed[0, at, :] = (unit * gain).astype(BF16)
        d_normed = dnorm[0, at, :]
        sum_s[0:8] += (d_normed * unit).reshape(size // 8, 8, DI).sum(axis=0)
        d_unit = d_normed * gain
        along = jnp.mean(d_unit * unit, axis=-1, keepdims=True)
        d_gated = scale * (d_unit - unit * along)
        dgate[0, at, :] = (d_gated * ssd * (sig * (1.0 + z * (1.0 - sig)))).astype(BF16)
        d_ssd = (d_gated * silu).astype(BF16)
        dy[0, at, :] = d_ssd
        d_ssd = d_ssd.astype(F32)
        doff_s[at, :] = (grow * d_ssd).astype(BF16)
        sum_s[8:16] += (d_ssd * value).reshape(size // 8, 8, DI).sum(axis=0)
        high, low = split(d_ssd * base)
        high_s[at, :] = high
        low_s[at, :] = low
        return carry

    lax.fori_loop(0, PIECE // size, chunk, 0)
    d_state = dot_tn(cmat, doff_s[...]).astype(BF16)
    pay[:, 0] = d_state.reshape(NEAR, NB, DI)
    reach[0] = collect(high_s[...], low_s[...], spread)
    high, low = split(sum_s[8:16])
    sums[0, 0:8] = sum_s[0:8]
    sums[0, 8:16, :LANES] = collect(high, low, spread)
    sums[0, 8:16, LANES:] = jnp.zeros((8, DI - LANES), F32)


def outer_kernel(rows_in, core_ref, cot, hid, normed, dgate, keep, send, total, sums):
    core = core_ref[0]
    count = cot.shape[0]
    tangent = cot[...].reshape(count * PIECE, D)
    hidden = hid[...].reshape(count * PIECE, D)
    total[...] = dot_tn(normed[...].reshape(count * PIECE, DI), tangent)
    for half in range(2):
        cols = slice(half * D, (half + 1) * D)
        sums[:, cols] = dot_tn(hidden, dgate[:, :, cols].reshape(count * PIECE, D))
    for d in range(D // rows_in):
        for half in range(2):
            start = (2 * d + half) * rows_in
            sums[d * rows_in : (d + 1) * rows_in, DI + half * D : DI + (half + 1) * D] = total[start : start + rows_in]
    blocks, rows, _ = keep.shape
    for y in range(blocks):
        mine = pl.multiple_of((2 * y + core) * rows, 16)
        other = pl.multiple_of((2 * y + 1 - core) * rows, 16)
        keep[y] = sums[pl.ds(mine, rows)]
        send[y] = sums[pl.ds(other, rows)].astype(BF16)


def join_kernel(cuts, axes, bit_ref, small, other, _, *refs):
    count = 1 + max(operand for group in cuts for operand, _, _ in group)
    keeps, recvs = refs[:count], refs[count : 2 * count]
    outs, sends = refs[2 * count : 2 * count + GROUPS], refs[2 * count + GROUPS : 2 * count + 2 * GROUPS]
    refs[-1][...] = small[...] + other[...]
    for g, group in enumerate(cuts):
        bit, axis = bit_ref[g], axes[g]
        base = 0
        for operand, start, width in group:
            keep, recv = keeps[operand], recvs[operand]
            source, target = slice(start, start + width), slice(base, base + width)
            for place in itertools.product(range(2), repeat=keep.ndim - 3):
                mine = place[:axis] + (bit,) + place[axis:] + (slice(None), source)
                away = place[:axis] + (1 - bit,) + place[axis:] + (slice(None), source)
                here = place + (slice(None), target)
                outs[g][here] = keep[mine] + recv[mine].astype(F32)
                sends[g][here] = (keep[away] + recv[away].astype(F32)).astype(BF16)
            base += width


def last_kernel(small, other, w_in, gain, *refs):
    keeps, recvs = refs[:GROUPS], refs[GROUPS : 2 * GROUPS]
    small_out, g_win, g_wout, g_gin = refs[2 * GROUPS :]
    small_out[...] = small[...] + other[...]
    rows, width = g_win.shape
    for g in range(GROUPS):
        total = keeps[g][...] + recvs[g][...].astype(F32)
        start = DI + SPANS[g].start
        stop = min(start + WIDTHS[g], width)
        g_win[:, start:stop] = total[:, : stop - start]
        first = g * RWIDTH
        for lo, hi, ref, row in ((0, DI, g_win, 0), (DI, DI + D, g_wout, 0), (DI + D, REST, g_wout, rows)):
            a, b = max(lo, first), min(hi, first + RWIDTH)
            if a < b:
                at = WIDTHS[g] + a - first
                ref[row : row + rows, a - lo : b - lo] = total[:, at : at + b - a]
    g_gin[...] = jnp.sum(g_win[...] * w_in[...].astype(F32), axis=-1, keepdims=True) / gain[...].astype(F32)


def result_kernel(tok, normed, wo, _, out):
    out[0] = (tok[0].astype(F32) + dot(normed[0], wo[...])).astype(BF16)


def pair_kernel(act, step, cum, dy, st, u, dcm, dbm, xdt_s, doff_s, dsc_s):
    spread = heads_to_lanes()
    size, cumul = step[0], cum[0]
    grown = jnp.exp(cumul)
    for t in range(DI // 256):
        cols = slice(t * 256, (t + 1) * 256)
        xdt_s[:, cols] = (expand(size, spread[:, cols]) * act[0, :, cols].astype(F32)).astype(BF16)
        doff_s[:, cols] = (expand(grown, spread[:, cols]) * dy[0, :, cols].astype(F32)).astype(BF16)
    bmat, cmat = act[0, :, DI : DI + N], act[0, :, DI + N :]
    scores = dot_nt(cmat, bmat)
    lower = triangle(PIECE, True)
    turned = cumul.T
    dsc_s[...] = jnp.zeros_like(dsc_s)
    left = lax.broadcasted_iota(jnp.int32, (PIECE, LANES), 1) < HP
    zero = jnp.zeros((PIECE, LANES), BF16)
    for pair in range(H // 2):
        cols = slice(pair * LANES, (pair + 1) * LANES)
        xdt = xdt_s[:, cols]
        slope = dy[0, :, cols]
        slope_t = slope.astype(F32).T.astype(BF16)
        both = []
        for side in (0, 1):
            h = 2 * pair + side
            differ = cumul[:, h : h + 1] - turned[h : h + 1, :]
            decay = jnp.exp(jnp.where(lower, differ, -1e30))
            mix = (scores * decay).astype(BF16)
            own = jnp.where(left, slope, zero) if side == 0 else jnp.where(left, zero, slope)
            dsc_s[...] += dot_nt(own, xdt) * decay
            both.append(dot(slope_t[side * HP : (side + 1) * HP], mix))
        u[0, :, cols] = jnp.concatenate(both, axis=0).T
    d_scores = dsc_s[...].astype(BF16)
    state = st[:, 0].reshape(N, DI)
    dcm[0] = dot_nt(doff_s[...], state) + dot(d_scores, bmat)
    dbm[0] = dot_tn(d_scores, cmat)


def back_kernel(
    later, st, act, cum, step, raw, u, dcm, dbm, dy, dsilu, reach, heads, _, __, ___,
    dpre, edge, draw, hsum, dw_s, far_s, size_s, high_s, low_s, wts_s, sum_s
):
    spread = heads_to_lanes()
    size, cumul = step[0], cum[0]
    last = cumul[PIECE - 1 :]
    d_local = later[:, 0].reshape(N, DI)
    bmat = act[0, :, DI : DI + N]
    dw_s[...] = dot(bmat, d_local)
    far_s[...] = expand(jnp.exp(last - cumul), spread)
    size_s[...] = expand(size, spread)
    skip = expand(jnp.broadcast_to(heads[2:3], (8, LANES)), spread)[0:1]
    sum_s[...] = jnp.zeros_like(sum_s)
    rows = 16

    def chunk(i, carry):
        at = pl.ds(pl.multiple_of(i * rows, rows), rows)
        value = act[0, at, :DI].astype(F32)
        far, long = far_s[at, :], size_s[at, :]
        through = far * dw_s[at, :]
        d_xdt = u[0, at, :] + through
        d_value = long * d_xdt + skip * dy[0, at, :].astype(F32)
        dpre[0, at, :DI] = d_value * dsilu[0, at, :DI]
        high, low = split(value * d_xdt)
        high_s[at, :] = high
        low_s[at, :] = low
        xdt = long * value
        wts_s[at, :] = (far * xdt).astype(BF16)
        sum_s[0:8] += (xdt * through).reshape(rows // 8, 8, DI).sum(axis=0)
        return carry

    lax.fori_loop(0, PIECE // rows, chunk, 0)
    for j in range(NEAR):
        prod = later[j, 0].astype(F32) * st[j, 0].astype(F32)
        sum_s[8:16] += prod.reshape(NB // 8, 8, DI).sum(axis=0)
    d_bmat = dbm[0] + dot_nt(wts_s[...], d_local)
    dpre[0, :, DI : DI + N] = d_bmat * dsilu[0, :, DI : DI + N]
    dpre[0, :, DI + N :] = dcm[0] * dsilu[0, :, DI + N :]
    edge[0] = dpre[0, 0:8, :]
    q = collect(high_s[...], low_s[...], spread)
    high, low = split(sum_s[...])
    sums = collect(high, low, spread)
    d_last = jnp.sum(sums[0:8], axis=0, keepdims=True)
    d_last = d_last + jnp.exp(last) * jnp.sum(sums[8:16], axis=0, keepdims=True)
    d_cum = reach[0] - size * q
    row = lax.broadcasted_iota(jnp.int32, (PIECE, LANES), 0)
    d_cum = d_cum + jnp.where(row == PIECE - 1, d_last, 0.0)
    d_rate = running(triangle(PIECE, False), d_cum)
    decay = jnp.exp(heads[1:2])
    d_size = q - d_rate * decay
    d_raw = d_size * jax.nn.sigmoid(raw[0] + heads[0:1])
    draw[0] = d_raw
    for_bias = jnp.sum(d_raw, axis=0, keepdims=True)
    for_log = -jnp.sum(d_rate * size, axis=0, keepdims=True) * decay
    pick = lax.broadcasted_iota(jnp.int32, (8, LANES), 0)
    hsum[0] = jnp.where(pick == 0, for_bias, jnp.where(pick == 1, for_log, 0.0))


def input_kernel(core_ref, dpre, edge, draw, hid, par, gone, dproj, small, *refs):
    keeps, sends = refs[:GROUPS], refs[GROUPS : 2 * GROUPS]
    ext, *totals = refs[2 * GROUPS :]
    small[...] = gone[...]
    core = core_ref[0]
    count = dpre.shape[0]
    for r in range(count):
        ext[:PIECE] = dpre[r]
        ext[PIECE:] = edge[r]
        for t in range(CONV // LANES):
            cols = slice(t * LANES, (t + 1) * LANES)
            sum_k = par[KW - 1 : KW, cols] * ext[0:PIECE, cols]
            for k in range(KW - 1):
                sum_k = sum_k + par[k : k + 1, cols] * ext[pl.ds(KW - 1 - k, PIECE), cols]
            dproj[r, :, cols] = sum_k.astype(BF16)
        dproj[r, :, CONV:] = draw[r].astype(BF16)
    hidden = hid[...].reshape(count * PIECE, D)
    for keep, send, total, cols in zip(keeps, sends, totals, SPANS):
        total[...] = dot_tn(hidden, dproj[:, :, cols].reshape(count * PIECE, cols.stop - cols.start))
        blocks, rows, _ = keep.shape
        for y in range(blocks):
            mine = pl.multiple_of((2 * y + core) * rows, 16)
            other = pl.multiple_of((2 * y + 1 - core) * rows, 16)
            keep[y] = total[pl.ds(mine, rows)]
            send[y] = total[pl.ds(other, rows)].astype(BF16)


def taps_kernel(dpre, conv, sums, hsum, small, ext):
    @pl.when(pl.program_id(0) == 0)
    def _():
        small[...] = jnp.zeros_like(small)

    for t in range(CONV // LANES):
        cols = slice(t * LANES, (t + 1) * LANES)
        slope = dpre[0, :, cols]
        ext[...] = conv[0, :, cols].astype(F32)
        for k in range(KW):
            prod = slope * ext[pl.ds(HALO - KW + 1 + k, PIECE), :]
            small[k : k + 1, cols] += jnp.sum(prod, axis=0, keepdims=True)
        small[4:5, cols] += jnp.sum(slope, axis=0, keepdims=True)
    small[6:7, :DI] += jnp.sum(sums[0, 0:8], axis=0, keepdims=True)
    small[7:8, 0:LANES] += hsum[0, 0:1]
    small[7:8, LANES : 2 * LANES] += hsum[0, 1:2]
    small[7:8, 2 * LANES : 3 * LANES] += jnp.sum(sums[0, 8:16, :LANES], axis=0, keepdims=True)


def slope_kernel(dgate, wg0, wg1, dh):
    dh[0] = dot_nt(dgate[0, :, :D], wg0[...]) + dot_nt(dgate[0, :, D:], wg1[...])


def token_kernel(tok, cot, dh, dproj, weight, par, _, grad, dh_s):
    dh_s[...] = dh[0] + dot_nt(dproj[0], weight[...])
    gain = par[5:6, :D]
    rows = 32

    def chunk(i, carry):
        at = pl.ds(pl.multiple_of(i * rows, rows), rows)
        x = tok[0, at, :].astype(F32)
        scale = lax.rsqrt(jnp.mean(x * x, axis=-1, keepdims=True) + EPS)
        unit = x * scale
        d_unit = dh_s[at, :] * gain
        along = jnp.mean(d_unit * unit, axis=-1, keepdims=True)
        grad[0, at, :] = (cot[0, at, :].astype(F32) + scale * (d_unit - unit * along)).astype(BF16)
        return carry

    lax.fori_loop(0, PIECE // rows, chunk, 0)


def local(size, tokens, cotangent, norm_in, w_in, conv_w, conv_b, dt_bias, a_log, skip, norm_out, w_out):
    devices, along = size
    bits = int(math.log2(devices))
    core_bit = int(math.log2(along))
    me = lax.axis_index(AX)
    core = ((me >> core_bit) & 1).astype(jnp.int32)
    core_arg = core.reshape(1)
    high_bits = list(range(bits - 1, core_bit, -1))
    far_bits = list(range(core_bit - 1, -1, -1))
    dims = [far_bits[-1:], far_bits[:-1], high_bits] if core_bit == 3 else [far_bits[-3:], far_bits[:-3], high_bits]
    orders = [dims[1] + dims[2] + dims[0], dims[0] + dims[1] + dims[2], dims[2] + dims[0] + dims[1]]
    if [len(dim) for dim in dims] == [1, 2, 1]:
        x, (top, low), y = dims[0][0], dims[1], dims[2][0]
        orders = [[top, low, y, x], [top, x, low, y], [top, y, x, low]]

    def swap(x, bit):
        return lax.ppermute(x, AX, [(i, i ^ (1 << bit)) for i in range(devices)])

    def bit_of(bit):
        return (me >> bit) & 1

    def after(x, other):
        rows, cols = min(x.shape[-2], other.shape[-2], 8), min(x.shape[-1], other.shape[-1])
        part = other[(0,) * (other.ndim - 2)][:rows, :cols].astype(x.dtype)
        return x + 0 * jnp.pad(part, ((0, x.shape[-2] - rows), (0, x.shape[-1] - cols)))

    def gather(x, order):
        have = []
        for bit in order:
            if order is orders[0]:
                if len(have) == HALO_TURN:
                    x = after(x, halo)
            other = swap(x, bit)
            have = sorted(have + [bit], reverse=True)
            mine = bit_of(bit) == 0
            low, high = jnp.where(mine, x, other), jnp.where(mine, other, x)
            x = jnp.stack([low, high], axis=have.index(bit))
        return x

    micro, batch, count = tokens.shape[:3]
    tok = tokens.reshape(micro * batch, count, D)
    cot = cotangent.reshape(micro * batch, count, D)
    R = micro * batch
    heads = jnp.zeros((8, LANES), F32)
    for i, a in enumerate((dt_bias, a_log, skip)):
        heads = heads.at[i, :H].set(a)

    own_conv, own_in, own_out = conv_b.shape[0], norm_in.shape[0], norm_out.shape[0]
    owned_by = ((own_conv, tuple(range(KW + 1))), (own_in, (KW + 1,)), (own_out, (KW + 2,)))

    halo = lax.ppermute(tok[:, count - HALO :], "near", [(i, i + 1) for i in range(NEAR - 1)])
    rows_in = w_in.shape[0]
    kinds = jnp.concatenate(
        [
            conv_w.T,
            conv_b[None],
            jnp.pad(norm_in, (0, own_conv - own_in))[None],
            jnp.pad(norm_out, (0, own_conv - own_out))[None],
        ],
        axis=0,
    )
    turns = -(-kinds.shape[0] // rows_in)
    kinds = jnp.pad(kinds, ((0, turns * rows_in - kinds.shape[0]), (0, 0)))
    kinds = jnp.concatenate([kinds[t * rows_in : (t + 1) * rows_in] for t in range(turns)], axis=1)
    spare = PC - (w_in.shape[1] - DI)
    kinds = jnp.pad(kinds, ((0, 0), (0, spare - kinds.shape[1])))
    first = jnp.concatenate([w_in[:, DI:], kinds], axis=1)
    blocks = devices // (2 * along)
    mine, recv = [], []
    for g in range(GROUPS):
        part = gather(first[:, SPANS[g]], orders[g])
        part = part.reshape(blocks, along * rows_in, WIDTHS[g])
        mine.append(part)
        recv.append(swap(part, core_bit))

    rest = jnp.concatenate([w_in[:, :D], w_in[:, D:DI], w_out], axis=0)
    rest = lax.all_gather(rest, AX, axis=0, tiled=False)
    wg0 = rest[:, :rows_in].reshape(D, D)
    wg1 = rest[:, rows_in : 2 * rows_in].reshape(D, D)
    wo = rest[:, 2 * rows_in :].reshape(DI, D)

    smem = pl.BlockSpec(memory_space=pltpu.SMEM)
    anywhere = pl.BlockSpec(memory_space=pl.ANY)
    inside = pl.BlockSpec(memory_space=pltpu.VMEM)
    halves = [(blocks, along * rows_in, width) for width in WIDTHS]
    par_spec, head_spec = whole((8, CONV)), whole((8, LANES))
    row_d, row_i, row_c = per_row((PIECE, D)), per_row((PIECE, DI)), per_row((PIECE, CONV))
    row_l = per_row((PIECE, LANES))
    state_spec = pl.BlockSpec((NEAR, 1, NB, DI), lambda r: (0, r, 0, 0))
    hid, conv, raw, act, dsilu, step, cum, pay, weight, par = pl.pallas_call(
        functools.partial(enter_kernel, owned_by),
        grid=(R,),
        in_specs=[smem, row_d, per_row((HALO, D)), head_spec] + [whole(half) for half in halves] * 2,
        out_specs=[
            row_d, per_row((HALO + PIECE, CONV)), row_l, row_c, row_c, row_l, row_l,
            pl.BlockSpec((NEAR, 1, NB, DI + LANES), lambda r: (0, r, 0, 0)),
            whole((D, PC)),
            par_spec,
        ],
        out_shape=[
            struct((R, PIECE, D), BF16), struct((R, HALO + PIECE, CONV), BF16), struct((R, PIECE, LANES), F32),
            struct((R, PIECE, CONV), BF16), struct((R, PIECE, CONV), F32), struct((R, PIECE, LANES), F32),
            struct((R, PIECE, LANES), F32), struct((NEAR, R, NB, DI + LANES), BF16), struct((D, PC), BF16),
            struct((8, CONV), F32),
        ],
        scratch_shapes=[pltpu.VMEM((HALO + PIECE, CONV), F32)],
        compiler_params=params(60),
        cost_estimate=cost(R * 2e9, 2e7),
        name="enter",
    )(core_arg, tok, halo, heads, *mine, *recv)

    def exchange(x):
        return lax.all_to_all(x, "near", split_axis=0, concat_axis=0, tiled=True)

    def carry_on(pieces, growths, backward, ready):
        shape = pieces.shape

        def kernel(p, g, _, o):
            pass_kernel(backward, p, g, o)

        return pl.pallas_call(
            kernel,
            grid=(1,),
            in_specs=[whole(shape), pl.BlockSpec((NEAR, R, NB, LANES), lambda r: (0, 0, 0, DI // LANES)), anywhere],
            out_specs=whole((NEAR, R, NB, DI)),
            out_shape=struct((NEAR, R, NB, DI), BF16),
            compiler_params=params(60),
            cost_estimate=cost(1e7, 2e6),
            name="pass",
        )(pieces, growths, ready)

    pieces = exchange(pay)
    intra = pl.pallas_call(
        inside_kernel,
        grid=(R,),
        in_specs=[row_c, row_l, row_l],
        out_specs=row_i,
        out_shape=struct((R, PIECE, DI), F32),
        scratch_shapes=[pltpu.VMEM((PIECE, DI), BF16)],
        compiler_params=params(60),
        cost_estimate=cost(R * 4e9, 5e6),
        name="inside",
    )(act, step, cum)
    gate, dnorm = pl.pallas_call(
        gate_kernel,
        grid=(R,),
        in_specs=[row_d, row_d, whole((D, D)), whole((D, D)), whole((DI, D))],
        out_specs=[row_i, row_i],
        out_shape=[struct((R, PIECE, DI), BF16), struct((R, PIECE, DI), F32)],
        compiler_params=params(60),
        cost_estimate=cost(R * 2e9, 1e7),
        name="gates",
    )(hid, cot, wg0, wg1, wo)
    st = exchange(carry_on(pieces, pieces, False, intra))

    wide = pltpu.VMEM((PIECE, DI), F32)
    slim = pltpu.VMEM((PIECE, DI), BF16)
    normed, dgate, dy, reach, back, sums = pl.pallas_call(
        middle_kernel,
        grid=(R,),
        in_specs=[state_spec, row_c, row_i, row_l, row_i, row_i, par_spec, head_spec],
        out_specs=[row_i, row_i, row_i, row_l, state_spec, per_row((16, DI))],
        out_shape=[
            struct((R, PIECE, DI), BF16), struct((R, PIECE, DI), BF16), struct((R, PIECE, DI), BF16),
            struct((R, PIECE, LANES), F32), struct((NEAR, R, NB, DI), BF16), struct((R, 16, DI), F32),
        ],
        scratch_shapes=[wide, wide, slim, slim, slim, pltpu.VMEM((16, DI), F32)],
        compiler_params=params(60),
        cost_estimate=cost(R * 2e9, 1.5e7),
        name="middle",
    )(st, act, intra, cum, gate, dnorm, par, heads)

    pieces_b = exchange(back)
    rows_out = w_out.shape[0]
    rest_shape = (blocks, along * rows_in, REST)
    rest_keep, rest_send = pl.pallas_call(
        functools.partial(outer_kernel, rows_in),
        in_specs=[smem] + [inside] * 4,
        out_specs=[inside] * 2,
        out_shape=[struct(rest_shape, F32), struct(rest_shape, BF16)],
        scratch_shapes=[pltpu.VMEM((DI, D), F32), pltpu.VMEM((D, REST), F32)],
        compiler_params=params(60),
        cost_estimate=cost(6e9, 2e7),
        name="outer",
    )(core_arg, cot, hid, normed, dgate)
    rest_recv = swap(rest_send, core_bit)

    u, dcm, dbm = pl.pallas_call(
        pair_kernel,
        grid=(R,),
        in_specs=[row_c, row_l, row_l, row_i, state_spec],
        out_specs=[row_i, row_l, row_l],
        out_shape=[struct((R, PIECE, DI), F32), struct((R, PIECE, N), F32), struct((R, PIECE, N), F32)],
        scratch_shapes=[slim, slim, pltpu.VMEM((PIECE, PIECE), F32)],
        compiler_params=params(60),
        cost_estimate=cost(R * 8e9, 1e7),
        name="pair",
    )(act, step, cum, dy, st)
    dh = pl.pallas_call(
        slope_kernel,
        grid=(R,),
        in_specs=[row_i, whole((D, D)), whole((D, D))],
        out_specs=row_d,
        out_shape=struct((R, PIECE, D), F32),
        compiler_params=params(60),
        cost_estimate=cost(R * 6e8, 6e6),
        name="slope",
    )(dgate, wg0, wg1)
    later_p = carry_on(pieces_b, pieces, True, rest_keep)
    block_out = pl.pallas_call(
        result_kernel,
        grid=(R,),
        in_specs=[row_d, row_i, whole((DI, D)), anywhere],
        out_specs=row_d,
        out_shape=struct((R, PIECE, D), BF16),
        compiler_params=params(60),
        cost_estimate=cost(R * 6e8, 6e6),
        name="result",
    )(tok, normed, wo, later_p)
    later = exchange(later_p)

    dpre, edge, draw, hsum = pl.pallas_call(
        back_kernel,
        grid=(R,),
        in_specs=[
            state_spec, state_spec, row_c, row_l, row_l, row_l, row_i, row_l, row_l, row_i, row_c, row_l, head_spec,
            anywhere, anywhere, anywhere,
        ],
        out_specs=[row_c, per_row((8, CONV)), row_l, per_row((8, LANES))],
        out_shape=[
            struct((R, PIECE, CONV), F32), struct((R, 8, CONV), F32),
            struct((R, PIECE, LANES), F32), struct((R, 8, LANES), F32),
        ],
        scratch_shapes=[wide, wide, wide, slim, slim, slim, pltpu.VMEM((16, DI), F32)],
        compiler_params=params(60),
        cost_estimate=cost(R * 2e9, 1.5e7),
        name="back",
    )(later, st, act, cum, step, raw, u, dcm, dbm, dy, dsilu, reach, heads, dh, block_out, rest_recv)
    edge = lax.ppermute(edge, "near", [(i + 1, i) for i in range(NEAR - 1)])

    small = pl.pallas_call(
        taps_kernel,
        grid=(R,),
        in_specs=[row_c, per_row((HALO + PIECE, CONV)), per_row((16, DI)), per_row((8, LANES))],
        out_specs=whole((8, CONV)),
        out_shape=struct((8, CONV), F32),
        scratch_shapes=[pltpu.VMEM((HALO + PIECE, LANES), F32)],
        compiler_params=params(60),
        cost_estimate=cost(2e7, 6e6),
        name="taps",
    )(dpre, conv, sums, hsum)

    dproj, small, *parts = pl.pallas_call(
        input_kernel,
        in_specs=[smem] + [inside] * 6,
        out_specs=[inside] * (2 + 2 * GROUPS),
        out_shape=[struct((R, PIECE, PC), BF16), struct((8, CONV), F32)]
        + [pltpu.VMEM(half, F32) for half in halves] + [pltpu.VMEM(half, BF16) for half in halves],
        scratch_shapes=[pltpu.VMEM((PIECE + 8, CONV), F32), *(pltpu.VMEM((D, width), F32) for width in WIDTHS)],
        compiler_params=params(44),
        cost_estimate=cost(2e9, 1e7),
        name="input",
    )(core_arg, dpre, edge, draw, hid, par, small)

    def by_bits(x):
        count = x.size // (rows_in * x.shape[-1])
        return x.reshape((2,) * int(math.log2(count)) + (rows_in, x.shape[-1]))

    have = [sorted(order, reverse=True) for order in orders]
    cuts = [[(g, 0, WIDTHS[g]), (GROUPS, g * RWIDTH, RWIDTH)] for g in range(GROUPS)]
    keeps = parts[:GROUPS] + [rest_keep]
    recvs = [swap(x, core_bit) for x in parts[GROUPS:]] + [rest_recv]
    other = swap(small, core_bit)
    ahead = small
    for turn in range(bits - 1):
        now = [order[::-1][turn] for order in orders]
        axes = [have[g].index(now[g]) for g in range(GROUPS)]
        shapes = [(2,) * (bits - 2 - turn) + (rows_in, WIDTHS[g] + RWIDTH) for g in range(GROUPS)]
        *made, small = pl.pallas_call(
            functools.partial(join_kernel, cuts, axes),
            in_specs=[smem, inside, inside, anywhere] + [inside] * (2 * len(keeps)),
            out_specs=[inside] * (2 * GROUPS + 1),
            out_shape=[pltpu.VMEM(shape, F32) for shape in shapes]
            + [pltpu.VMEM(shape, BF16) for shape in shapes] + [pltpu.VMEM((8, CONV), F32)],
            compiler_params=params(40),
            cost_estimate=cost(1e6, 8e6),
            name="join",
        )(
            jnp.stack([bit_of(bit) for bit in now]).astype(jnp.int32),
            small, other, ahead, *map(by_bits, keeps), *map(by_bits, recvs),
        )
        if turn == 0:
            grad_tokens = pl.pallas_call(
                token_kernel,
                grid=(R,),
                in_specs=[row_d, row_d, row_d, per_row((PIECE, PC)), whole((D, PC)), par_spec, anywhere],
                out_specs=row_d,
                out_shape=struct((R, PIECE, D), BF16),
                scratch_shapes=[pltpu.VMEM((PIECE, D), F32)],
                compiler_params=params(32),
                cost_estimate=cost(R * 2e9, 1.5e7),
                name="token",
            )(tok, cot, dh, dproj, weight, par, small)
            ahead = grad_tokens
        for g in range(GROUPS):
            have[g].remove(now[g])
        cuts = [[(g, 0, WIDTHS[g] + RWIDTH)] for g in range(GROUPS)]
        keeps = made[:GROUPS]
        recvs = [swap(x, now[g]) for g, x in enumerate(made[GROUPS:])]
        other = swap(small, orders[0][::-1][turn])
    flat = [x.reshape(rows_in, x.shape[-1]) for x in keeps + recvs]
    small, g_win, g_wout, g_gin = pl.pallas_call(
        last_kernel,
        in_specs=[inside] * (4 + 2 * GROUPS),
        out_specs=[inside] * 4,
        out_shape=[
            struct((8, CONV), F32), struct(w_in.shape, F32), struct(w_out.shape, F32), struct((rows_in, 1), F32),
        ],
        compiler_params=params(32),
        cost_estimate=cost(1e6, 1e6),
        name="last",
    )(small, other, w_in, norm_in[:, None], *flat)
    g_gin = g_gin[:, 0]
    taps = lax.dynamic_slice(small, (0, me * own_conv), (5, own_conv))
    g_gout = lax.dynamic_slice(small, (6, me * own_out), (1, own_out))[0]
    return (
        block_out.reshape(tokens.shape),
        grad_tokens.reshape(tokens.shape),
        g_gin,
        g_win,
        taps[:KW].T,
        taps[KW],
        small[7, :H],
        small[7, LANES : LANES + H],
        small[7, 2 * LANES : 2 * LANES + H],
        g_gout,
        g_wout,
    )


def solution(mesh):
    dp, seq = mesh.shape["dp"], mesh.shape["seq"]
    inner = Mesh(mesh.devices.reshape(dp, seq // NEAR, NEAR), AX)
    split_seq = ("far", "near")
    act = P(None, "dp", split_seq, None)
    vec, mat = P(AX), P(AX, None)

    def run(*args):
        return local((dp * seq, seq), *args)

    return jax.shard_map(
        run,
        mesh=inner,
        in_specs=(act, act, vec, mat, mat, vec, P(), P(), P(), vec, mat),
        out_specs=(act, act, vec, mat, mat, vec, P(), P(), P(), vec, mat),
        check_vma=False,
    )
```

```python
import functools
import itertools
import math

import jax
import jax.numpy as jnp
from jax import lax
from jax.experimental import pallas as pl
from jax.experimental.pallas import tpu as pltpu
from jax.sharding import Mesh
from jax.sharding import PartitionSpec as P

H = 24
HP = 64
N = 128
KW = 4
SEQ_LEN = 2048
PIECE = 256
D = 768
DI = H * HP
CONV = DI + 2 * N
PC = 1920
WIDTHS = (640, 640, 640)
REST = DI + 2 * D
RWIDTH = REST // len(WIDTHS)
GROUPS = len(WIDTHS)
SPANS = tuple(slice(sum(WIDTHS[:g]), sum(WIDTHS[: g + 1])) for g in range(GROUPS))
NEAR = SEQ_LEN // PIECE
NB = N // NEAR
HALO = 16
LANES = 128
HALO_TURN = 2
EPS = 1e-05
F32 = jnp.float32
BF16 = jnp.bfloat16
AX = ("dp", "far", "near")
MIB = 1 << 20


def dot(a, b):
    return lax.dot_general(a, b, (((1,), (0,)), ((), ())), preferred_element_type=F32)


def dot_nt(a, b):
    return lax.dot_general(a, b, (((1,), (1,)), ((), ())), preferred_element_type=F32)


def dot_tn(a, b):
    return lax.dot_general(a, b, (((0,), (0,)), ((), ())), preferred_element_type=F32)


def split(x):
    high = x.astype(BF16)
    return high, (x - high.astype(F32)).astype(BF16)


def heads_to_lanes():
    head = lax.broadcasted_iota(jnp.int32, (LANES, DI), 0)
    lane = lax.broadcasted_iota(jnp.int32, (LANES, DI), 1)
    return jnp.where((lane >> 6) == head, 1.0, 0.0).astype(BF16)


def expand(x, spread):
    high, low = split(x)
    return dot(high, spread) + dot(low, spread)


def collect(high, low, spread):
    return dot_nt(high, spread) + dot_nt(low, spread)


def triangle(count, lower):
    row = lax.broadcasted_iota(jnp.int32, (count, count), 0)
    col = lax.broadcasted_iota(jnp.int32, (count, count), 1)
    return (row >= col) if lower else (row <= col)


def running(mask, x):
    ones = jnp.where(mask, 1.0, 0.0).astype(BF16)
    high, rest = split(x)
    left = x - high.astype(F32)
    mid, low = split(left)
    return dot(ones, high) + dot(ones, mid) + dot(ones, low)


def softplus(z):
    e = jnp.exp(-jnp.abs(z))
    near = e * (1.0 + e * (-0.5 + e * (1.0 / 3.0 + e * (-0.25 + e * 0.2))))
    return jnp.maximum(z, 0.0) + jnp.where(e < 0.02, near, jnp.log(1.0 + e))


def params(limit):
    return pltpu.CompilerParams(vmem_limit_bytes=limit * MIB)


def cost(flops, nbytes, trans=0):
    return pl.CostEstimate(flops=int(flops), bytes_accessed=int(nbytes), transcendentals=int(trans))


def whole(shape):
    return pl.BlockSpec(shape, lambda *_: (0,) * len(shape))


def per_row(shape):
    return pl.BlockSpec((1,) + shape, lambda r: (r,) + (0,) * len(shape))


def struct(shape, kind):
    return jax.ShapeDtypeStruct(shape, kind)


def assemble(core, mine, recv, weight_s):
    count, rows, _ = mine[0].shape
    for g, cols in enumerate(SPANS):
        for y in range(count):
            first = pl.multiple_of((2 * y + core) * rows, 16)
            other = pl.multiple_of((2 * y + 1 - core) * rows, 16)
            weight_s[pl.ds(first, rows), cols] = mine[g][y]
            weight_s[pl.ds(other, rows), cols] = recv[g][y]


def lay_out(weight, par, owned):
    held = weight[:, CONV:]
    for own, kinds in owned:
        rows_in = own * D // CONV if len(kinds) > 1 else (own if kinds[0] == KW + 1 else own // 2)
        devices = D // rows_in
        width = own * devices
        lane = lax.broadcasted_iota(jnp.int32, (LANES, width), 1)
        row = lax.broadcasted_iota(jnp.int32, (LANES, width), 0)
        source = lax.broadcasted_iota(jnp.int32, (devices, D), 1)
        device = lax.broadcasted_iota(jnp.int32, (devices, D), 0)
        place = lax.broadcasted_iota(jnp.int32, (devices, width), 1)
        holder = lax.broadcasted_iota(jnp.int32, (devices, width), 0)
        mine = (place >= holder * own) & (place < holder * own + own)
        for kind in kinds:
            at, block = kind % rows_in, kind // rows_in
            pick = jnp.where(source == device * rows_in + at, 1.0, 0.0).astype(BF16)
            start = H + block * (rows_in * CONV // D)
            spread = jnp.where(row == start + lane % own, 1.0, 0.0).astype(BF16)
            values = dot(dot(pick, held).astype(BF16), spread)
            par[kind : kind + 1, :width] = jnp.sum(jnp.where(mine, values, 0.0), axis=0, keepdims=True)


def enter_kernel(
    owned, core_ref, tok, halo, heads, *refs
):
    mine, recv, rest = refs[:GROUPS], refs[GROUPS : 2 * GROUPS], refs[2 * GROUPS :]
    hid, conv, raw, act, dsilu, step, cum, pay, weight, par, ext = rest

    @pl.when(pl.program_id(0) == 0)
    def _():
        assemble(core_ref[0], mine, recv, weight)
        par[...] = jnp.zeros_like(par)
        lay_out(weight, par, owned)

    gain = par[5:6, :D]
    rows = jnp.concatenate([halo[0], tok[0]], axis=0).astype(F32)
    scale = lax.rsqrt(jnp.mean(rows * rows, axis=-1, keepdims=True) + EPS)
    hidden = (rows * scale * gain).astype(BF16)
    hid[0] = hidden[HALO:]
    for t in range(CONV // 256):
        cols = slice(t * 256, (t + 1) * 256)
        part = dot(hidden, weight[:, cols]).astype(BF16)
        conv[0, :, cols] = part
        ext[:, cols] = part.astype(F32)
    for t in range(CONV // LANES):
        cols = slice(t * LANES, (t + 1) * LANES)
        total = par[4:5, cols]
        for k in range(KW):
            total = total + par[k : k + 1, cols] * ext[pl.ds(HALO - KW + 1 + k, PIECE), cols]
        gate = jax.nn.sigmoid(total)
        act[0, :, cols] = (total * gate).astype(BF16)
        dsilu[0, :, cols] = gate * (1.0 + total * (1.0 - gate))
    raw_step = dot(hidden[HALO:], weight[:, CONV:]).astype(BF16).astype(F32)
    raw_step = jnp.where(lax.broadcasted_iota(jnp.int32, (PIECE, LANES), 1) < H, raw_step, 0.0)
    raw[0] = raw_step
    size = softplus(raw_step + heads[0:1])
    cumul = running(triangle(PIECE, True), size * -jnp.exp(heads[1:2]))
    step[0] = size
    cum[0] = cumul
    spread = heads_to_lanes()
    last = cumul[PIECE - 1 :]
    reach = jnp.exp(last - cumul) * size
    bmat = act[0, :, DI : DI + N]
    for t in range(DI // 256):
        cols = slice(t * 256, (t + 1) * 256)
        weights = (expand(reach, spread[:, cols]) * act[0, :, cols].astype(F32)).astype(BF16)
        state = dot_tn(bmat, weights).astype(BF16)
        pay[:, 0, :, cols] = state.reshape(NEAR, NB, 256)
    growth = jnp.exp(last)
    high, low = split(growth)
    row = lax.broadcasted_iota(jnp.int32, (NB, LANES), 0)
    growths = jnp.where(row == 0, high.astype(F32), jnp.where(row == 1, low.astype(F32), 0.0))
    for j in range(NEAR):
        pay[j, 0, :, DI:] = growths.astype(BF16)


def pass_kernel(backward, pieces, growths, out):
    spread = heads_to_lanes()
    count = out.shape[1]
    for r in range(count):
        high = jnp.concatenate([growths[j, r, 0:1, :] for j in range(NEAR)], axis=0)
        low = jnp.concatenate([growths[j, r, 1:2, :] for j in range(NEAR)], axis=0)
        grow = dot(high, spread) + dot(low, spread)
        state = jnp.zeros((NB, DI), F32)
        order = range(NEAR - 1, -1, -1) if backward else range(NEAR)
        for j in order:
            out[j, r] = state.astype(BF16)
            state = grow[j : j + 1] * state + pieces[j, r, :, :DI].astype(F32)


def inside_kernel(act, step, cum, intra, xdt_s):
    spread = heads_to_lanes()
    size, cumul = step[0], cum[0]
    for t in range(DI // 256):
        cols = slice(t * 256, (t + 1) * 256)
        xdt_s[:, cols] = (expand(size, spread[:, cols]) * act[0, :, cols].astype(F32)).astype(BF16)
    bmat, cmat = act[0, :, DI : DI + N], act[0, :, DI + N :]
    scores = dot_nt(cmat, bmat)
    lower = triangle(PIECE, True)
    turned = cumul.T
    left = lax.broadcasted_iota(jnp.int32, (PIECE, LANES), 1) < HP
    for pair in range(H // 2):
        cols = slice(pair * LANES, (pair + 1) * LANES)
        xdt = xdt_s[:, cols]
        both = []
        for h in (2 * pair, 2 * pair + 1):
            differ = cumul[:, h : h + 1] - turned[h : h + 1, :]
            mix = (scores * jnp.exp(jnp.where(lower, differ, -1e30))).astype(BF16)
            both.append(dot(mix, xdt))
        intra[0, :, cols] = jnp.where(left, both[0], both[1])


def gate_kernel(hid, cot, wg0, wg1, wo, gate, dnorm):
    gate[0, :, :D] = dot(hid[0], wg0[...]).astype(BF16)
    gate[0, :, D:] = dot(hid[0], wg1[...]).astype(BF16)
    dnorm[0] = dot_nt(cot[0], wo[...])


def middle_kernel(
    st, act, intra, cum, gate, dnorm, par, heads,
    normed, dgate, dy, reach, pay, sums, off_s, grow_s, high_s, low_s, doff_s, sum_s
):
    spread = heads_to_lanes()
    state = st[:, 0].reshape(N, DI)
    cmat = act[0, :, DI + N :]
    off_s[...] = dot(cmat, state)
    grow_s[...] = expand(jnp.exp(cum[0]), spread)
    skip = expand(jnp.broadcast_to(heads[2:3], (8, LANES)), spread)[0:1]
    gain = par[6:7, :DI]
    sum_s[...] = jnp.zeros_like(sum_s)
    size = 16

    def chunk(i, carry):
        at = pl.ds(pl.multiple_of(i * size, size), size)
        value = act[0, at, :DI].astype(F32)
        grow = grow_s[at, :]
        base = intra[0, at, :] + grow * off_s[at, :]
        ssd = base + skip * value
        z = gate[0, at, :].astype(F32)
        sig = jax.nn.sigmoid(z)
        silu = z * sig
        gated = ssd * silu
        scale = lax.rsqrt(jnp.mean(gated * gated, axis=-1, keepdims=True) + EPS)
        unit = gated * scale
        normed[0, at, :] = (unit * gain).astype(BF16)
        d_normed = dnorm[0, at, :]
        sum_s[0:8] += (d_normed * unit).reshape(size // 8, 8, DI).sum(axis=0)
        d_unit = d_normed * gain
        along = jnp.mean(d_unit * unit, axis=-1, keepdims=True)
        d_gated = scale * (d_unit - unit * along)
        dgate[0, at, :] = (d_gated * ssd * (sig * (1.0 + z * (1.0 - sig)))).astype(BF16)
        d_ssd = (d_gated * silu).astype(BF16)
        dy[0, at, :] = d_ssd
        d_ssd = d_ssd.astype(F32)
        doff_s[at, :] = (grow * d_ssd).astype(BF16)
        sum_s[8:16] += (d_ssd * value).reshape(size // 8, 8, DI).sum(axis=0)
        high, low = split(d_ssd * base)
        high_s[at, :] = high
        low_s[at, :] = low
        return carry

    lax.fori_loop(0, PIECE // size, chunk, 0, unroll=True)
    d_state = dot_tn(cmat, doff_s[...]).astype(BF16)
    pay[:, 0] = d_state.reshape(NEAR, NB, DI)
    reach[0] = collect(high_s[...], low_s[...], spread)
    high, low = split(sum_s[8:16])
    sums[0, 0:8] = sum_s[0:8]
    sums[0, 8:16, :LANES] = collect(high, low, spread)
    sums[0, 8:16, LANES:] = jnp.zeros((8, DI - LANES), F32)


def outer_kernel(rows_in, core_ref, cot, hid, normed, dgate, keep, send, total, sums):
    core = core_ref[0]
    count = cot.shape[0]
    tangent = cot[...].reshape(count * PIECE, D)
    hidden = hid[...].reshape(count * PIECE, D)
    total[...] = dot_tn(normed[...].reshape(count * PIECE, DI), tangent)
    for half in range(2):
        cols = slice(half * D, (half + 1) * D)
        sums[:, cols] = dot_tn(hidden, dgate[:, :, cols].reshape(count * PIECE, D))
    for d in range(D // rows_in):
        for half in range(2):
            start = (2 * d + half) * rows_in
            sums[d * rows_in : (d + 1) * rows_in, DI + half * D : DI + (half + 1) * D] = total[start : start + rows_in]
    blocks, rows, _ = keep.shape
    for y in range(blocks):
        mine = pl.multiple_of((2 * y + core) * rows, 16)
        other = pl.multiple_of((2 * y + 1 - core) * rows, 16)
        keep[y] = sums[pl.ds(mine, rows)]
        send[y] = sums[pl.ds(other, rows)].astype(BF16)


def join_kernel(cuts, axes, bit_ref, small, other, _, *refs):
    count = 1 + max(operand for group in cuts for operand, _, _ in group)
    keeps, recvs = refs[:count], refs[count : 2 * count]
    outs, sends = refs[2 * count : 2 * count + GROUPS], refs[2 * count + GROUPS : 2 * count + 2 * GROUPS]
    refs[-1][...] = small[...] + other[...]
    for g, group in enumerate(cuts):
        bit, axis = bit_ref[g], axes[g]
        base = 0
        for operand, start, width in group:
            keep, recv = keeps[operand], recvs[operand]
            source, target = slice(start, start + width), slice(base, base + width)
            for place in itertools.product(range(2), repeat=keep.ndim - 3):
                mine = place[:axis] + (bit,) + place[axis:] + (slice(None), source)
                away = place[:axis] + (1 - bit,) + place[axis:] + (slice(None), source)
                here = place + (slice(None), target)
                outs[g][here] = keep[mine] + recv[mine].astype(F32)
                sends[g][here] = (keep[away] + recv[away].astype(F32)).astype(BF16)
            base += width


def last_kernel(small, other, w_in, gain, *refs):
    keeps, recvs = refs[:GROUPS], refs[GROUPS : 2 * GROUPS]
    small_out, g_win, g_wout, g_gin = refs[2 * GROUPS :]
    small_out[...] = small[...] + other[...]
    rows, width = g_win.shape
    for g in range(GROUPS):
        total = keeps[g][...] + recvs[g][...].astype(F32)
        start = DI + SPANS[g].start
        stop = min(start + WIDTHS[g], width)
        g_win[:, start:stop] = total[:, : stop - start]
        first = g * RWIDTH
        for lo, hi, ref, row in ((0, DI, g_win, 0), (DI, DI + D, g_wout, 0), (DI + D, REST, g_wout, rows)):
            a, b = max(lo, first), min(hi, first + RWIDTH)
            if a < b:
                at = WIDTHS[g] + a - first
                ref[row : row + rows, a - lo : b - lo] = total[:, at : at + b - a]
    g_gin[...] = jnp.sum(g_win[...] * w_in[...].astype(F32), axis=-1, keepdims=True) / gain[...].astype(F32)


def result_kernel(tok, normed, wo, _, out):
    out[0] = (tok[0].astype(F32) + dot(normed[0], wo[...])).astype(BF16)


def pair_kernel(act, step, cum, dy, st, u, dcm, dbm, xdt_s, doff_s, dsc_s):
    spread = heads_to_lanes()
    size, cumul = step[0], cum[0]
    grown = jnp.exp(cumul)
    for t in range(DI // 256):
        cols = slice(t * 256, (t + 1) * 256)
        xdt_s[:, cols] = (expand(size, spread[:, cols]) * act[0, :, cols].astype(F32)).astype(BF16)
        doff_s[:, cols] = (expand(grown, spread[:, cols]) * dy[0, :, cols].astype(F32)).astype(BF16)
    bmat, cmat = act[0, :, DI : DI + N], act[0, :, DI + N :]
    scores = dot_nt(cmat, bmat)
    lower = triangle(PIECE, True)
    turned = cumul.T
    dsc_s[...] = jnp.zeros_like(dsc_s)
    left = lax.broadcasted_iota(jnp.int32, (PIECE, LANES), 1) < HP
    zero = jnp.zeros((PIECE, LANES), BF16)
    for pair in range(H // 2):
        cols = slice(pair * LANES, (pair + 1) * LANES)
        xdt = xdt_s[:, cols]
        slope = dy[0, :, cols]
        slope_t = slope.astype(F32).T.astype(BF16)
        both = []
        for side in (0, 1):
            h = 2 * pair + side
            differ = cumul[:, h : h + 1] - turned[h : h + 1, :]
            decay = jnp.exp(jnp.where(lower, differ, -1e30))
            mix = (scores * decay).astype(BF16)
            own = jnp.where(left, slope, zero) if side == 0 else jnp.where(left, zero, slope)
            dsc_s[...] += dot_nt(own, xdt) * decay
            both.append(dot(slope_t[side * HP : (side + 1) * HP], mix))
        u[0, :, cols] = jnp.concatenate(both, axis=0).T
    d_scores = dsc_s[...].astype(BF16)
    state = st[:, 0].reshape(N, DI)
    dcm[0] = dot_nt(doff_s[...], state) + dot(d_scores, bmat)
    dbm[0] = dot_tn(d_scores, cmat)


def back_kernel(
    later, st, act, cum, step, raw, u, dcm, dbm, dy, dsilu, reach, heads, _, __, ___,
    dpre, edge, draw, hsum, dw_s, far_s, size_s, high_s, low_s, wts_s, sum_s
):
    spread = heads_to_lanes()
    size, cumul = step[0], cum[0]
    last = cumul[PIECE - 1 :]
    d_local = later[:, 0].reshape(N, DI)
    bmat = act[0, :, DI : DI + N]
    dw_s[...] = dot(bmat, d_local)
    far_s[...] = expand(jnp.exp(last - cumul), spread)
    size_s[...] = expand(size, spread)
    skip = expand(jnp.broadcast_to(heads[2:3], (8, LANES)), spread)[0:1]
    sum_s[...] = jnp.zeros_like(sum_s)
    rows = 16

    def chunk(i, carry):
        at = pl.ds(pl.multiple_of(i * rows, rows), rows)
        value = act[0, at, :DI].astype(F32)
        far, long = far_s[at, :], size_s[at, :]
        through = far * dw_s[at, :]
        d_xdt = u[0, at, :] + through
        d_value = long * d_xdt + skip * dy[0, at, :].astype(F32)
        dpre[0, at, :DI] = d_value * dsilu[0, at, :DI]
        high, low = split(value * d_xdt)
        high_s[at, :] = high
        low_s[at, :] = low
        xdt = long * value
        wts_s[at, :] = (far * xdt).astype(BF16)
        sum_s[0:8] += (xdt * through).reshape(rows // 8, 8, DI).sum(axis=0)
        return carry

    lax.fori_loop(0, PIECE // rows, chunk, 0, unroll=True)
    for j in range(NEAR):
        prod = later[j, 0].astype(F32) * st[j, 0].astype(F32)
        sum_s[8:16] += prod.reshape(NB // 8, 8, DI).sum(axis=0)
    d_bmat = dbm[0] + dot_nt(wts_s[...], d_local)
    dpre[0, :, DI : DI + N] = d_bmat * dsilu[0, :, DI : DI + N]
    dpre[0, :, DI + N :] = dcm[0] * dsilu[0, :, DI + N :]
    edge[0] = dpre[0, 0:8, :]
    q = collect(high_s[...], low_s[...], spread)
    high, low = split(sum_s[...])
    sums = collect(high, low, spread)
    d_last = jnp.sum(sums[0:8], axis=0, keepdims=True)
    d_last = d_last + jnp.exp(last) * jnp.sum(sums[8:16], axis=0, keepdims=True)
    d_cum = reach[0] - size * q
    row = lax.broadcasted_iota(jnp.int32, (PIECE, LANES), 0)
    d_cum = d_cum + jnp.where(row == PIECE - 1, d_last, 0.0)
    d_rate = running(triangle(PIECE, False), d_cum)
    decay = jnp.exp(heads[1:2])
    d_size = q - d_rate * decay
    d_raw = d_size * jax.nn.sigmoid(raw[0] + heads[0:1])
    draw[0] = d_raw
    for_bias = jnp.sum(d_raw, axis=0, keepdims=True)
    for_log = -jnp.sum(d_rate * size, axis=0, keepdims=True) * decay
    pick = lax.broadcasted_iota(jnp.int32, (8, LANES), 0)
    hsum[0] = jnp.where(pick == 0, for_bias, jnp.where(pick == 1, for_log, 0.0))


def input_kernel(core_ref, dpre, edge, draw, hid, par, gone, dproj, small, *refs):
    keeps, sends = refs[:GROUPS], refs[GROUPS : 2 * GROUPS]
    ext, *totals = refs[2 * GROUPS :]
    small[...] = gone[...]
    core = core_ref[0]
    count = dpre.shape[0]
    for r in range(count):
        ext[:PIECE] = dpre[r]
        ext[PIECE:] = edge[r]
        for t in range(CONV // LANES):
            cols = slice(t * LANES, (t + 1) * LANES)
            sum_k = par[KW - 1 : KW, cols] * ext[0:PIECE, cols]
            for k in range(KW - 1):
                sum_k = sum_k + par[k : k + 1, cols] * ext[pl.ds(KW - 1 - k, PIECE), cols]
            dproj[r, :, cols] = sum_k.astype(BF16)
        dproj[r, :, CONV:] = draw[r].astype(BF16)
    hidden = hid[...].reshape(count * PIECE, D)
    for keep, send, total, cols in zip(keeps, sends, totals, SPANS):
        total[...] = dot_tn(hidden, dproj[:, :, cols].reshape(count * PIECE, cols.stop - cols.start))
        blocks, rows, _ = keep.shape
        for y in range(blocks):
            mine = pl.multiple_of((2 * y + core) * rows, 16)
            other = pl.multiple_of((2 * y + 1 - core) * rows, 16)
            keep[y] = total[pl.ds(mine, rows)]
            send[y] = total[pl.ds(other, rows)].astype(BF16)


def taps_kernel(dpre, conv, sums, hsum, small, ext):
    @pl.when(pl.program_id(0) == 0)
    def _():
        small[...] = jnp.zeros_like(small)

    for t in range(CONV // LANES):
        cols = slice(t * LANES, (t + 1) * LANES)
        slope = dpre[0, :, cols]
        ext[...] = conv[0, :, cols].astype(F32)
        for k in range(KW):
            prod = slope * ext[pl.ds(HALO - KW + 1 + k, PIECE), :]
            small[k : k + 1, cols] += jnp.sum(prod, axis=0, keepdims=True)
        small[4:5, cols] += jnp.sum(slope, axis=0, keepdims=True)
    small[6:7, :DI] += jnp.sum(sums[0, 0:8], axis=0, keepdims=True)
    small[7:8, 0:LANES] += hsum[0, 0:1]
    small[7:8, LANES : 2 * LANES] += hsum[0, 1:2]
    small[7:8, 2 * LANES : 3 * LANES] += jnp.sum(sums[0, 8:16, :LANES], axis=0, keepdims=True)


def slope_kernel(dgate, wg0, wg1, dh):
    dh[0] = dot_nt(dgate[0, :, :D], wg0[...]) + dot_nt(dgate[0, :, D:], wg1[...])


def token_kernel(tok, cot, dh, dproj, weight, par, _, grad, dh_s):
    dh_s[...] = dh[0] + dot_nt(dproj[0], weight[...])
    gain = par[5:6, :D]
    rows = 32

    def chunk(i, carry):
        at = pl.ds(pl.multiple_of(i * rows, rows), rows)
        x = tok[0, at, :].astype(F32)
        scale = lax.rsqrt(jnp.mean(x * x, axis=-1, keepdims=True) + EPS)
        unit = x * scale
        d_unit = dh_s[at, :] * gain
        along = jnp.mean(d_unit * unit, axis=-1, keepdims=True)
        grad[0, at, :] = (cot[0, at, :].astype(F32) + scale * (d_unit - unit * along)).astype(BF16)
        return carry

    lax.fori_loop(0, PIECE // rows, chunk, 0, unroll=True)


def local(size, tokens, cotangent, norm_in, w_in, conv_w, conv_b, dt_bias, a_log, skip, norm_out, w_out):
    devices, along = size
    bits = int(math.log2(devices))
    core_bit = int(math.log2(along))
    me = lax.axis_index(AX)
    core = ((me >> core_bit) & 1).astype(jnp.int32)
    core_arg = core.reshape(1)
    high_bits = list(range(bits - 1, core_bit, -1))
    far_bits = list(range(core_bit - 1, -1, -1))
    dims = [far_bits[-1:], far_bits[:-1], high_bits] if core_bit == 3 else [far_bits[-3:], far_bits[:-3], high_bits]
    orders = [dims[1] + dims[2] + dims[0], dims[0] + dims[1] + dims[2], dims[2] + dims[0] + dims[1]]
    if [len(dim) for dim in dims] == [1, 2, 1]:
        x, (top, low), y = dims[0][0], dims[1], dims[2][0]
        orders = [[top, low, y, x], [top, x, low, y], [top, y, x, low]]

    def swap(x, bit):
        return lax.ppermute(x, AX, [(i, i ^ (1 << bit)) for i in range(devices)])

    def bit_of(bit):
        return (me >> bit) & 1

    def after(x, other):
        rows, cols = min(x.shape[-2], other.shape[-2], 8), min(x.shape[-1], other.shape[-1])
        part = other[(0,) * (other.ndim - 2)][:rows, :cols].astype(x.dtype)
        return x + 0 * jnp.pad(part, ((0, x.shape[-2] - rows), (0, x.shape[-1] - cols)))

    def gather(x, order):
        have = []
        for bit in order:
            if order is orders[0]:
                if len(have) == HALO_TURN:
                    x = after(x, halo)
            other = swap(x, bit)
            have = sorted(have + [bit], reverse=True)
            mine = bit_of(bit) == 0
            low, high = jnp.where(mine, x, other), jnp.where(mine, other, x)
            x = jnp.stack([low, high], axis=have.index(bit))
        return x

    micro, batch, count = tokens.shape[:3]
    tok = tokens.reshape(micro * batch, count, D)
    cot = cotangent.reshape(micro * batch, count, D)
    R = micro * batch
    heads = jnp.zeros((8, LANES), F32)
    for i, a in enumerate((dt_bias, a_log, skip)):
        heads = heads.at[i, :H].set(a)

    own_conv, own_in, own_out = conv_b.shape[0], norm_in.shape[0], norm_out.shape[0]
    owned_by = ((own_conv, tuple(range(KW + 1))), (own_in, (KW + 1,)), (own_out, (KW + 2,)))

    halo = lax.ppermute(tok[:, count - HALO :], "near", [(i, i + 1) for i in range(NEAR - 1)])
    rows_in = w_in.shape[0]
    kinds = jnp.concatenate(
        [
            conv_w.T,
            conv_b[None],
            jnp.pad(norm_in, (0, own_conv - own_in))[None],
            jnp.pad(norm_out, (0, own_conv - own_out))[None],
        ],
        axis=0,
    )
    turns = -(-kinds.shape[0] // rows_in)
    kinds = jnp.pad(kinds, ((0, turns * rows_in - kinds.shape[0]), (0, 0)))
    kinds = jnp.concatenate([kinds[t * rows_in : (t + 1) * rows_in] for t in range(turns)], axis=1)
    spare = PC - (w_in.shape[1] - DI)
    kinds = jnp.pad(kinds, ((0, 0), (0, spare - kinds.shape[1])))
    first = jnp.concatenate([w_in[:, DI:], kinds], axis=1)
    blocks = devices // (2 * along)
    mine, recv = [], []
    for g in range(GROUPS):
        part = gather(first[:, SPANS[g]], orders[g])
        part = part.reshape(blocks, along * rows_in, WIDTHS[g])
        mine.append(part)
        recv.append(swap(part, core_bit))

    rest = jnp.concatenate([w_in[:, :D], w_in[:, D:DI], w_out], axis=0)
    rest = lax.all_gather(rest, AX, axis=0, tiled=False)
    wg0 = rest[:, :rows_in].reshape(D, D)
    wg1 = rest[:, rows_in : 2 * rows_in].reshape(D, D)
    wo = rest[:, 2 * rows_in :].reshape(DI, D)

    smem = pl.BlockSpec(memory_space=pltpu.SMEM)
    anywhere = pl.BlockSpec(memory_space=pl.ANY)
    inside = pl.BlockSpec(memory_space=pltpu.VMEM)
    halves = [(blocks, along * rows_in, width) for width in WIDTHS]
    par_spec, head_spec = whole((8, CONV)), whole((8, LANES))
    row_d, row_i, row_c = per_row((PIECE, D)), per_row((PIECE, DI)), per_row((PIECE, CONV))
    row_l = per_row((PIECE, LANES))
    state_spec = pl.BlockSpec((NEAR, 1, NB, DI), lambda r: (0, r, 0, 0))
    hid, conv, raw, act, dsilu, step, cum, pay, weight, par = pl.pallas_call(
        functools.partial(enter_kernel, owned_by),
        grid=(R,),
        in_specs=[smem, row_d, per_row((HALO, D)), head_spec] + [whole(half) for half in halves] * 2,
        out_specs=[
            row_d, per_row((HALO + PIECE, CONV)), row_l, row_c, row_c, row_l, row_l,
            pl.BlockSpec((NEAR, 1, NB, DI + LANES), lambda r: (0, r, 0, 0)),
            whole((D, PC)),
            par_spec,
        ],
        out_shape=[
            struct((R, PIECE, D), BF16), struct((R, HALO + PIECE, CONV), BF16), struct((R, PIECE, LANES), F32),
            struct((R, PIECE, CONV), BF16), struct((R, PIECE, CONV), F32), struct((R, PIECE, LANES), F32),
            struct((R, PIECE, LANES), F32), struct((NEAR, R, NB, DI + LANES), BF16), struct((D, PC), BF16),
            struct((8, CONV), F32),
        ],
        scratch_shapes=[pltpu.VMEM((HALO + PIECE, CONV), F32)],
        compiler_params=params(60),
        cost_estimate=cost(R * 2e9, 2e7),
        name="enter",
    )(core_arg, tok, halo, heads, *mine, *recv)

    def exchange(x):
        return lax.all_to_all(x, "near", split_axis=0, concat_axis=0, tiled=True)

    def carry_on(pieces, growths, backward, ready):
        shape = pieces.shape

        def kernel(p, g, _, o):
            pass_kernel(backward, p, g, o)

        return pl.pallas_call(
            kernel,
            grid=(1,),
            in_specs=[whole(shape), pl.BlockSpec((NEAR, R, NB, LANES), lambda r: (0, 0, 0, DI // LANES)), anywhere],
            out_specs=whole((NEAR, R, NB, DI)),
            out_shape=struct((NEAR, R, NB, DI), BF16),
            compiler_params=params(60),
            cost_estimate=cost(1e7, 2e6),
            name="pass",
        )(pieces, growths, ready)

    pieces = exchange(pay)
    intra = pl.pallas_call(
        inside_kernel,
        grid=(R,),
        in_specs=[row_c, row_l, row_l],
        out_specs=row_i,
        out_shape=struct((R, PIECE, DI), F32),
        scratch_shapes=[pltpu.VMEM((PIECE, DI), BF16)],
        compiler_params=params(60),
        cost_estimate=cost(R * 4e9, 5e6),
        name="inside",
    )(act, step, cum)
    gate, dnorm = pl.pallas_call(
        gate_kernel,
        grid=(R,),
        in_specs=[row_d, row_d, whole((D, D)), whole((D, D)), whole((DI, D))],
        out_specs=[row_i, row_i],
        out_shape=[struct((R, PIECE, DI), BF16), struct((R, PIECE, DI), F32)],
        compiler_params=params(60),
        cost_estimate=cost(R * 2e9, 1e7),
        name="gates",
    )(hid, cot, wg0, wg1, wo)
    st = exchange(carry_on(pieces, pieces, False, intra))

    wide = pltpu.VMEM((PIECE, DI), F32)
    slim = pltpu.VMEM((PIECE, DI), BF16)
    normed, dgate, dy, reach, back, sums = pl.pallas_call(
        middle_kernel,
        grid=(R,),
        in_specs=[state_spec, row_c, row_i, row_l, row_i, row_i, par_spec, head_spec],
        out_specs=[row_i, row_i, row_i, row_l, state_spec, per_row((16, DI))],
        out_shape=[
            struct((R, PIECE, DI), BF16), struct((R, PIECE, DI), BF16), struct((R, PIECE, DI), BF16),
            struct((R, PIECE, LANES), F32), struct((NEAR, R, NB, DI), BF16), struct((R, 16, DI), F32),
        ],
        scratch_shapes=[wide, wide, slim, slim, slim, pltpu.VMEM((16, DI), F32)],
        compiler_params=params(60),
        cost_estimate=cost(R * 2e9, 1.5e7),
        name="middle",
    )(st, act, intra, cum, gate, dnorm, par, heads)

    pieces_b = exchange(back)
    rows_out = w_out.shape[0]
    rest_shape = (blocks, along * rows_in, REST)
    rest_keep, rest_send = pl.pallas_call(
        functools.partial(outer_kernel, rows_in),
        in_specs=[smem] + [inside] * 4,
        out_specs=[inside] * 2,
        out_shape=[struct(rest_shape, F32), struct(rest_shape, BF16)],
        scratch_shapes=[pltpu.VMEM((DI, D), F32), pltpu.VMEM((D, REST), F32)],
        compiler_params=params(60),
        cost_estimate=cost(6e9, 2e7),
        name="outer",
    )(core_arg, cot, hid, normed, dgate)
    rest_recv = swap(rest_send, core_bit)

    u, dcm, dbm = pl.pallas_call(
        pair_kernel,
        grid=(R,),
        in_specs=[row_c, row_l, row_l, row_i, state_spec],
        out_specs=[row_i, row_l, row_l],
        out_shape=[struct((R, PIECE, DI), F32), struct((R, PIECE, N), F32), struct((R, PIECE, N), F32)],
        scratch_shapes=[slim, slim, pltpu.VMEM((PIECE, PIECE), F32)],
        compiler_params=params(60),
        cost_estimate=cost(R * 8e9, 1e7),
        name="pair",
    )(act, step, cum, dy, st)
    dh = pl.pallas_call(
        slope_kernel,
        grid=(R,),
        in_specs=[row_i, whole((D, D)), whole((D, D))],
        out_specs=row_d,
        out_shape=struct((R, PIECE, D), F32),
        compiler_params=params(60),
        cost_estimate=cost(R * 6e8, 6e6),
        name="slope",
    )(dgate, wg0, wg1)
    later_p = carry_on(pieces_b, pieces, True, rest_keep)
    block_out = pl.pallas_call(
        result_kernel,
        grid=(R,),
        in_specs=[row_d, row_i, whole((DI, D)), anywhere],
        out_specs=row_d,
        out_shape=struct((R, PIECE, D), BF16),
        compiler_params=params(60),
        cost_estimate=cost(R * 6e8, 6e6),
        name="result",
    )(tok, normed, wo, later_p)
    later = exchange(later_p)

    dpre, edge, draw, hsum = pl.pallas_call(
        back_kernel,
        grid=(R,),
        in_specs=[
            state_spec, state_spec, row_c, row_l, row_l, row_l, row_i, row_l, row_l, row_i, row_c, row_l, head_spec,
            anywhere, anywhere, anywhere,
        ],
        out_specs=[row_c, per_row((8, CONV)), row_l, per_row((8, LANES))],
        out_shape=[
            struct((R, PIECE, CONV), F32), struct((R, 8, CONV), F32),
            struct((R, PIECE, LANES), F32), struct((R, 8, LANES), F32),
        ],
        scratch_shapes=[wide, wide, wide, slim, slim, slim, pltpu.VMEM((16, DI), F32)],
        compiler_params=params(60),
        cost_estimate=cost(R * 2e9, 1.5e7),
        name="back",
    )(later, st, act, cum, step, raw, u, dcm, dbm, dy, dsilu, reach, heads, dh, block_out, rest_recv)
    edge = lax.ppermute(edge, "near", [(i + 1, i) for i in range(NEAR - 1)])

    small = pl.pallas_call(
        taps_kernel,
        grid=(R,),
        in_specs=[row_c, per_row((HALO + PIECE, CONV)), per_row((16, DI)), per_row((8, LANES))],
        out_specs=whole((8, CONV)),
        out_shape=struct((8, CONV), F32),
        scratch_shapes=[pltpu.VMEM((HALO + PIECE, LANES), F32)],
        compiler_params=params(60),
        cost_estimate=cost(2e7, 6e6),
        name="taps",
    )(dpre, conv, sums, hsum)

    dproj, small, *parts = pl.pallas_call(
        input_kernel,
        in_specs=[smem] + [inside] * 6,
        out_specs=[inside] * (2 + 2 * GROUPS),
        out_shape=[struct((R, PIECE, PC), BF16), struct((8, CONV), F32)]
        + [pltpu.VMEM(half, F32) for half in halves] + [pltpu.VMEM(half, BF16) for half in halves],
        scratch_shapes=[pltpu.VMEM((PIECE + 8, CONV), F32), *(pltpu.VMEM((D, width), F32) for width in WIDTHS)],
        compiler_params=params(44),
        cost_estimate=cost(2e9, 1e7),
        name="input",
    )(core_arg, dpre, edge, draw, hid, par, small)

    def by_bits(x):
        count = x.size // (rows_in * x.shape[-1])
        return x.reshape((2,) * int(math.log2(count)) + (rows_in, x.shape[-1]))

    have = [sorted(order, reverse=True) for order in orders]
    cuts = [[(g, 0, WIDTHS[g]), (GROUPS, g * RWIDTH, RWIDTH)] for g in range(GROUPS)]
    keeps = parts[:GROUPS] + [rest_keep]
    recvs = [swap(x, core_bit) for x in parts[GROUPS:]] + [rest_recv]
    other = swap(small, core_bit)
    ahead = small
    for turn in range(bits - 1):
        now = [order[::-1][turn] for order in orders]
        axes = [have[g].index(now[g]) for g in range(GROUPS)]
        shapes = [(2,) * (bits - 2 - turn) + (rows_in, WIDTHS[g] + RWIDTH) for g in range(GROUPS)]
        *made, small = pl.pallas_call(
            functools.partial(join_kernel, cuts, axes),
            in_specs=[smem, inside, inside, anywhere] + [inside] * (2 * len(keeps)),
            out_specs=[inside] * (2 * GROUPS + 1),
            out_shape=[pltpu.VMEM(shape, F32) for shape in shapes]
            + [pltpu.VMEM(shape, BF16) for shape in shapes] + [pltpu.VMEM((8, CONV), F32)],
            compiler_params=params(40),
            cost_estimate=cost(1e6, 8e6),
            name="join",
        )(
            jnp.stack([bit_of(bit) for bit in now]).astype(jnp.int32),
            small, other, ahead, *map(by_bits, keeps), *map(by_bits, recvs),
        )
        if turn == 0:
            grad_tokens = pl.pallas_call(
                token_kernel,
                grid=(R,),
                in_specs=[row_d, row_d, row_d, per_row((PIECE, PC)), whole((D, PC)), par_spec, anywhere],
                out_specs=row_d,
                out_shape=struct((R, PIECE, D), BF16),
                scratch_shapes=[pltpu.VMEM((PIECE, D), F32)],
                compiler_params=params(32),
                cost_estimate=cost(R * 2e9, 1.5e7),
                name="token",
            )(tok, cot, dh, dproj, weight, par, small)
            ahead = grad_tokens
        for g in range(GROUPS):
            have[g].remove(now[g])
        cuts = [[(g, 0, WIDTHS[g] + RWIDTH)] for g in range(GROUPS)]
        keeps = made[:GROUPS]
        recvs = [swap(x, now[g]) for g, x in enumerate(made[GROUPS:])]
        other = swap(small, orders[0][::-1][turn])
    flat = [x.reshape(rows_in, x.shape[-1]) for x in keeps + recvs]
    small, g_win, g_wout, g_gin = pl.pallas_call(
        last_kernel,
        in_specs=[inside] * (4 + 2 * GROUPS),
        out_specs=[inside] * 4,
        out_shape=[
            struct((8, CONV), F32), struct(w_in.shape, F32), struct(w_out.shape, F32), struct((rows_in, 1), F32),
        ],
        compiler_params=params(32),
        cost_estimate=cost(1e6, 1e6),
        name="last",
    )(small, other, w_in, norm_in[:, None], *flat)
    g_gin = g_gin[:, 0]
    taps = lax.dynamic_slice(small, (0, me * own_conv), (5, own_conv))
    g_gout = lax.dynamic_slice(small, (6, me * own_out), (1, own_out))[0]
    return (
        block_out.reshape(tokens.shape),
        grad_tokens.reshape(tokens.shape),
        g_gin,
        g_win,
        taps[:KW].T,
        taps[KW],
        small[7, :H],
        small[7, LANES : LANES + H],
        small[7, 2 * LANES : 2 * LANES + H],
        g_gout,
        g_wout,
    )


def solution(mesh):
    dp, seq = mesh.shape["dp"], mesh.shape["seq"]
    inner = Mesh(mesh.devices.reshape(dp, seq // NEAR, NEAR), AX)
    split_seq = ("far", "near")
    act = P(None, "dp", split_seq, None)
    vec, mat = P(AX), P(AX, None)

    def run(*args):
        return local((dp * seq, seq), *args)

    return jax.shard_map(
        run,
        mesh=inner,
        in_specs=(act, act, vec, mat, mat, vec, P(), P(), P(), vec, mat),
        out_specs=(act, act, vec, mat, mat, vec, P(), P(), P(), vec, mat),
        check_vma=False,
    )
```

```python
import functools
import itertools
import math

import jax
import jax.numpy as jnp
from jax import lax
from jax.experimental import pallas as pl
from jax.experimental.pallas import tpu as pltpu
from jax.sharding import Mesh
from jax.sharding import PartitionSpec as P

H = 24
HP = 64
N = 128
KW = 4
SEQ_LEN = 2048
PIECE = 256
D = 768
DI = H * HP
CONV = DI + 2 * N
PC = 1920
WIDTHS = (640, 640, 640)
REST = DI + 2 * D
RWIDTH = REST // len(WIDTHS)
GROUPS = len(WIDTHS)
SPANS = tuple(slice(sum(WIDTHS[:g]), sum(WIDTHS[: g + 1])) for g in range(GROUPS))
NEAR = SEQ_LEN // PIECE
QUAD = NEAR // 2
NQ = N // QUAD
HALO = 16
LANES = 128
HALO_TURN = 2
SPLIT_TURN = 3
EPS = 1e-05
F32 = jnp.float32
BF16 = jnp.bfloat16
AX = ("dp", "far", "near")
MIB = 1 << 20


def dot(a, b):
    return lax.dot_general(a, b, (((1,), (0,)), ((), ())), preferred_element_type=F32)


def dot_nt(a, b):
    return lax.dot_general(a, b, (((1,), (1,)), ((), ())), preferred_element_type=F32)


def dot_tn(a, b):
    return lax.dot_general(a, b, (((0,), (0,)), ((), ())), preferred_element_type=F32)


def split(x):
    high = x.astype(BF16)
    return high, (x - high.astype(F32)).astype(BF16)


def heads_to_lanes():
    head = lax.broadcasted_iota(jnp.int32, (LANES, DI), 0)
    lane = lax.broadcasted_iota(jnp.int32, (LANES, DI), 1)
    return jnp.where((lane >> 6) == head, 1.0, 0.0).astype(BF16)


def expand(x, spread):
    high, low = split(x)
    return dot(high, spread) + dot(low, spread)


def collect(high, low, spread):
    return dot_nt(high, spread) + dot_nt(low, spread)


def triangle(count, lower):
    row = lax.broadcasted_iota(jnp.int32, (count, count), 0)
    col = lax.broadcasted_iota(jnp.int32, (count, count), 1)
    return (row >= col) if lower else (row <= col)


def running(mask, x):
    ones = jnp.where(mask, 1.0, 0.0).astype(BF16)
    high, rest = split(x)
    left = x - high.astype(F32)
    mid, low = split(left)
    return dot(ones, high) + dot(ones, mid) + dot(ones, low)


def softplus(z):
    e = jnp.exp(-jnp.abs(z))
    near = e * (1.0 + e * (-0.5 + e * (1.0 / 3.0 + e * (-0.25 + e * 0.2))))
    return jnp.maximum(z, 0.0) + jnp.where(e < 0.02, near, jnp.log(1.0 + e))


def params(limit):
    return pltpu.CompilerParams(vmem_limit_bytes=limit * MIB)


def cost(flops, nbytes, trans=0):
    return pl.CostEstimate(flops=int(flops), bytes_accessed=int(nbytes), transcendentals=int(trans))


def whole(shape):
    return pl.BlockSpec(shape, lambda *_: (0,) * len(shape))


def per_row(shape):
    return pl.BlockSpec((1,) + shape, lambda r: (r,) + (0,) * len(shape))


def struct(shape, kind):
    return jax.ShapeDtypeStruct(shape, kind)


def assemble(core, mine, recv, weight_s, spans):
    count, rows, _ = mine[0].shape
    for g, cols in enumerate(spans):
        for y in range(count):
            first = pl.multiple_of((2 * y + core) * rows, 16)
            other = pl.multiple_of((2 * y + 1 - core) * rows, 16)
            weight_s[pl.ds(first, rows), cols] = mine[g][y]
            weight_s[pl.ds(other, rows), cols] = recv[g][y]


def lay_out(weight, par, owned):
    held = weight[:, CONV:]
    rows_in = owned[1][0]
    devices = D // rows_in
    total = 1 + max(max(kinds) for _, kinds in owned)
    source = lax.broadcasted_iota(jnp.int32, (devices, D), 1)
    device = lax.broadcasted_iota(jnp.int32, (devices, D), 0)
    picks = [jnp.where(source == device * rows_in + kind % rows_in, 1.0, 0.0) for kind in range(total)]
    picked = dot(jnp.concatenate(picks, axis=0).astype(BF16), held).astype(BF16)
    for own, kinds in owned:
        width = own * devices
        lane = lax.broadcasted_iota(jnp.int32, (LANES, width), 1)
        row = lax.broadcasted_iota(jnp.int32, (LANES, width), 0)
        place = lax.broadcasted_iota(jnp.int32, (devices, width), 1)
        holder = lax.broadcasted_iota(jnp.int32, (devices, width), 0)
        mine = (place >= holder * own) & (place < holder * own + own)
        for block in sorted({kind // rows_in for kind in kinds}):
            some = [kind for kind in kinds if kind // rows_in == block]
            start = H + block * (rows_in * CONV // D)
            spread = jnp.where(row == start + lane % own, 1.0, 0.0).astype(BF16)
            values = dot(picked[some[0] * devices : (some[-1] + 1) * devices], spread)
            for i, kind in enumerate(some):
                part = jnp.where(mine, values[i * devices : (i + 1) * devices], 0.0)
                par[kind : kind + 1, :width] = jnp.sum(part, axis=0, keepdims=True)


def enter_kernel(
    owned, core_ref, quad_ref, tok, halo, heads, *refs
):
    mine, recv, rest = refs[:GROUPS], refs[GROUPS : 2 * GROUPS], refs[2 * GROUPS :]
    hid, conv, raw, act, step, cum, *pays, par, ext, state_s, weight = rest

    @pl.when(pl.program_id(0) == 0)
    def _():
        assemble(core_ref[0], mine, recv, weight, SPANS)
        par[...] = jnp.zeros_like(par)
        lay_out(weight, par, owned)

    gain = par[5:6, :D]
    rows = jnp.concatenate([halo[0], tok[0]], axis=0).astype(F32)
    scale = lax.rsqrt(jnp.mean(rows * rows, axis=-1, keepdims=True) + EPS)
    hidden = (rows * scale * gain).astype(BF16)
    hid[0] = hidden[HALO:]
    for t in range(CONV // 256):
        cols = slice(t * 256, (t + 1) * 256)
        part = dot(hidden, weight[:, cols]).astype(BF16)
        conv[0, :, cols] = part
        ext[:, cols] = part.astype(F32)
    for t in range(CONV // LANES):
        cols = slice(t * LANES, (t + 1) * LANES)
        total = par[4:5, cols]
        for k in range(KW):
            total = total + par[k : k + 1, cols] * ext[pl.ds(HALO - KW + 1 + k, PIECE), cols]
        gate = jax.nn.sigmoid(total)
        act[0, :, cols] = (total * gate).astype(BF16)
    raw_step = dot(hidden[HALO:], weight[:, CONV:]).astype(BF16).astype(F32)
    raw_step = jnp.where(lax.broadcasted_iota(jnp.int32, (PIECE, LANES), 1) < H, raw_step, 0.0)
    raw[0] = raw_step
    size = softplus(raw_step + heads[0:1])
    cumul = running(triangle(PIECE, True), size * -jnp.exp(heads[1:2]))
    step[0] = size
    cum[0] = cumul
    spread = heads_to_lanes()
    last = cumul[PIECE - 1 :]
    reach = jnp.exp(last - cumul) * size
    bmat = act[0, :, DI : DI + N]
    for t in range(DI // 256):
        cols = slice(t * 256, (t + 1) * 256)
        weights = (expand(reach, spread[:, cols]) * act[0, :, cols].astype(F32)).astype(BF16)
        state_s[:, cols] = dot_tn(bmat, weights).astype(BF16)
    growth = jnp.exp(last)
    high, low = split(growth)
    row = lax.broadcasted_iota(jnp.int32, (NQ, LANES), 0)
    growths = jnp.where(row == 0, high.astype(F32), jnp.where(row == 1, low.astype(F32), 0.0)).astype(BF16)
    for k, pay in enumerate(pays):
        pay[0, :, :DI] = state_s[quarter(quad_ref, k), :]
        pay[0, :, DI:] = growths


def quarter(quad_ref, k):
    return pl.ds(pl.multiple_of(quad_ref[k] * NQ, NQ), NQ)


def pass_kernel(backward, final, quad_ref, *refs):
    slots, grows, refs = refs[:QUAD], refs[QUAD : 2 * QUAD], refs[2 * QUAD :]
    begin, _, *outs, pieces, growths, made = refs
    count = begin.shape[0]
    for k in range(QUAD):
        pieces[quad_ref[k]] = slots[k][:, :, :DI]
        growths[quad_ref[k]] = grows[k][...]
    spread = heads_to_lanes()
    order = list(range(QUAD))[:: -1 if backward else 1]
    for r in range(count):
        high = jnp.concatenate([growths[j, r, 0:1, :] for j in range(QUAD)], axis=0)
        low = jnp.concatenate([growths[j, r, 1:2, :] for j in range(QUAD)], axis=0)
        grow = dot(high, spread) + dot(low, spread)
        state = begin[r].astype(F32) if final else jnp.zeros((NQ, DI), F32)
        for j in order:
            if final:
                made[j, r] = state.astype(BF16)
            state = grow[j : j + 1] * state + pieces[j, r].astype(F32)
        if not final:
            outs[0][r] = state.astype(BF16)
    if final:
        for k in range(QUAD):
            outs[k][...] = made[quad_ref[k]]


def inside_kernel(act, step, cum, conv, par, intra, dsilu, xdt_s, ext):
    for t in range(CONV // LANES):
        cols = slice(t * LANES, (t + 1) * LANES)
        ext[...] = conv[0, :, cols].astype(F32)
        total = par[4:5, cols]
        for k in range(KW):
            total = total + par[k : k + 1, cols] * ext[pl.ds(HALO - KW + 1 + k, PIECE), :]
        gate = jax.nn.sigmoid(total)
        dsilu[0, :, cols] = gate * (1.0 + total * (1.0 - gate))
    spread = heads_to_lanes()
    size, cumul = step[0], cum[0]
    for t in range(DI // 256):
        cols = slice(t * 256, (t + 1) * 256)
        xdt_s[:, cols] = (expand(size, spread[:, cols]) * act[0, :, cols].astype(F32)).astype(BF16)
    bmat, cmat = act[0, :, DI : DI + N], act[0, :, DI + N :]
    scores = dot_nt(cmat, bmat)
    lower = triangle(PIECE, True)
    turned = cumul.T
    left = lax.broadcasted_iota(jnp.int32, (PIECE, LANES), 1) < HP
    for pair in range(H // 2):
        cols = slice(pair * LANES, (pair + 1) * LANES)
        xdt = xdt_s[:, cols]
        both = []
        for h in (2 * pair, 2 * pair + 1):
            differ = cumul[:, h : h + 1] - turned[h : h + 1, :]
            mix = (scores * jnp.exp(jnp.where(lower, differ, -1e30))).astype(BF16)
            both.append(dot(mix, xdt))
        intra[0, :, cols] = jnp.where(left, both[0], both[1])


def gate_kernel(rows_in, core_ref, hid, cot, *refs):
    mine, recv = refs[:GROUPS], refs[GROUPS : 2 * GROUPS]
    gate, dnorm, wg, wo, weight, all_s, wide_s, wo_s = refs[4 * GROUPS :]
    assemble(core_ref[0], refs[2 * GROUPS : 3 * GROUPS], refs[3 * GROUPS : 4 * GROUPS], weight, SPANS)
    assemble(core_ref[0], mine, recv, all_s, [slice(g * RWIDTH, (g + 1) * RWIDTH) for g in range(GROUPS)])
    wg[...] = all_s[:, :DI]
    wide_s[...] = all_s[:, DI:].astype(F32)
    for d in range(D // rows_in):
        for half in range(2):
            start = (2 * d + half) * rows_in
            wo_s[start : start + rows_in] = wide_s[d * rows_in : (d + 1) * rows_in, half * D : (half + 1) * D]
    wo[...] = wo_s[...].astype(BF16)
    for r in range(hid.shape[0]):
        gate[r] = dot(hid[r], wg[...]).astype(BF16)
        dnorm[r] = dot_nt(cot[r], wo[...])


def middle_kernel(
    quad_ref, s0, s1, s2, s3, act, intra, cum, gate, dnorm, par, heads,
    normed, dgate, dy, reach, p0, p1, p2, p3, sums, st, off_s, grow_s, high_s, low_s, doff_s, sum_s, state_s
):
    spread = heads_to_lanes()
    for k, slot in enumerate((s0, s1, s2, s3)):
        state_s[quarter(quad_ref, k), :] = slot[0]
    state = state_s[...]
    st[0] = state
    cmat = act[0, :, DI + N :]
    off_s[...] = dot(cmat, state)
    grow_s[...] = expand(jnp.exp(cum[0]), spread)
    skip = expand(jnp.broadcast_to(heads[2:3], (8, LANES)), spread)[0:1]
    gain = par[6:7, :DI]
    sum_s[...] = jnp.zeros_like(sum_s)
    size = 16

    def chunk(i, carry):
        at = pl.ds(pl.multiple_of(i * size, size), size)
        value = act[0, at, :DI].astype(F32)
        grow = grow_s[at, :]
        base = intra[0, at, :] + grow * off_s[at, :]
        ssd = base + skip * value
        z = gate[0, at, :].astype(F32)
        sig = jax.nn.sigmoid(z)
        silu = z * sig
        gated = ssd * silu
        scale = lax.rsqrt(jnp.mean(gated * gated, axis=-1, keepdims=True) + EPS)
        unit = gated * scale
        normed[0, at, :] = (unit * gain).astype(BF16)
        d_normed = dnorm[0, at, :]
        sum_s[0:8] += (d_normed * unit).reshape(size // 8, 8, DI).sum(axis=0)
        d_unit = d_normed * gain
        along = jnp.mean(d_unit * unit, axis=-1, keepdims=True)
        d_gated = scale * (d_unit - unit * along)
        dgate[0, at, :] = (d_gated * ssd * (sig * (1.0 + z * (1.0 - sig)))).astype(BF16)
        d_ssd = (d_gated * silu).astype(BF16)
        dy[0, at, :] = d_ssd
        d_ssd = d_ssd.astype(F32)
        doff_s[at, :] = (grow * d_ssd).astype(BF16)
        sum_s[8:16] += (d_ssd * value).reshape(size // 8, 8, DI).sum(axis=0)
        high, low = split(d_ssd * base)
        high_s[at, :] = high
        low_s[at, :] = low
        return carry

    lax.fori_loop(0, PIECE // size, chunk, 0, unroll=True)
    state_s[...] = dot_tn(cmat, doff_s[...]).astype(BF16)
    for k, slot in enumerate((p0, p1, p2, p3)):
        slot[0] = state_s[quarter(quad_ref, k), :]
    reach[0] = collect(high_s[...], low_s[...], spread)
    high, low = split(sum_s[8:16])
    sums[0, 0:8] = sum_s[0:8]
    sums[0, 8:16, :LANES] = collect(high, low, spread)
    sums[0, 8:16, LANES:] = jnp.zeros((8, DI - LANES), F32)


def outer_kernel(rows_in, core_ref, cot, hid, normed, dgate, _, keep, send, total, sums):
    core = core_ref[0]
    count = cot.shape[0]
    tangent = cot[...].reshape(count * PIECE, D)
    hidden = hid[...].reshape(count * PIECE, D)
    total[...] = dot_tn(normed[...].reshape(count * PIECE, DI), tangent)
    for half in range(2):
        cols = slice(half * D, (half + 1) * D)
        sums[:, cols] = dot_tn(hidden, dgate[:, :, cols].reshape(count * PIECE, D))
    for d in range(D // rows_in):
        for half in range(2):
            start = (2 * d + half) * rows_in
            sums[d * rows_in : (d + 1) * rows_in, DI + half * D : DI + (half + 1) * D] = total[start : start + rows_in]
    blocks, rows, _ = keep.shape
    for y in range(blocks):
        mine = pl.multiple_of((2 * y + core) * rows, 16)
        other = pl.multiple_of((2 * y + 1 - core) * rows, 16)
        keep[y] = sums[pl.ds(mine, rows)]
        send[y] = sums[pl.ds(other, rows)].astype(BF16)


def join_kernel(cuts, axes, bit_ref, small, other, _, *refs):
    count = 1 + max(operand for group in cuts for operand, _, _ in group)
    keeps, recvs = refs[:count], refs[count : 2 * count]
    outs, sends = refs[2 * count : 2 * count + GROUPS], refs[2 * count + GROUPS : 2 * count + 2 * GROUPS]
    refs[-1][...] = small[...] + other[...]
    for g, group in enumerate(cuts):
        bit, axis = bit_ref[g], axes[g]
        base = 0
        for operand, start, width in group:
            keep, recv = keeps[operand], recvs[operand]
            source, target = slice(start, start + width), slice(base, base + width)
            for place in itertools.product(range(2), repeat=keep.ndim - 3):
                mine = place[:axis] + (bit,) + place[axis:] + (slice(None), source)
                away = place[:axis] + (1 - bit,) + place[axis:] + (slice(None), source)
                here = place + (slice(None), target)
                outs[g][here] = keep[mine] + recv[mine].astype(F32)
                sends[g][here] = (keep[away] + recv[away].astype(F32)).astype(BF16)
            base += width


def last_kernel(small, other, w_in, gain, *refs):
    keeps, recvs = refs[:GROUPS], refs[GROUPS : 2 * GROUPS]
    small_out, g_win, g_wout, g_gin = refs[2 * GROUPS :]
    small_out[...] = small[...] + other[...]
    rows, width = g_win.shape
    for g in range(GROUPS):
        total = keeps[g][...] + recvs[g][...].astype(F32)
        start = DI + SPANS[g].start
        stop = min(start + WIDTHS[g], width)
        g_win[:, start:stop] = total[:, : stop - start]
        first = g * RWIDTH
        for lo, hi, ref, row in ((0, DI, g_win, 0), (DI, DI + D, g_wout, 0), (DI + D, REST, g_wout, rows)):
            a, b = max(lo, first), min(hi, first + RWIDTH)
            if a < b:
                at = WIDTHS[g] + a - first
                ref[row : row + rows, a - lo : b - lo] = total[:, at : at + b - a]
    g_gin[...] = jnp.sum(g_win[...] * w_in[...].astype(F32), axis=-1, keepdims=True) / gain[...].astype(F32)


def result_kernel(tok, normed, wo, _, out):
    out[0] = (tok[0].astype(F32) + dot(normed[0], wo[...])).astype(BF16)


def pair_kernel(act, step, cum, dy, st, u, dcm, dbm, xdt_s, doff_s, dsc_s):
    spread = heads_to_lanes()
    size, cumul = step[0], cum[0]
    grown = jnp.exp(cumul)
    for t in range(DI // 256):
        cols = slice(t * 256, (t + 1) * 256)
        xdt_s[:, cols] = (expand(size, spread[:, cols]) * act[0, :, cols].astype(F32)).astype(BF16)
        doff_s[:, cols] = (expand(grown, spread[:, cols]) * dy[0, :, cols].astype(F32)).astype(BF16)
    bmat, cmat = act[0, :, DI : DI + N], act[0, :, DI + N :]
    scores = dot_nt(cmat, bmat)
    lower = triangle(PIECE, True)
    turned = cumul.T
    dsc_s[...] = jnp.zeros_like(dsc_s)
    left = lax.broadcasted_iota(jnp.int32, (PIECE, LANES), 1) < HP
    zero = jnp.zeros((PIECE, LANES), BF16)
    for pair in range(H // 2):
        cols = slice(pair * LANES, (pair + 1) * LANES)
        xdt = xdt_s[:, cols]
        slope = dy[0, :, cols]
        slope_t = slope.astype(F32).T.astype(BF16)
        both = []
        for side in (0, 1):
            h = 2 * pair + side
            differ = cumul[:, h : h + 1] - turned[h : h + 1, :]
            decay = jnp.exp(jnp.where(lower, differ, -1e30))
            mix = (scores * decay).astype(BF16)
            own = jnp.where(left, slope, zero) if side == 0 else jnp.where(left, zero, slope)
            dsc_s[...] += dot_nt(own, xdt) * decay
            both.append(dot(slope_t[side * HP : (side + 1) * HP], mix))
        u[0, :, cols] = jnp.concatenate(both, axis=0).T
    d_scores = dsc_s[...].astype(BF16)
    dcm[0] = dot_nt(doff_s[...], st[0]) + dot(d_scores, bmat)
    dbm[0] = dot_tn(d_scores, cmat)


def back_kernel(
    quad_ref, l0, l1, l2, l3, st, act, cum, step, raw, u, dcm, dbm, dy, dsilu, reach, heads, _,
    dpre, edge, draw, hsum, dw_s, far_s, size_s, high_s, low_s, wts_s, sum_s, state_s
):
    spread = heads_to_lanes()
    size, cumul = step[0], cum[0]
    last = cumul[PIECE - 1 :]
    for k, slot in enumerate((l0, l1, l2, l3)):
        state_s[quarter(quad_ref, k), :] = slot[0]
    d_local = state_s[...]
    bmat = act[0, :, DI : DI + N]
    dw_s[...] = dot(bmat, d_local)
    far_s[...] = expand(jnp.exp(last - cumul), spread)
    size_s[...] = expand(size, spread)
    skip = expand(jnp.broadcast_to(heads[2:3], (8, LANES)), spread)[0:1]
    sum_s[...] = jnp.zeros_like(sum_s)
    rows = 16

    def chunk(i, carry):
        at = pl.ds(pl.multiple_of(i * rows, rows), rows)
        value = act[0, at, :DI].astype(F32)
        far, long = far_s[at, :], size_s[at, :]
        through = far * dw_s[at, :]
        d_xdt = u[0, at, :] + through
        d_value = long * d_xdt + skip * dy[0, at, :].astype(F32)
        dpre[0, at, :DI] = d_value * dsilu[0, at, :DI]
        high, low = split(value * d_xdt)
        high_s[at, :] = high
        low_s[at, :] = low
        xdt = long * value
        wts_s[at, :] = (far * xdt).astype(BF16)
        sum_s[0:8] += (xdt * through).reshape(rows // 8, 8, DI).sum(axis=0)
        return carry

    lax.fori_loop(0, PIECE // rows, chunk, 0, unroll=True)
    for j in range(N // 16):
        prod = state_s[j * 16 : (j + 1) * 16, :].astype(F32) * st[0, j * 16 : (j + 1) * 16, :].astype(F32)
        sum_s[8:16] += prod.reshape(2, 8, DI).sum(axis=0)
    d_bmat = dbm[0] + dot_nt(wts_s[...], d_local)
    dpre[0, :, DI : DI + N] = d_bmat * dsilu[0, :, DI : DI + N]
    dpre[0, :, DI + N :] = dcm[0] * dsilu[0, :, DI + N :]
    edge[0] = dpre[0, 0:8, :]
    q = collect(high_s[...], low_s[...], spread)
    high, low = split(sum_s[...])
    sums = collect(high, low, spread)
    d_last = jnp.sum(sums[0:8], axis=0, keepdims=True)
    d_last = d_last + jnp.exp(last) * jnp.sum(sums[8:16], axis=0, keepdims=True)
    d_cum = reach[0] - size * q
    row = lax.broadcasted_iota(jnp.int32, (PIECE, LANES), 0)
    d_cum = d_cum + jnp.where(row == PIECE - 1, d_last, 0.0)
    d_rate = running(triangle(PIECE, False), d_cum)
    decay = jnp.exp(heads[1:2])
    d_size = q - d_rate * decay
    d_raw = d_size * jax.nn.sigmoid(raw[0] + heads[0:1])
    draw[0] = d_raw
    for_bias = jnp.sum(d_raw, axis=0, keepdims=True)
    for_log = -jnp.sum(d_rate * size, axis=0, keepdims=True) * decay
    pick = lax.broadcasted_iota(jnp.int32, (8, LANES), 0)
    hsum[0] = jnp.where(pick == 0, for_bias, jnp.where(pick == 1, for_log, 0.0))


def input_kernel(core_ref, dpre, edge, draw, hid, par, gone, dproj, small, *refs):
    keeps, sends = refs[:GROUPS], refs[GROUPS : 2 * GROUPS]
    ext, *totals = refs[2 * GROUPS :]
    small[...] = gone[...]
    core = core_ref[0]
    count = dpre.shape[0]
    for r in range(count):
        ext[:PIECE] = dpre[r]
        ext[PIECE:] = edge[r]
        for t in range(CONV // LANES):
            cols = slice(t * LANES, (t + 1) * LANES)
            sum_k = par[KW - 1 : KW, cols] * ext[0:PIECE, cols]
            for k in range(KW - 1):
                sum_k = sum_k + par[k : k + 1, cols] * ext[pl.ds(KW - 1 - k, PIECE), cols]
            dproj[r, :, cols] = sum_k.astype(BF16)
        dproj[r, :, CONV:] = draw[r].astype(BF16)
    hidden = hid[...].reshape(count * PIECE, D)
    for keep, send, total, cols in zip(keeps, sends, totals, SPANS):
        total[...] = dot_tn(hidden, dproj[:, :, cols].reshape(count * PIECE, cols.stop - cols.start))
        blocks, rows, _ = keep.shape
        for y in range(blocks):
            mine = pl.multiple_of((2 * y + core) * rows, 16)
            other = pl.multiple_of((2 * y + 1 - core) * rows, 16)
            keep[y] = total[pl.ds(mine, rows)]
            send[y] = total[pl.ds(other, rows)].astype(BF16)


def taps_kernel(dpre, conv, sums, hsum, small, ext):
    @pl.when(pl.program_id(0) == 0)
    def _():
        small[...] = jnp.zeros_like(small)

    for t in range(CONV // LANES):
        cols = slice(t * LANES, (t + 1) * LANES)
        slope = dpre[0, :, cols]
        ext[...] = conv[0, :, cols].astype(F32)
        for k in range(KW):
            prod = slope * ext[pl.ds(HALO - KW + 1 + k, PIECE), :]
            small[k : k + 1, cols] += jnp.sum(prod, axis=0, keepdims=True)
        small[4:5, cols] += jnp.sum(slope, axis=0, keepdims=True)
    small[6:7, :DI] += jnp.sum(sums[0, 0:8], axis=0, keepdims=True)
    small[7:8, 0:LANES] += hsum[0, 0:1]
    small[7:8, LANES : 2 * LANES] += hsum[0, 1:2]
    small[7:8, 2 * LANES : 3 * LANES] += jnp.sum(sums[0, 8:16, :LANES], axis=0, keepdims=True)


def slope_kernel(dgate, wg, _, dh):
    dh[0] = dot_nt(dgate[0], wg[...])


def token_kernel(tok, cot, dh, dproj, weight, par, _, grad, dh_s):
    dh_s[...] = dh[0] + dot_nt(dproj[0], weight[...])
    gain = par[5:6, :D]
    rows = 32

    def chunk(i, carry):
        at = pl.ds(pl.multiple_of(i * rows, rows), rows)
        x = tok[0, at, :].astype(F32)
        scale = lax.rsqrt(jnp.mean(x * x, axis=-1, keepdims=True) + EPS)
        unit = x * scale
        d_unit = dh_s[at, :] * gain
        along = jnp.mean(d_unit * unit, axis=-1, keepdims=True)
        grad[0, at, :] = (cot[0, at, :].astype(F32) + scale * (d_unit - unit * along)).astype(BF16)
        return carry

    lax.fori_loop(0, PIECE // rows, chunk, 0, unroll=True)


def local(size, tokens, cotangent, norm_in, w_in, conv_w, conv_b, dt_bias, a_log, skip, norm_out, w_out):
    devices, along = size
    bits = int(math.log2(devices))
    core_bit = int(math.log2(along))
    me = lax.axis_index(AX)
    core = ((me >> core_bit) & 1).astype(jnp.int32)
    core_arg = core.reshape(1)
    high_bits = list(range(bits - 1, core_bit, -1))
    far_bits = list(range(core_bit - 1, -1, -1))
    dims = [far_bits[-1:], far_bits[:-1], high_bits] if core_bit == 3 else [far_bits[-3:], far_bits[:-3], high_bits]
    orders = [dims[1] + dims[2] + dims[0], dims[0] + dims[1] + dims[2], dims[2] + dims[0] + dims[1]]
    if [len(dim) for dim in dims] == [1, 2, 1]:
        x, (top, low), y = dims[0][0], dims[1], dims[2][0]
        orders = [[top, low, y, x], [top, x, low, y], [top, y, x, low]]

    def swap(x, bit):
        return lax.ppermute(x, AX, [(i, i ^ (1 << bit)) for i in range(devices)])

    def bit_of(bit):
        return (me >> bit) & 1

    def after(x, other):
        rows, cols = min(x.shape[-2], other.shape[-2], 8), min(x.shape[-1], other.shape[-1])
        part = other[(0,) * (other.ndim - 2)][:rows, :cols].astype(x.dtype)
        return x + 0 * jnp.pad(part, ((0, x.shape[-2] - rows), (0, x.shape[-1] - cols)))

    def gather(x, order, have):
        for bit in order:
            if order is lead and len(have) == HALO_TURN:
                x = after(x, halo)
            other = swap(x, bit)
            have = sorted(have + [bit], reverse=True)
            mine = bit_of(bit) == 0
            low, high = jnp.where(mine, x, other), jnp.where(mine, other, x)
            x = jnp.stack([low, high], axis=have.index(bit))
        return x, have

    micro, batch, count = tokens.shape[:3]
    tok = tokens.reshape(micro * batch, count, D)
    cot = cotangent.reshape(micro * batch, count, D)
    R = micro * batch
    heads = jnp.zeros((8, LANES), F32)
    for i, a in enumerate((dt_bias, a_log, skip)):
        heads = heads.at[i, :H].set(a)

    own_conv, own_in, own_out = conv_b.shape[0], norm_in.shape[0], norm_out.shape[0]
    owned_by = ((own_conv, tuple(range(KW + 1))), (own_in, (KW + 1,)), (own_out, (KW + 2,)))

    halo = lax.ppermute(tok[:, count - HALO :], "near", [(i, i + 1) for i in range(NEAR - 1)])
    rows_in = w_in.shape[0]
    kinds = jnp.concatenate(
        [
            conv_w.T,
            conv_b[None],
            jnp.pad(norm_in, (0, own_conv - own_in))[None],
            jnp.pad(norm_out, (0, own_conv - own_out))[None],
        ],
        axis=0,
    )
    turns = -(-kinds.shape[0] // rows_in)
    kinds = jnp.pad(kinds, ((0, turns * rows_in - kinds.shape[0]), (0, 0)))
    kinds = jnp.concatenate([kinds[t * rows_in : (t + 1) * rows_in] for t in range(turns)], axis=1)
    spare = PC - (w_in.shape[1] - DI)
    kinds = jnp.pad(kinds, ((0, 0), (0, spare - kinds.shape[1])))
    first = jnp.concatenate([w_in[:, DI:], kinds], axis=1)
    blocks = devices // (2 * along)
    rest = jnp.concatenate([w_in[:, :DI], w_out[:rows_in], w_out[rows_in:]], axis=1)
    lead = orders[0][:SPLIT_TURN]
    groups = []
    for g in range(GROUPS):
        both = jnp.concatenate([first[:, SPANS[g]], rest[:, g * RWIDTH : (g + 1) * RWIDTH]], axis=1)
        groups.append(gather(both, lead if g == 0 else orders[g][:SPLIT_TURN], []))
    halves = [(blocks, along * rows_in, width) for width in WIDTHS]
    mine = [
        gather(x[..., : WIDTHS[g]], orders[g][SPLIT_TURN:], have)[0].reshape(halves[g])
        for g, (x, have) in enumerate(groups)
    ]
    recv = [swap(x, core_bit) for x in mine]
    rest_half = (blocks, along * rows_in, RWIDTH)
    rest_mine = [
        gather(after(x[..., WIDTHS[g] :], mine[g]), orders[g][SPLIT_TURN:], have)[0].reshape(rest_half)
        for g, (x, have) in enumerate(groups)
    ]

    smem = pl.BlockSpec(memory_space=pltpu.SMEM)
    anywhere = pl.BlockSpec(memory_space=pl.ANY)
    inside = pl.BlockSpec(memory_space=pltpu.VMEM)
    halves = [(blocks, along * rows_in, width) for width in WIDTHS]
    par_spec, head_spec = whole((8, CONV)), whole((8, LANES))
    row_d, row_i, row_c = per_row((PIECE, D)), per_row((PIECE, DI)), per_row((PIECE, CONV))
    row_l = per_row((PIECE, LANES))
    slot, slot_wide, whole_state = per_row((NQ, DI)), per_row((NQ, DI + LANES)), per_row((N, DI))
    quad = lax.axis_index("near") % QUAD
    quad_arg = jnp.stack([quad ^ k for k in range(QUAD)]).astype(jnp.int32)
    hid, conv, raw, act, step, cum, *pays, par = pl.pallas_call(
        functools.partial(enter_kernel, owned_by),
        grid=(R,),
        in_specs=[smem, smem, row_d, per_row((HALO, D)), head_spec] + [whole(half) for half in halves] * 2,
        out_specs=[
            row_d, per_row((HALO + PIECE, CONV)), row_l, row_c, row_l, row_l,
            *[slot_wide] * QUAD,
            par_spec,
        ],
        out_shape=[
            struct((R, PIECE, D), BF16), struct((R, HALO + PIECE, CONV), BF16), struct((R, PIECE, LANES), F32),
            struct((R, PIECE, CONV), BF16), struct((R, PIECE, LANES), F32),
            struct((R, PIECE, LANES), F32), *[struct((R, NQ, DI + LANES), BF16)] * QUAD,
            struct((8, CONV), F32),
        ],
        scratch_shapes=[
            pltpu.VMEM((HALO + PIECE, CONV), F32), pltpu.VMEM((N, DI), BF16), pltpu.VMEM((D, PC), BF16),
        ],
        compiler_params=params(60),
        cost_estimate=cost(R * 2e9, 2e7),
        name="enter",
    )(core_arg, quad_arg, tok, halo, heads, *mine, *recv)

    def exchange(slots):
        return slots[:1] + [
            lax.ppermute(slots[k], "near", [(i, i ^ k) for i in range(NEAR)]) for k in range(1, QUAD)
        ]

    def hold(x, ready):
        return pl.pallas_call(
            lambda *_: None,
            in_specs=[anywhere, anywhere],
            out_specs=anywhere,
            out_shape=struct(x.shape, x.dtype),
            input_output_aliases={0: 0},
            name="hold",
        )(x, ready)

    def carry_on(slots, grows, backward, begin, ready):
        final = begin is not None
        width = slots[0].shape[-1]
        shape, kind = (R, NQ, DI), BF16
        outs = QUAD if final else 1
        return pl.pallas_call(
            functools.partial(pass_kernel, backward, final),
            grid=(1,),
            in_specs=[smem] + [whole((R, NQ, width))] * QUAD
            + [pl.BlockSpec((R, NQ, LANES), lambda r: (0, 0, DI // LANES))] * QUAD
            + [whole(shape) if final else anywhere, anywhere],
            out_specs=[whole(shape)] * outs,
            out_shape=[struct(shape, kind)] * outs,
            scratch_shapes=[
                pltpu.VMEM((QUAD, *shape), kind), pltpu.VMEM((QUAD, R, NQ, LANES), kind),
                pltpu.VMEM((QUAD, *shape), kind),
            ],
            compiler_params=params(60),
            cost_estimate=cost(1e7, 2e6),
            name="carry" if final else "total",
        )(quad_arg, *slots, *grows, begin if final else ready, ready)

    def crossing(total, backward):
        pairs = [(i + QUAD, i) if backward else (i, i + QUAD) for i in range(QUAD)]
        return lax.ppermute(total, "near", pairs)

    pieces = exchange(list(pays))
    intra, dsilu = pl.pallas_call(
        inside_kernel,
        grid=(R,),
        in_specs=[row_c, row_l, row_l, per_row((HALO + PIECE, CONV)), par_spec],
        out_specs=[row_i, row_c],
        out_shape=[struct((R, PIECE, DI), F32), struct((R, PIECE, CONV), F32)],
        scratch_shapes=[pltpu.VMEM((PIECE, DI), BF16), pltpu.VMEM((HALO + PIECE, LANES), F32)],
        compiler_params=params(60),
        cost_estimate=cost(R * 4e9, 5e6),
        name="inside",
    )(act, step, cum, conv, par)
    rest_other = [swap(x, core_bit) for x in rest_mine]
    gate, dnorm, wg, wo, weight = pl.pallas_call(
        functools.partial(gate_kernel, rows_in),
        in_specs=[smem] + [inside] * (2 + 4 * GROUPS),
        out_specs=[inside] * 5,
        out_shape=[
            struct((R, PIECE, DI), BF16), struct((R, PIECE, DI), F32), struct((D, DI), BF16), struct((DI, D), BF16),
            struct((D, PC), BF16),
        ],
        scratch_shapes=[pltpu.VMEM((D, REST), BF16), pltpu.VMEM((D, 2 * D), F32), pltpu.VMEM((DI, D), F32)],
        compiler_params=params(60),
        cost_estimate=cost(R * 2e9, 1e7),
        name="gates",
    )(core_arg, hid, cot, *rest_mine, *rest_other, *mine, *recv)
    total = carry_on(pieces, pieces, False, None, intra)[0]
    st = exchange(list(carry_on(pieces, pieces, False, crossing(total, False), gate)))

    wide = pltpu.VMEM((PIECE, DI), F32)
    slim = pltpu.VMEM((PIECE, DI), BF16)
    normed, dgate, dy, reach, b0, b1, b2, b3, sums, state = pl.pallas_call(
        middle_kernel,
        grid=(R,),
        in_specs=[smem, *[slot] * QUAD, row_c, row_i, row_l, row_i, row_i, par_spec, head_spec],
        out_specs=[row_i, row_i, row_i, row_l, *[slot] * QUAD, per_row((16, DI)), whole_state],
        out_shape=[
            struct((R, PIECE, DI), BF16), struct((R, PIECE, DI), BF16), struct((R, PIECE, DI), BF16),
            struct((R, PIECE, LANES), F32), *[struct((R, NQ, DI), BF16)] * QUAD, struct((R, 16, DI), F32),
            struct((R, N, DI), BF16),
        ],
        scratch_shapes=[wide, wide, slim, slim, slim, pltpu.VMEM((16, DI), F32), pltpu.VMEM((N, DI), BF16)],
        compiler_params=params(60),
        cost_estimate=cost(R * 2e9, 1.5e7),
        name="middle",
    )(quad_arg, *st, act, intra, cum, gate, dnorm, par, heads)

    pieces_b = exchange([b0, b1, b2, b3])
    rows_out = w_out.shape[0]
    u, dcm, dbm = pl.pallas_call(
        pair_kernel,
        grid=(R,),
        in_specs=[row_c, row_l, row_l, row_i, whole_state],
        out_specs=[row_i, row_l, row_l],
        out_shape=[struct((R, PIECE, DI), F32), struct((R, PIECE, N), F32), struct((R, PIECE, N), F32)],
        scratch_shapes=[slim, slim, pltpu.VMEM((PIECE, PIECE), F32)],
        compiler_params=params(60),
        cost_estimate=cost(R * 8e9, 1e7),
        name="pair",
    )(act, step, cum, dy, state)
    total = carry_on(pieces_b, pieces, True, None, u)[0]
    rest_shape = (blocks, along * rows_in, REST)
    rest_keep, rest_send = pl.pallas_call(
        functools.partial(outer_kernel, rows_in),
        in_specs=[smem] + [inside] * 4 + [anywhere],
        out_specs=[inside] * 2,
        out_shape=[struct(rest_shape, F32), struct(rest_shape, BF16)],
        scratch_shapes=[pltpu.VMEM((DI, D), F32), pltpu.VMEM((D, REST), F32)],
        compiler_params=params(60),
        cost_estimate=cost(6e9, 2e7),
        name="outer",
    )(core_arg, cot, hid, normed, dgate, pieces_b[0])
    carried = carry_on(pieces_b, pieces, True, crossing(total, True), rest_keep)
    rest_recv = swap(hold(rest_send, carried[0]), core_bit)
    later = exchange(list(carried))

    dpre, edge, draw, hsum = pl.pallas_call(
        back_kernel,
        grid=(R,),
        in_specs=[
            smem, *[slot] * QUAD, whole_state,
            row_c, row_l, row_l, row_l, row_i, row_l, row_l, row_i, row_c, row_l, head_spec, anywhere,
        ],
        out_specs=[row_c, per_row((8, CONV)), row_l, per_row((8, LANES))],
        out_shape=[
            struct((R, PIECE, CONV), F32), struct((R, 8, CONV), F32),
            struct((R, PIECE, LANES), F32), struct((R, 8, LANES), F32),
        ],
        scratch_shapes=[wide, wide, wide, slim, slim, slim, pltpu.VMEM((16, DI), F32), pltpu.VMEM((N, DI), BF16)],
        compiler_params=params(60),
        cost_estimate=cost(R * 2e9, 1.5e7),
        name="back",
    )(quad_arg, *later, state, act, cum, step, raw, u, dcm, dbm, dy, dsilu, reach, heads, rest_keep)
    edge = lax.ppermute(edge, "near", [(i + 1, i) for i in range(NEAR - 1)])

    small = pl.pallas_call(
        taps_kernel,
        grid=(R,),
        in_specs=[row_c, per_row((HALO + PIECE, CONV)), per_row((16, DI)), per_row((8, LANES))],
        out_specs=whole((8, CONV)),
        out_shape=struct((8, CONV), F32),
        scratch_shapes=[pltpu.VMEM((HALO + PIECE, LANES), F32)],
        compiler_params=params(60),
        cost_estimate=cost(2e7, 6e6),
        name="taps",
    )(dpre, conv, sums, hsum)

    dproj, small, *parts = pl.pallas_call(
        input_kernel,
        in_specs=[smem] + [inside] * 6,
        out_specs=[inside] * (2 + 2 * GROUPS),
        out_shape=[struct((R, PIECE, PC), BF16), struct((8, CONV), F32)]
        + [pltpu.VMEM(half, F32) for half in halves] + [pltpu.VMEM(half, BF16) for half in halves],
        scratch_shapes=[pltpu.VMEM((PIECE + 8, CONV), F32), *(pltpu.VMEM((D, width), F32) for width in WIDTHS)],
        compiler_params=params(44),
        cost_estimate=cost(2e9, 1e7),
        name="input",
    )(core_arg, dpre, edge, draw, hid, par, small)

    def by_bits(x):
        count = x.size // (rows_in * x.shape[-1])
        return x.reshape((2,) * int(math.log2(count)) + (rows_in, x.shape[-1]))

    have = [sorted(order, reverse=True) for order in orders]
    cuts = [[(g, 0, WIDTHS[g]), (GROUPS, g * RWIDTH, RWIDTH)] for g in range(GROUPS)]
    keeps = parts[:GROUPS] + [rest_keep]
    recvs = [swap(x, core_bit) for x in parts[GROUPS:]] + [rest_recv]
    other = swap(small, core_bit)
    ahead = small
    for turn in range(bits - 1):
        now = [order[::-1][turn] for order in orders]
        axes = [have[g].index(now[g]) for g in range(GROUPS)]
        shapes = [(2,) * (bits - 2 - turn) + (rows_in, WIDTHS[g] + RWIDTH) for g in range(GROUPS)]
        *made, small = pl.pallas_call(
            functools.partial(join_kernel, cuts, axes),
            in_specs=[smem, inside, inside, anywhere] + [inside] * (2 * len(keeps)),
            out_specs=[inside] * (2 * GROUPS + 1),
            out_shape=[pltpu.VMEM(shape, F32) for shape in shapes]
            + [pltpu.VMEM(shape, BF16) for shape in shapes] + [pltpu.VMEM((8, CONV), F32)],
            compiler_params=params(40),
            cost_estimate=cost(1e6, 8e6),
            name="join",
        )(
            jnp.stack([bit_of(bit) for bit in now]).astype(jnp.int32),
            small, other, ahead, *map(by_bits, keeps), *map(by_bits, recvs),
        )
        if turn == 1:
            ahead = block_out = pl.pallas_call(
                result_kernel,
                grid=(R,),
                in_specs=[row_d, row_i, whole((DI, D)), anywhere],
                out_specs=row_d,
                out_shape=struct((R, PIECE, D), BF16),
                compiler_params=params(32),
                cost_estimate=cost(R * 6e8, 6e6),
                name="result",
            )(tok, normed, wo, small)
        if turn == 0:
            dh = pl.pallas_call(
                slope_kernel,
                grid=(R,),
                in_specs=[row_i, whole((D, DI)), anywhere],
                out_specs=row_d,
                out_shape=struct((R, PIECE, D), F32),
                compiler_params=params(32),
                cost_estimate=cost(R * 6e8, 6e6),
                name="slope",
            )(dgate, wg, small)
            grad_tokens = pl.pallas_call(
                token_kernel,
                grid=(R,),
                in_specs=[row_d, row_d, row_d, per_row((PIECE, PC)), whole((D, PC)), par_spec, anywhere],
                out_specs=row_d,
                out_shape=struct((R, PIECE, D), BF16),
                scratch_shapes=[pltpu.VMEM((PIECE, D), F32)],
                compiler_params=params(32),
                cost_estimate=cost(R * 2e9, 1.5e7),
                name="token",
            )(tok, cot, dh, dproj, weight, par, small)
            ahead = grad_tokens
        for g in range(GROUPS):
            have[g].remove(now[g])
        cuts = [[(g, 0, WIDTHS[g] + RWIDTH)] for g in range(GROUPS)]
        keeps = made[:GROUPS]
        recvs = [swap(x, now[g]) for g, x in enumerate(made[GROUPS:])]
        other = swap(small, orders[0][::-1][turn])
    flat = [x.reshape(rows_in, x.shape[-1]) for x in keeps + recvs]
    small, g_win, g_wout, g_gin = pl.pallas_call(
        last_kernel,
        in_specs=[inside] * (4 + 2 * GROUPS),
        out_specs=[inside] * 4,
        out_shape=[
            struct((8, CONV), F32), struct(w_in.shape, F32), struct(w_out.shape, F32), struct((rows_in, 1), F32),
        ],
        compiler_params=params(32),
        cost_estimate=cost(1e6, 1e6),
        name="last",
    )(small, other, w_in, norm_in[:, None], *flat)
    g_gin = g_gin[:, 0]
    taps = lax.dynamic_slice(small, (0, me * own_conv), (5, own_conv))
    g_gout = lax.dynamic_slice(small, (6, me * own_out), (1, own_out))[0]
    return (
        block_out.reshape(tokens.shape),
        grad_tokens.reshape(tokens.shape),
        g_gin,
        g_win,
        taps[:KW].T,
        taps[KW],
        small[7, :H],
        small[7, LANES : LANES + H],
        small[7, 2 * LANES : 2 * LANES + H],
        g_gout,
        g_wout,
    )


def solution(mesh):
    dp, seq = mesh.shape["dp"], mesh.shape["seq"]
    inner = Mesh(mesh.devices.reshape(dp, seq // NEAR, NEAR), AX)
    split_seq = ("far", "near")
    act = P(None, "dp", split_seq, None)
    vec, mat = P(AX), P(AX, None)

    def run(*args):
        return local((dp * seq, seq), *args)

    return jax.shard_map(
        run,
        mesh=inner,
        in_specs=(act, act, vec, mat, mat, vec, P(), P(), P(), vec, mat),
        out_specs=(act, act, vec, mat, mat, vec, P(), P(), P(), vec, mat),
        check_vma=False,
    )
```

```python
import functools
import itertools
import math

import jax
import jax.numpy as jnp
from jax import lax
from jax.experimental import pallas as pl
from jax.experimental.pallas import tpu as pltpu
from jax.sharding import Mesh
from jax.sharding import PartitionSpec as P

H = 24
HP = 64
N = 128
KW = 4
SEQ_LEN = 2048
PIECE = 256
D = 768
DI = H * HP
CONV = DI + 2 * N
PC = 1920
WIDTHS = (640, 640, 640)
REST = DI + 2 * D
RWIDTH = REST // len(WIDTHS)
GROUPS = len(WIDTHS)
SPANS = tuple(slice(sum(WIDTHS[:g]), sum(WIDTHS[: g + 1])) for g in range(GROUPS))
NEAR = SEQ_LEN // PIECE
QUAD = NEAR // 2
NQ = N // QUAD
HALO = 16
LANES = 128
HALO_TURN = 2
SPLIT_TURN = 3
EPS = 1e-05
F32 = jnp.float32
BF16 = jnp.bfloat16
AX = ("dp", "far", "near")
MIB = 1 << 20


def dot(a, b):
    return lax.dot_general(a, b, (((1,), (0,)), ((), ())), preferred_element_type=F32)


def dot_nt(a, b):
    return lax.dot_general(a, b, (((1,), (1,)), ((), ())), preferred_element_type=F32)


def dot_tn(a, b):
    return lax.dot_general(a, b, (((0,), (0,)), ((), ())), preferred_element_type=F32)


def split(x):
    high = x.astype(BF16)
    return high, (x - high.astype(F32)).astype(BF16)


def heads_to_lanes():
    head = lax.broadcasted_iota(jnp.int32, (LANES, DI), 0)
    lane = lax.broadcasted_iota(jnp.int32, (LANES, DI), 1)
    return jnp.where((lane >> 6) == head, 1.0, 0.0).astype(BF16)


def expand(x, spread):
    high, low = split(x)
    return dot(high, spread) + dot(low, spread)


def collect(high, low, spread):
    return dot_nt(high, spread) + dot_nt(low, spread)


def triangle(count, lower):
    row = lax.broadcasted_iota(jnp.int32, (count, count), 0)
    col = lax.broadcasted_iota(jnp.int32, (count, count), 1)
    return (row >= col) if lower else (row <= col)


def running(mask, x):
    ones = jnp.where(mask, 1.0, 0.0).astype(BF16)
    high, rest = split(x)
    left = x - high.astype(F32)
    mid, low = split(left)
    return dot(ones, high) + dot(ones, mid) + dot(ones, low)


def softplus(z):
    e = jnp.exp(-jnp.abs(z))
    near = e * (1.0 + e * (-0.5 + e * (1.0 / 3.0 + e * (-0.25 + e * 0.2))))
    return jnp.maximum(z, 0.0) + jnp.where(e < 0.02, near, jnp.log(1.0 + e))


def params(limit):
    return pltpu.CompilerParams(vmem_limit_bytes=limit * MIB)


def cost(flops, nbytes, trans=0):
    return pl.CostEstimate(flops=int(flops), bytes_accessed=int(nbytes), transcendentals=int(trans))


def whole(shape):
    return pl.BlockSpec(shape, lambda *_: (0,) * len(shape))


def per_row(shape):
    return pl.BlockSpec((1,) + shape, lambda r: (r,) + (0,) * len(shape))


def struct(shape, kind):
    return jax.ShapeDtypeStruct(shape, kind)


def assemble(core, mine, recv, weight_s, spans):
    count, rows, _ = mine[0].shape
    for g, cols in enumerate(spans):
        for y in range(count):
            first = pl.multiple_of((2 * y + core) * rows, 16)
            other = pl.multiple_of((2 * y + 1 - core) * rows, 16)
            weight_s[pl.ds(first, rows), cols] = mine[g][y]
            weight_s[pl.ds(other, rows), cols] = recv[g][y]


def lay_out(weight, par, owned):
    held = weight[:, CONV:]
    rows_in = owned[1][0]
    devices = D // rows_in
    total = 1 + max(max(kinds) for _, kinds in owned)
    source = lax.broadcasted_iota(jnp.int32, (devices, D), 1)
    device = lax.broadcasted_iota(jnp.int32, (devices, D), 0)
    picks = [jnp.where(source == device * rows_in + kind % rows_in, 1.0, 0.0) for kind in range(total)]
    picked = dot(jnp.concatenate(picks, axis=0).astype(BF16), held).astype(BF16)
    for own, kinds in owned:
        width = own * devices
        lane = lax.broadcasted_iota(jnp.int32, (LANES, width), 1)
        row = lax.broadcasted_iota(jnp.int32, (LANES, width), 0)
        place = lax.broadcasted_iota(jnp.int32, (devices, width), 1)
        holder = lax.broadcasted_iota(jnp.int32, (devices, width), 0)
        mine = (place >= holder * own) & (place < holder * own + own)
        for block in sorted({kind // rows_in for kind in kinds}):
            some = [kind for kind in kinds if kind // rows_in == block]
            start = H + block * (rows_in * CONV // D)
            spread = jnp.where(row == start + lane % own, 1.0, 0.0).astype(BF16)
            values = dot(picked[some[0] * devices : (some[-1] + 1) * devices], spread)
            for i, kind in enumerate(some):
                part = jnp.where(mine, values[i * devices : (i + 1) * devices], 0.0)
                par[kind : kind + 1, :width] = jnp.sum(part, axis=0, keepdims=True)


def enter_kernel(
    owned, core_ref, quad_ref, tok, halo, heads, *refs
):
    mine, recv, rest = refs[:GROUPS], refs[GROUPS : 2 * GROUPS], refs[2 * GROUPS :]
    hid, conv, raw, act, step, cum, *pays, par, ext, state_s, weight = rest

    @pl.when(pl.program_id(0) == 0)
    def _():
        assemble(core_ref[0], mine, recv, weight, SPANS)
        par[...] = jnp.zeros_like(par)
        lay_out(weight, par, owned)

    gain = par[5:6, :D]
    rows = jnp.concatenate([halo[0], tok[0]], axis=0).astype(F32)
    scale = lax.rsqrt(jnp.mean(rows * rows, axis=-1, keepdims=True) + EPS)
    hidden = (rows * scale * gain).astype(BF16)
    hid[0] = hidden[HALO:]
    for t in range(CONV // 256):
        cols = slice(t * 256, (t + 1) * 256)
        part = dot(hidden, weight[:, cols]).astype(BF16)
        conv[0, :, cols] = part
        ext[:, cols] = part.astype(F32)
    for t in range(CONV // LANES):
        cols = slice(t * LANES, (t + 1) * LANES)
        total = par[4:5, cols]
        for k in range(KW):
            total = total + par[k : k + 1, cols] * ext[pl.ds(HALO - KW + 1 + k, PIECE), cols]
        gate = jax.nn.sigmoid(total)
        act[0, :, cols] = (total * gate).astype(BF16)
    raw_step = dot(hidden[HALO:], weight[:, CONV:]).astype(BF16).astype(F32)
    raw_step = jnp.where(lax.broadcasted_iota(jnp.int32, (PIECE, LANES), 1) < H, raw_step, 0.0)
    raw[0] = raw_step
    size = softplus(raw_step + heads[0:1])
    cumul = running(triangle(PIECE, True), size * -jnp.exp(heads[1:2]))
    step[0] = size
    cum[0] = cumul
    spread = heads_to_lanes()
    last = cumul[PIECE - 1 :]
    reach = jnp.exp(last - cumul) * size
    bmat = act[0, :, DI : DI + N]
    for t in range(DI // 256):
        cols = slice(t * 256, (t + 1) * 256)
        weights = (expand(reach, spread[:, cols]) * act[0, :, cols].astype(F32)).astype(BF16)
        state_s[:, cols] = dot_tn(bmat, weights).astype(BF16)
    growth = jnp.exp(last)
    high, low = split(growth)
    row = lax.broadcasted_iota(jnp.int32, (NQ, LANES), 0)
    growths = jnp.where(row == 0, high.astype(F32), jnp.where(row == 1, low.astype(F32), 0.0)).astype(BF16)
    for k, pay in enumerate(pays):
        pay[0, :, :DI] = state_s[quarter(quad_ref, k), :]
        pay[0, :, DI:] = growths


def quarter(quad_ref, k):
    return pl.ds(pl.multiple_of(quad_ref[k] * NQ, NQ), NQ)


def pass_kernel(backward, final, quad_ref, *refs):
    slots, grows, refs = refs[:QUAD], refs[QUAD : 2 * QUAD], refs[2 * QUAD :]
    begin, _, *outs, pieces, growths, made = refs
    count = begin.shape[0]
    for k in range(QUAD):
        pieces[quad_ref[k]] = slots[k][:, :, :DI]
        growths[quad_ref[k]] = grows[k][...]
    spread = heads_to_lanes()
    order = list(range(QUAD))[:: -1 if backward else 1]
    for r in range(count):
        high = jnp.concatenate([growths[j, r, 0:1, :] for j in range(QUAD)], axis=0)
        low = jnp.concatenate([growths[j, r, 1:2, :] for j in range(QUAD)], axis=0)
        grow = dot(high, spread) + dot(low, spread)
        state = begin[r].astype(F32) if final else jnp.zeros((NQ, DI), F32)
        for j in order:
            if final:
                made[j, r] = state.astype(BF16)
            state = grow[j : j + 1] * state + pieces[j, r].astype(F32)
        if not final:
            outs[0][r] = state.astype(BF16)
    if final:
        for k in range(QUAD):
            outs[k][...] = made[quad_ref[k]]


def inside_kernel(act, step, cum, conv, par, intra, dsilu, xdt_s, ext):
    for t in range(CONV // LANES):
        cols = slice(t * LANES, (t + 1) * LANES)
        ext[...] = conv[0, :, cols].astype(F32)
        total = par[4:5, cols]
        for k in range(KW):
            total = total + par[k : k + 1, cols] * ext[pl.ds(HALO - KW + 1 + k, PIECE), :]
        gate = jax.nn.sigmoid(total)
        dsilu[0, :, cols] = gate * (1.0 + total * (1.0 - gate))
    spread = heads_to_lanes()
    size, cumul = step[0], cum[0]
    for t in range(DI // 256):
        cols = slice(t * 256, (t + 1) * 256)
        xdt_s[:, cols] = (expand(size, spread[:, cols]) * act[0, :, cols].astype(F32)).astype(BF16)
    bmat, cmat = act[0, :, DI : DI + N], act[0, :, DI + N :]
    scores = dot_nt(cmat, bmat)
    lower = triangle(PIECE, True)
    turned = cumul.T
    left = lax.broadcasted_iota(jnp.int32, (PIECE, LANES), 1) < HP
    for pair in range(H // 2):
        cols = slice(pair * LANES, (pair + 1) * LANES)
        xdt = xdt_s[:, cols]
        both = []
        for h in (2 * pair, 2 * pair + 1):
            differ = cumul[:, h : h + 1] - turned[h : h + 1, :]
            mix = (scores * jnp.exp(jnp.where(lower, differ, -1e30))).astype(BF16)
            both.append(dot(mix, xdt))
        intra[0, :, cols] = jnp.where(left, both[0], both[1])


def gate_kernel(core_ref, hid, mine, recv, *refs):
    gate, wg, low, weight = refs[2 * GROUPS :]
    assemble(core_ref[0], refs[:GROUPS], refs[GROUPS : 2 * GROUPS], weight, SPANS)
    core = core_ref[0]
    rows = mine.shape[1]
    for y in range(mine.shape[0]):
        first = pl.ds(pl.multiple_of((2 * y + core) * rows, 16), rows)
        other = pl.ds(pl.multiple_of((2 * y + 1 - core) * rows, 16), rows)
        wg[first, :] = mine[y, :, :DI]
        wg[other, :] = recv[y, :, :DI]
        low[first, :] = mine[y, :, DI:]
        low[other, :] = recv[y, :, DI:]
    for r in range(hid.shape[0]):
        gate[r] = dot(hid[r], wg[...]).astype(BF16)


def slant_kernel(rows_in, cot, low, dnorm, wo, wide_s, wo_s):
    wide_s[...] = low[...].astype(F32)
    for d in range(D // rows_in):
        for half in range(2):
            start = (2 * d + half) * rows_in
            wo_s[start : start + rows_in] = wide_s[d * rows_in : (d + 1) * rows_in, half * D : (half + 1) * D]
    wo[...] = wo_s[...].astype(BF16)
    for r in range(cot.shape[0]):
        dnorm[r] = dot_nt(cot[r], wo[...])


def middle_kernel(
    quad_ref, s0, s1, s2, s3, act, intra, cum, gate, dnorm, par, heads,
    normed, dgate, dy, reach, p0, p1, p2, p3, sums, st, off_s, grow_s, high_s, low_s, doff_s, sum_s, state_s
):
    spread = heads_to_lanes()
    for k, slot in enumerate((s0, s1, s2, s3)):
        state_s[quarter(quad_ref, k), :] = slot[0]
    state = state_s[...]
    st[0] = state
    cmat = act[0, :, DI + N :]
    off_s[...] = dot(cmat, state)
    grow_s[...] = expand(jnp.exp(cum[0]), spread)
    skip = expand(jnp.broadcast_to(heads[2:3], (8, LANES)), spread)[0:1]
    gain = par[6:7, :DI]
    sum_s[...] = jnp.zeros_like(sum_s)
    size = 16

    def chunk(i, carry):
        at = pl.ds(pl.multiple_of(i * size, size), size)
        value = act[0, at, :DI].astype(F32)
        grow = grow_s[at, :]
        base = intra[0, at, :] + grow * off_s[at, :]
        ssd = base + skip * value
        z = gate[0, at, :].astype(F32)
        sig = jax.nn.sigmoid(z)
        silu = z * sig
        gated = ssd * silu
        scale = lax.rsqrt(jnp.mean(gated * gated, axis=-1, keepdims=True) + EPS)
        unit = gated * scale
        normed[0, at, :] = (unit * gain).astype(BF16)
        d_normed = dnorm[0, at, :]
        sum_s[0:8] += (d_normed * unit).reshape(size // 8, 8, DI).sum(axis=0)
        d_unit = d_normed * gain
        along = jnp.mean(d_unit * unit, axis=-1, keepdims=True)
        d_gated = scale * (d_unit - unit * along)
        dgate[0, at, :] = (d_gated * ssd * (sig * (1.0 + z * (1.0 - sig)))).astype(BF16)
        d_ssd = (d_gated * silu).astype(BF16)
        dy[0, at, :] = d_ssd
        d_ssd = d_ssd.astype(F32)
        doff_s[at, :] = (grow * d_ssd).astype(BF16)
        sum_s[8:16] += (d_ssd * value).reshape(size // 8, 8, DI).sum(axis=0)
        high, low = split(d_ssd * base)
        high_s[at, :] = high
        low_s[at, :] = low
        return carry

    lax.fori_loop(0, PIECE // size, chunk, 0, unroll=True)
    state_s[...] = dot_tn(cmat, doff_s[...]).astype(BF16)
    for k, slot in enumerate((p0, p1, p2, p3)):
        slot[0] = state_s[quarter(quad_ref, k), :]
    reach[0] = collect(high_s[...], low_s[...], spread)
    high, low = split(sum_s[8:16])
    sums[0, 0:8] = sum_s[0:8]
    sums[0, 8:16, :LANES] = collect(high, low, spread)
    sums[0, 8:16, LANES:] = jnp.zeros((8, DI - LANES), F32)


def outer_kernel(rows_in, core_ref, cot, hid, normed, dgate, _, keep, send, total, sums):
    core = core_ref[0]
    count = cot.shape[0]
    tangent = cot[...].reshape(count * PIECE, D)
    hidden = hid[...].reshape(count * PIECE, D)
    total[...] = dot_tn(normed[...].reshape(count * PIECE, DI), tangent)
    for half in range(2):
        cols = slice(half * D, (half + 1) * D)
        sums[:, cols] = dot_tn(hidden, dgate[:, :, cols].reshape(count * PIECE, D))
    for d in range(D // rows_in):
        for half in range(2):
            start = (2 * d + half) * rows_in
            sums[d * rows_in : (d + 1) * rows_in, DI + half * D : DI + (half + 1) * D] = total[start : start + rows_in]
    blocks, rows, _ = keep.shape
    for y in range(blocks):
        mine = pl.multiple_of((2 * y + core) * rows, 16)
        other = pl.multiple_of((2 * y + 1 - core) * rows, 16)
        keep[y] = sums[pl.ds(mine, rows)]
        send[y] = sums[pl.ds(other, rows)].astype(BF16)


def part_kernel(axis, bit_ref, keep, recv, out, send):
    bit = bit_ref[0]
    for place in itertools.product(range(2), repeat=keep.ndim - 3):
        mine, away = place[:axis] + (bit,) + place[axis:], place[:axis] + (1 - bit,) + place[axis:]
        out[place] = keep[mine] + recv[mine].astype(F32)
        send[place] = (keep[away] + recv[away].astype(F32)).astype(BF16)


def join_kernel(cuts, axes, bit_ref, small, other, _, *refs):
    count = 1 + max(operand for group in cuts for operand, _, _ in group)
    keeps, recvs = refs[:count], refs[count : 2 * count]
    outs, sends = refs[2 * count : 2 * count + GROUPS], refs[2 * count + GROUPS : 2 * count + 2 * GROUPS]
    refs[-1][...] = small[...] + other[...]
    for g, group in enumerate(cuts):
        bit, axis = bit_ref[g], axes[g]
        base = 0
        for operand, start, width in group:
            keep, recv = keeps[operand], recvs[operand]
            source, target = slice(start, start + width), slice(base, base + width)
            for place in itertools.product(range(2), repeat=keep.ndim - 3):
                mine = place[:axis] + (bit,) + place[axis:] + (slice(None), source)
                away = place[:axis] + (1 - bit,) + place[axis:] + (slice(None), source)
                here = place + (slice(None), target)
                outs[g][here] = keep[mine] + recv[mine].astype(F32)
                sends[g][here] = (keep[away] + recv[away].astype(F32)).astype(BF16)
            base += width


def last_kernel(small, other, w_in, gain, *refs):
    keeps, recvs = refs[:GROUPS], refs[GROUPS : 2 * GROUPS]
    small_out, g_win, g_wout, g_gin = refs[2 * GROUPS :]
    small_out[...] = small[...] + other[...]
    rows, width = g_win.shape
    for g in range(GROUPS):
        total = keeps[g][...] + recvs[g][...].astype(F32)
        start = DI + SPANS[g].start
        stop = min(start + WIDTHS[g], width)
        g_win[:, start:stop] = total[:, : stop - start]
        if g == 0:
            first = WIDTHS[0]
            g_win[:, :DI] = total[:, first : first + DI]
            g_wout[:rows] = total[:, first + DI : first + DI + D]
            g_wout[rows:] = total[:, first + DI + D :]
    g_gin[...] = jnp.sum(g_win[...] * w_in[...].astype(F32), axis=-1, keepdims=True) / gain[...].astype(F32)


def result_kernel(tok, normed, wo, _, out):
    out[0] = (tok[0].astype(F32) + dot(normed[0], wo[...])).astype(BF16)


def pair_kernel(act, step, cum, dy, st, u, dcm, dbm, xdt_s, doff_s, dsc_s):
    spread = heads_to_lanes()
    size, cumul = step[0], cum[0]
    grown = jnp.exp(cumul)
    for t in range(DI // 256):
        cols = slice(t * 256, (t + 1) * 256)
        xdt_s[:, cols] = (expand(size, spread[:, cols]) * act[0, :, cols].astype(F32)).astype(BF16)
        doff_s[:, cols] = (expand(grown, spread[:, cols]) * dy[0, :, cols].astype(F32)).astype(BF16)
    bmat, cmat = act[0, :, DI : DI + N], act[0, :, DI + N :]
    scores = dot_nt(cmat, bmat)
    lower = triangle(PIECE, True)
    turned = cumul.T
    dsc_s[...] = jnp.zeros_like(dsc_s)
    left = lax.broadcasted_iota(jnp.int32, (PIECE, LANES), 1) < HP
    zero = jnp.zeros((PIECE, LANES), BF16)
    for pair in range(H // 2):
        cols = slice(pair * LANES, (pair + 1) * LANES)
        xdt = xdt_s[:, cols]
        slope = dy[0, :, cols]
        slope_t = slope.astype(F32).T.astype(BF16)
        both = []
        for side in (0, 1):
            h = 2 * pair + side
            differ = cumul[:, h : h + 1] - turned[h : h + 1, :]
            decay = jnp.exp(jnp.where(lower, differ, -1e30))
            mix = (scores * decay).astype(BF16)
            own = jnp.where(left, slope, zero) if side == 0 else jnp.where(left, zero, slope)
            dsc_s[...] += dot_nt(own, xdt) * decay
            both.append(dot(slope_t[side * HP : (side + 1) * HP], mix))
        u[0, :, cols] = jnp.concatenate(both, axis=0).T
    d_scores = dsc_s[...].astype(BF16)
    dcm[0] = dot_nt(doff_s[...], st[0]) + dot(d_scores, bmat)
    dbm[0] = dot_tn(d_scores, cmat)


def back_kernel(
    quad_ref, l0, l1, l2, l3, st, act, cum, step, raw, u, dcm, dbm, dy, dsilu, reach, heads, _,
    dpre, edge, draw, hsum, dw_s, far_s, size_s, high_s, low_s, wts_s, sum_s, state_s
):
    spread = heads_to_lanes()
    size, cumul = step[0], cum[0]
    last = cumul[PIECE - 1 :]
    for k, slot in enumerate((l0, l1, l2, l3)):
        state_s[quarter(quad_ref, k), :] = slot[0]
    d_local = state_s[...]
    bmat = act[0, :, DI : DI + N]
    dw_s[...] = dot(bmat, d_local)
    far_s[...] = expand(jnp.exp(last - cumul), spread)
    size_s[...] = expand(size, spread)
    skip = expand(jnp.broadcast_to(heads[2:3], (8, LANES)), spread)[0:1]
    sum_s[...] = jnp.zeros_like(sum_s)
    rows = 16

    def chunk(i, carry):
        at = pl.ds(pl.multiple_of(i * rows, rows), rows)
        value = act[0, at, :DI].astype(F32)
        far, long = far_s[at, :], size_s[at, :]
        through = far * dw_s[at, :]
        d_xdt = u[0, at, :] + through
        d_value = long * d_xdt + skip * dy[0, at, :].astype(F32)
        dpre[0, at, :DI] = d_value * dsilu[0, at, :DI]
        high, low = split(value * d_xdt)
        high_s[at, :] = high
        low_s[at, :] = low
        xdt = long * value
        wts_s[at, :] = (far * xdt).astype(BF16)
        sum_s[0:8] += (xdt * through).reshape(rows // 8, 8, DI).sum(axis=0)
        return carry

    lax.fori_loop(0, PIECE // rows, chunk, 0, unroll=True)
    for j in range(N // 16):
        prod = state_s[j * 16 : (j + 1) * 16, :].astype(F32) * st[0, j * 16 : (j + 1) * 16, :].astype(F32)
        sum_s[8:16] += prod.reshape(2, 8, DI).sum(axis=0)
    d_bmat = dbm[0] + dot_nt(wts_s[...], d_local)
    dpre[0, :, DI : DI + N] = d_bmat * dsilu[0, :, DI : DI + N]
    dpre[0, :, DI + N :] = dcm[0] * dsilu[0, :, DI + N :]
    edge[0] = dpre[0, 0:8, :]
    q = collect(high_s[...], low_s[...], spread)
    high, low = split(sum_s[...])
    sums = collect(high, low, spread)
    d_last = jnp.sum(sums[0:8], axis=0, keepdims=True)
    d_last = d_last + jnp.exp(last) * jnp.sum(sums[8:16], axis=0, keepdims=True)
    d_cum = reach[0] - size * q
    row = lax.broadcasted_iota(jnp.int32, (PIECE, LANES), 0)
    d_cum = d_cum + jnp.where(row == PIECE - 1, d_last, 0.0)
    d_rate = running(triangle(PIECE, False), d_cum)
    decay = jnp.exp(heads[1:2])
    d_size = q - d_rate * decay
    d_raw = d_size * jax.nn.sigmoid(raw[0] + heads[0:1])
    draw[0] = d_raw
    for_bias = jnp.sum(d_raw, axis=0, keepdims=True)
    for_log = -jnp.sum(d_rate * size, axis=0, keepdims=True) * decay
    pick = lax.broadcasted_iota(jnp.int32, (8, LANES), 0)
    hsum[0] = jnp.where(pick == 0, for_bias, jnp.where(pick == 1, for_log, 0.0))


def input_kernel(core_ref, dpre, edge, draw, hid, par, gone, dproj, small, *refs):
    keeps, sends = refs[:GROUPS], refs[GROUPS : 2 * GROUPS]
    ext, *totals = refs[2 * GROUPS :]
    small[...] = gone[...]
    core = core_ref[0]
    count = dpre.shape[0]
    for r in range(count):
        ext[:PIECE] = dpre[r]
        ext[PIECE:] = edge[r]
        for t in range(CONV // LANES):
            cols = slice(t * LANES, (t + 1) * LANES)
            sum_k = par[KW - 1 : KW, cols] * ext[0:PIECE, cols]
            for k in range(KW - 1):
                sum_k = sum_k + par[k : k + 1, cols] * ext[pl.ds(KW - 1 - k, PIECE), cols]
            dproj[r, :, cols] = sum_k.astype(BF16)
        dproj[r, :, CONV:] = draw[r].astype(BF16)
    hidden = hid[...].reshape(count * PIECE, D)
    for keep, send, total, cols in zip(keeps, sends, totals, SPANS):
        total[...] = dot_tn(hidden, dproj[:, :, cols].reshape(count * PIECE, cols.stop - cols.start))
        blocks, rows, _ = keep.shape
        for y in range(blocks):
            mine = pl.multiple_of((2 * y + core) * rows, 16)
            other = pl.multiple_of((2 * y + 1 - core) * rows, 16)
            keep[y] = total[pl.ds(mine, rows)]
            send[y] = total[pl.ds(other, rows)].astype(BF16)


def taps_kernel(dpre, conv, sums, hsum, small, ext):
    @pl.when(pl.program_id(0) == 0)
    def _():
        small[...] = jnp.zeros_like(small)

    for t in range(CONV // LANES):
        cols = slice(t * LANES, (t + 1) * LANES)
        slope = dpre[0, :, cols]
        ext[...] = conv[0, :, cols].astype(F32)
        for k in range(KW):
            prod = slope * ext[pl.ds(HALO - KW + 1 + k, PIECE), :]
            small[k : k + 1, cols] += jnp.sum(prod, axis=0, keepdims=True)
        small[4:5, cols] += jnp.sum(slope, axis=0, keepdims=True)
    small[6:7, :DI] += jnp.sum(sums[0, 0:8], axis=0, keepdims=True)
    small[7:8, 0:LANES] += hsum[0, 0:1]
    small[7:8, LANES : 2 * LANES] += hsum[0, 1:2]
    small[7:8, 2 * LANES : 3 * LANES] += jnp.sum(sums[0, 8:16, :LANES], axis=0, keepdims=True)


def slope_kernel(dgate, wg, _, dh):
    dh[0] = dot_nt(dgate[0], wg[...])


def token_kernel(tok, cot, dh, dproj, weight, par, _, grad, dh_s):
    dh_s[...] = dh[0] + dot_nt(dproj[0], weight[...])
    gain = par[5:6, :D]
    rows = 32

    def chunk(i, carry):
        at = pl.ds(pl.multiple_of(i * rows, rows), rows)
        x = tok[0, at, :].astype(F32)
        scale = lax.rsqrt(jnp.mean(x * x, axis=-1, keepdims=True) + EPS)
        unit = x * scale
        d_unit = dh_s[at, :] * gain
        along = jnp.mean(d_unit * unit, axis=-1, keepdims=True)
        grad[0, at, :] = (cot[0, at, :].astype(F32) + scale * (d_unit - unit * along)).astype(BF16)
        return carry

    lax.fori_loop(0, PIECE // rows, chunk, 0, unroll=True)


def local(size, tokens, cotangent, norm_in, w_in, conv_w, conv_b, dt_bias, a_log, skip, norm_out, w_out):
    devices, along = size
    bits = int(math.log2(devices))
    core_bit = int(math.log2(along))
    me = lax.axis_index(AX)
    core = ((me >> core_bit) & 1).astype(jnp.int32)
    core_arg = core.reshape(1)
    high_bits = list(range(bits - 1, core_bit, -1))
    far_bits = list(range(core_bit - 1, -1, -1))
    dims = [far_bits[-1:], far_bits[:-1], high_bits] if core_bit == 3 else [far_bits[-3:], far_bits[:-3], high_bits]
    orders = [dims[1] + dims[2] + dims[0], dims[0] + dims[1] + dims[2], dims[2] + dims[0] + dims[1]]
    if [len(dim) for dim in dims] == [1, 2, 1]:
        x, (top, low), y = dims[0][0], dims[1], dims[2][0]
        orders = [[top, low, y, x], [top, x, low, y], [top, y, x, low]]

    def swap(x, bit):
        return lax.ppermute(x, AX, [(i, i ^ (1 << bit)) for i in range(devices)])

    def bit_of(bit):
        return (me >> bit) & 1

    def after(x, other):
        rows, cols = min(x.shape[-2], other.shape[-2], 8), min(x.shape[-1], other.shape[-1])
        part = other[(0,) * (other.ndim - 2)][:rows, :cols].astype(x.dtype)
        return x + 0 * jnp.pad(part, ((0, x.shape[-2] - rows), (0, x.shape[-1] - cols)))

    def gather(x, order, have):
        for bit in order:
            if order is lead and len(have) == HALO_TURN:
                x = after(x, halo)
            other = swap(x, bit)
            have = sorted(have + [bit], reverse=True)
            mine = bit_of(bit) == 0
            low, high = jnp.where(mine, x, other), jnp.where(mine, other, x)
            x = jnp.stack([low, high], axis=have.index(bit))
        return x, have

    micro, batch, count = tokens.shape[:3]
    tok = tokens.reshape(micro * batch, count, D)
    cot = cotangent.reshape(micro * batch, count, D)
    R = micro * batch
    heads = jnp.zeros((8, LANES), F32)
    for i, a in enumerate((dt_bias, a_log, skip)):
        heads = heads.at[i, :H].set(a)

    own_conv, own_in, own_out = conv_b.shape[0], norm_in.shape[0], norm_out.shape[0]
    owned_by = ((own_conv, tuple(range(KW + 1))), (own_in, (KW + 1,)), (own_out, (KW + 2,)))

    halo = lax.ppermute(tok[:, count - HALO :], "near", [(i, i + 1) for i in range(NEAR - 1)])
    rows_in = w_in.shape[0]
    kinds = jnp.concatenate(
        [
            conv_w.T,
            conv_b[None],
            jnp.pad(norm_in, (0, own_conv - own_in))[None],
            jnp.pad(norm_out, (0, own_conv - own_out))[None],
        ],
        axis=0,
    )
    turns = -(-kinds.shape[0] // rows_in)
    kinds = jnp.pad(kinds, ((0, turns * rows_in - kinds.shape[0]), (0, 0)))
    kinds = jnp.concatenate([kinds[t * rows_in : (t + 1) * rows_in] for t in range(turns)], axis=1)
    spare = PC - (w_in.shape[1] - DI)
    kinds = jnp.pad(kinds, ((0, 0), (0, spare - kinds.shape[1])))
    first = jnp.concatenate([w_in[:, DI:], kinds], axis=1)
    blocks = devices // (2 * along)
    rest = jnp.concatenate([w_in[:, :DI], w_out[:rows_in], w_out[rows_in:]], axis=1)
    lead = orders[0][:SPLIT_TURN]
    groups = []
    for g in range(GROUPS):
        both = jnp.concatenate([first[:, SPANS[g]], rest[:, g * RWIDTH : (g + 1) * RWIDTH]], axis=1)
        groups.append(gather(both, lead if g == 0 else orders[g][:SPLIT_TURN], []))
    halves = [(blocks, along * rows_in, width) for width in WIDTHS]
    mine = [
        gather(x[..., : WIDTHS[g]], orders[g][SPLIT_TURN:], have)[0].reshape(halves[g])
        for g, (x, have) in enumerate(groups)
    ]
    recv = [swap(x, core_bit) for x in mine]
    rest_half = (blocks, along * rows_in, RWIDTH)
    rest_mine = [
        gather(after(x[..., WIDTHS[g] :], mine[g]), orders[g][SPLIT_TURN:], have)[0].reshape(rest_half)
        for g, (x, have) in enumerate(groups)
    ]

    smem = pl.BlockSpec(memory_space=pltpu.SMEM)
    anywhere = pl.BlockSpec(memory_space=pl.ANY)
    inside = pl.BlockSpec(memory_space=pltpu.VMEM)
    halves = [(blocks, along * rows_in, width) for width in WIDTHS]
    par_spec, head_spec = whole((8, CONV)), whole((8, LANES))
    row_d, row_i, row_c = per_row((PIECE, D)), per_row((PIECE, DI)), per_row((PIECE, CONV))
    row_l = per_row((PIECE, LANES))
    def hold(x, ready):
        return pl.pallas_call(
            lambda *_: None,
            in_specs=[anywhere, anywhere],
            out_specs=anywhere,
            out_shape=struct(x.shape, x.dtype),
            input_output_aliases={0: 0},
            name="hold",
        )(x, ready)

    slot, slot_wide, whole_state = per_row((NQ, DI)), per_row((NQ, DI + LANES)), per_row((N, DI))
    quad = lax.axis_index("near") % QUAD
    quad_arg = jnp.stack([quad ^ k for k in range(QUAD)]).astype(jnp.int32)
    hid, conv, raw, act, step, cum, *pays, par = pl.pallas_call(
        functools.partial(enter_kernel, owned_by),
        grid=(R,),
        in_specs=[smem, smem, row_d, per_row((HALO, D)), head_spec] + [whole(half) for half in halves] * 2,
        out_specs=[
            row_d, per_row((HALO + PIECE, CONV)), row_l, row_c, row_l, row_l,
            *[slot_wide] * QUAD,
            par_spec,
        ],
        out_shape=[
            struct((R, PIECE, D), BF16), struct((R, HALO + PIECE, CONV), BF16), struct((R, PIECE, LANES), F32),
            struct((R, PIECE, CONV), BF16), struct((R, PIECE, LANES), F32),
            struct((R, PIECE, LANES), F32), *[struct((R, NQ, DI + LANES), BF16)] * QUAD,
            struct((8, CONV), F32),
        ],
        scratch_shapes=[
            pltpu.VMEM((HALO + PIECE, CONV), F32), pltpu.VMEM((N, DI), BF16), pltpu.VMEM((D, PC), BF16),
        ],
        compiler_params=params(60),
        cost_estimate=cost(R * 2e9, 2e7),
        name="enter",
    )(core_arg, quad_arg, tok, halo, heads, *mine, *recv)

    def exchange(slots):
        return slots[:1] + [
            lax.ppermute(slots[k], "near", [(i, i ^ k) for i in range(NEAR)]) for k in range(1, QUAD)
        ]

    def carry_on(slots, grows, backward, begin, ready):
        final = begin is not None
        width = slots[0].shape[-1]
        shape, kind = (R, NQ, DI), BF16
        outs = QUAD if final else 1
        return pl.pallas_call(
            functools.partial(pass_kernel, backward, final),
            grid=(1,),
            in_specs=[smem] + [whole((R, NQ, width))] * QUAD
            + [pl.BlockSpec((R, NQ, LANES), lambda r: (0, 0, DI // LANES))] * QUAD
            + [whole(shape) if final else anywhere, anywhere],
            out_specs=[whole(shape)] * outs,
            out_shape=[struct(shape, kind)] * outs,
            scratch_shapes=[
                pltpu.VMEM((QUAD, *shape), kind), pltpu.VMEM((QUAD, R, NQ, LANES), kind),
                pltpu.VMEM((QUAD, *shape), kind),
            ],
            compiler_params=params(60),
            cost_estimate=cost(1e7, 2e6),
            name="carry" if final else "total",
        )(quad_arg, *slots, *grows, begin if final else ready, ready)

    def crossing(total, backward):
        pairs = [(i + QUAD, i) if backward else (i, i + QUAD) for i in range(QUAD)]
        return lax.ppermute(total, "near", pairs)

    pieces = exchange(list(pays))
    intra, dsilu = pl.pallas_call(
        inside_kernel,
        grid=(R,),
        in_specs=[row_c, row_l, row_l, per_row((HALO + PIECE, CONV)), par_spec],
        out_specs=[row_i, row_c],
        out_shape=[struct((R, PIECE, DI), F32), struct((R, PIECE, CONV), F32)],
        scratch_shapes=[pltpu.VMEM((PIECE, DI), BF16), pltpu.VMEM((HALO + PIECE, LANES), F32)],
        compiler_params=params(60),
        cost_estimate=cost(R * 4e9, 5e6),
        name="inside",
    )(act, step, cum, conv, par)
    rest_all = hold(jnp.concatenate(rest_mine, axis=-1), hid)
    rest_other = swap(rest_all, core_bit)
    gate, wg, low, weight = pl.pallas_call(
        gate_kernel,
        in_specs=[smem] + [inside] * (3 + 2 * GROUPS),
        out_specs=[inside] * 4,
        out_shape=[
            struct((R, PIECE, DI), BF16), struct((D, DI), BF16), struct((D, 2 * D), BF16), struct((D, PC), BF16),
        ],
        compiler_params=params(60),
        cost_estimate=cost(R * 1e9, 1e7),
        name="gates",
    )(core_arg, hid, rest_all, rest_other, *mine, *recv)
    dnorm, wo = pl.pallas_call(
        functools.partial(slant_kernel, rows_in),
        in_specs=[inside] * 2,
        out_specs=[inside] * 2,
        out_shape=[struct((R, PIECE, DI), F32), struct((DI, D), BF16)],
        scratch_shapes=[pltpu.VMEM((D, 2 * D), F32), pltpu.VMEM((DI, D), F32)],
        compiler_params=params(60),
        cost_estimate=cost(R * 1e9, 1e7),
        name="slant",
    )(cot, low)
    total = carry_on(pieces, pieces, False, None, intra)[0]
    st = exchange(list(carry_on(pieces, pieces, False, crossing(total, False), gate)))

    wide = pltpu.VMEM((PIECE, DI), F32)
    slim = pltpu.VMEM((PIECE, DI), BF16)
    normed, dgate, dy, reach, b0, b1, b2, b3, sums, state = pl.pallas_call(
        middle_kernel,
        grid=(R,),
        in_specs=[smem, *[slot] * QUAD, row_c, row_i, row_l, row_i, row_i, par_spec, head_spec],
        out_specs=[row_i, row_i, row_i, row_l, *[slot] * QUAD, per_row((16, DI)), whole_state],
        out_shape=[
            struct((R, PIECE, DI), BF16), struct((R, PIECE, DI), BF16), struct((R, PIECE, DI), BF16),
            struct((R, PIECE, LANES), F32), *[struct((R, NQ, DI), BF16)] * QUAD, struct((R, 16, DI), F32),
            struct((R, N, DI), BF16),
        ],
        scratch_shapes=[wide, wide, slim, slim, slim, pltpu.VMEM((16, DI), F32), pltpu.VMEM((N, DI), BF16)],
        compiler_params=params(60),
        cost_estimate=cost(R * 2e9, 1.5e7),
        name="middle",
    )(quad_arg, *st, act, intra, cum, gate, dnorm, par, heads)

    pieces_b = exchange([b0, b1, b2, b3])
    rows_out = w_out.shape[0]
    u, dcm, dbm = pl.pallas_call(
        pair_kernel,
        grid=(R,),
        in_specs=[row_c, row_l, row_l, row_i, whole_state],
        out_specs=[row_i, row_l, row_l],
        out_shape=[struct((R, PIECE, DI), F32), struct((R, PIECE, N), F32), struct((R, PIECE, N), F32)],
        scratch_shapes=[slim, slim, pltpu.VMEM((PIECE, PIECE), F32)],
        compiler_params=params(60),
        cost_estimate=cost(R * 8e9, 1e7),
        name="pair",
    )(act, step, cum, dy, state)
    total = carry_on(pieces_b, pieces, True, None, u)[0]
    rest_shape = (blocks, along * rows_in, REST)
    rest_keep, rest_send = pl.pallas_call(
        functools.partial(outer_kernel, rows_in),
        in_specs=[smem] + [inside] * 4 + [anywhere],
        out_specs=[inside] * 2,
        out_shape=[struct(rest_shape, F32), struct(rest_shape, BF16)],
        scratch_shapes=[pltpu.VMEM((DI, D), F32), pltpu.VMEM((D, REST), F32)],
        compiler_params=params(60),
        cost_estimate=cost(6e9, 2e7),
        name="outer",
    )(core_arg, cot, hid, normed, dgate, pieces_b[0])
    carried = carry_on(pieces_b, pieces, True, crossing(total, True), rest_keep)
    rest_recv = swap(hold(rest_send, carried[0]), core_bit)
    def by_bits(x):
        count = x.size // (rows_in * x.shape[-1])
        return x.reshape((2,) * int(math.log2(count)) + (rows_in, x.shape[-1]))

    rest_bits = orders[0][::-1][1::-1]
    rest_have = sorted(orders[0], reverse=True)

    def rest_step(keep, recv, bit):
        keep, recv = by_bits(keep), by_bits(recv)
        axis = rest_have.index(bit)
        rest_have.remove(bit)
        shape = keep.shape[1:]
        keep, send = pl.pallas_call(
            functools.partial(part_kernel, axis),
            in_specs=[smem, inside, inside],
            out_specs=[inside, inside],
            out_shape=[struct(shape, F32), struct(shape, BF16)],
            compiler_params=params(44),
            cost_estimate=cost(1e6, 1e7),
            name="part",
        )(bit_of(bit).reshape(1).astype(jnp.int32), keep, recv)
        return keep, swap(send, bit)

    rest_keep, rest_recv = rest_step(rest_keep, rest_recv, rest_bits[0])
    later = exchange(list(carried))

    dpre, edge, draw, hsum = pl.pallas_call(
        back_kernel,
        grid=(R,),
        in_specs=[
            smem, *[slot] * QUAD, whole_state,
            row_c, row_l, row_l, row_l, row_i, row_l, row_l, row_i, row_c, row_l, head_spec, anywhere,
        ],
        out_specs=[row_c, per_row((8, CONV)), row_l, per_row((8, LANES))],
        out_shape=[
            struct((R, PIECE, CONV), F32), struct((R, 8, CONV), F32),
            struct((R, PIECE, LANES), F32), struct((R, 8, LANES), F32),
        ],
        scratch_shapes=[wide, wide, wide, slim, slim, slim, pltpu.VMEM((16, DI), F32), pltpu.VMEM((N, DI), BF16)],
        compiler_params=params(60),
        cost_estimate=cost(R * 2e9, 1.5e7),
        name="back",
    )(quad_arg, *later, state, act, cum, step, raw, u, dcm, dbm, dy, dsilu, reach, heads, rest_keep)
    edge = lax.ppermute(edge, "near", [(i + 1, i) for i in range(NEAR - 1)])

    small = pl.pallas_call(
        taps_kernel,
        grid=(R,),
        in_specs=[row_c, per_row((HALO + PIECE, CONV)), per_row((16, DI)), per_row((8, LANES))],
        out_specs=whole((8, CONV)),
        out_shape=struct((8, CONV), F32),
        scratch_shapes=[pltpu.VMEM((HALO + PIECE, LANES), F32)],
        compiler_params=params(60),
        cost_estimate=cost(2e7, 6e6),
        name="taps",
    )(dpre, conv, sums, hsum)

    dproj, small, *parts = pl.pallas_call(
        input_kernel,
        in_specs=[smem] + [inside] * 6,
        out_specs=[inside] * (2 + 2 * GROUPS),
        out_shape=[struct((R, PIECE, PC), BF16), struct((8, CONV), F32)]
        + [pltpu.VMEM(half, F32) for half in halves] + [pltpu.VMEM(half, BF16) for half in halves],
        scratch_shapes=[pltpu.VMEM((PIECE + 8, CONV), F32), *(pltpu.VMEM((D, width), F32) for width in WIDTHS)],
        compiler_params=params(44),
        cost_estimate=cost(2e9, 1e7),
        name="input",
    )(core_arg, dpre, edge, draw, hid, par, small)

    have = [sorted(order, reverse=True) for order in orders]
    cuts = [[(g, 0, WIDTHS[g])] for g in range(GROUPS)]
    keeps, recvs = parts[:GROUPS], [swap(x, core_bit) for x in parts[GROUPS:]]
    rest_keep, rest_recv = rest_step(rest_keep, rest_recv, rest_bits[1])
    other = swap(small, core_bit)
    ahead = small
    for turn in range(bits - 1):
        now = [order[::-1][turn] for order in orders]
        axes = [have[g].index(now[g]) for g in range(GROUPS)]
        if turn == 2:
            keeps, recvs = keeps + [rest_keep], recvs + [rest_recv]
            cuts = [cuts[0] + [(GROUPS, 0, REST)], *cuts[1:]]
        shapes = [
            (2,) * (bits - 2 - turn) + (rows_in, sum(width for _, _, width in cuts[g])) for g in range(GROUPS)
        ]
        *made, small = pl.pallas_call(
            functools.partial(join_kernel, cuts, axes),
            in_specs=[smem, inside, inside, anywhere] + [inside] * (2 * len(keeps)),
            out_specs=[inside] * (2 * GROUPS + 1),
            out_shape=[pltpu.VMEM(shape, F32) for shape in shapes]
            + [pltpu.VMEM(shape, BF16) for shape in shapes] + [pltpu.VMEM((8, CONV), F32)],
            compiler_params=params(40),
            cost_estimate=cost(1e6, 8e6),
            name="join",
        )(
            jnp.stack([bit_of(bit) for bit in now]).astype(jnp.int32),
            small, other, ahead, *map(by_bits, keeps), *map(by_bits, recvs),
        )
        if turn == 1:
            ahead = block_out = pl.pallas_call(
                result_kernel,
                grid=(R,),
                in_specs=[row_d, row_i, whole((DI, D)), anywhere],
                out_specs=row_d,
                out_shape=struct((R, PIECE, D), BF16),
                compiler_params=params(32),
                cost_estimate=cost(R * 6e8, 6e6),
                name="result",
            )(tok, normed, wo, small)
        if turn == 0:
            dh = pl.pallas_call(
                slope_kernel,
                grid=(R,),
                in_specs=[row_i, whole((D, DI)), anywhere],
                out_specs=row_d,
                out_shape=struct((R, PIECE, D), F32),
                compiler_params=params(32),
                cost_estimate=cost(R * 6e8, 6e6),
                name="slope",
            )(dgate, wg, small)
            grad_tokens = pl.pallas_call(
                token_kernel,
                grid=(R,),
                in_specs=[row_d, row_d, row_d, per_row((PIECE, PC)), whole((D, PC)), par_spec, anywhere],
                out_specs=row_d,
                out_shape=struct((R, PIECE, D), BF16),
                scratch_shapes=[pltpu.VMEM((PIECE, D), F32)],
                compiler_params=params(32),
                cost_estimate=cost(R * 2e9, 1.5e7),
                name="token",
            )(tok, cot, dh, dproj, weight, par, small)
            ahead = grad_tokens
        for g in range(GROUPS):
            have[g].remove(now[g])
        cuts = [[(g, 0, shapes[g][-1])] for g in range(GROUPS)]
        keeps = made[:GROUPS]
        recvs = [swap(x, now[g]) for g, x in enumerate(made[GROUPS:])]
        other = swap(small, orders[0][::-1][turn])
    flat = [x.reshape(rows_in, x.shape[-1]) for x in [*keeps, *recvs]]
    small, g_win, g_wout, g_gin = pl.pallas_call(
        last_kernel,
        in_specs=[inside] * (4 + 2 * GROUPS),
        out_specs=[inside] * 4,
        out_shape=[
            struct((8, CONV), F32), struct(w_in.shape, F32), struct(w_out.shape, F32), struct((rows_in, 1), F32),
        ],
        compiler_params=params(32),
        cost_estimate=cost(1e6, 1e6),
        name="last",
    )(small, other, w_in, norm_in[:, None], *flat)
    g_gin = g_gin[:, 0]
    taps = lax.dynamic_slice(small, (0, me * own_conv), (5, own_conv))
    g_gout = lax.dynamic_slice(small, (6, me * own_out), (1, own_out))[0]
    return (
        block_out.reshape(tokens.shape),
        grad_tokens.reshape(tokens.shape),
        g_gin,
        g_win,
        taps[:KW].T,
        taps[KW],
        small[7, :H],
        small[7, LANES : LANES + H],
        small[7, 2 * LANES : 2 * LANES + H],
        g_gout,
        g_wout,
    )


def solution(mesh):
    dp, seq = mesh.shape["dp"], mesh.shape["seq"]
    inner = Mesh(mesh.devices.reshape(dp, seq // NEAR, NEAR), AX)
    split_seq = ("far", "near")
    act = P(None, "dp", split_seq, None)
    vec, mat = P(AX), P(AX, None)

    def run(*args):
        return local((dp * seq, seq), *args)

    return jax.shard_map(
        run,
        mesh=inner,
        in_specs=(act, act, vec, mat, mat, vec, P(), P(), P(), vec, mat),
        out_specs=(act, act, vec, mat, mat, vec, P(), P(), P(), vec, mat),
        check_vma=False,
    )
```
